32 devices in a mesh: batch: 16 (over z, y, x), head: 2 (over core).
Axes of the slice: x: 2, y: 2, z: 4, core: 2. Of those that a mesh axis runs over, the one named last changes fastest.
Arguments:
- tokens: bfloat16 [128, 640, 384], P(('batch', 'head')), may hold values from -6 to 6
- cotangent: bfloat16 [128, 640, 384], P(('batch', 'head')), may hold values from -9 to 9
- lengths: int32 [128], P('batch'), may hold values from 1 to 577, 49237 in all
- key_masks: int32 [128, 640], P('batch'), may hold values 0 or 1
- qkv_master: float32 [384, 3, 384], P('batch', None, 'head'), may hold values from -0.3125 to 0.3125
- out_master: float32 [384, 384], P('head', 'batch'), may hold values from -1.25 to 1.25
- up_master: float32 [384, 1536], P('batch', 'head'), may hold values from -0.3125 to 0.3125
- down_master: float32 [1536, 384], P('head', 'batch'), may hold values from -0.15625 to 0.15625
- norm_master: float32 [1536], P(('batch', 'head')), may hold values from -2 to 3
- qkv_moments: float32 [2, 384, 3, 384], P(None, 'batch', None, 'head'), may hold values from -9 to 31, as said below
- out_moments: float32 [2, 384, 384], P(None, 'head', 'batch'), may hold values from -9 to 31, as said below
- up_moments: float32 [2, 384, 1536], P(None, 'batch', 'head'), may hold values from -9 to 31, as said below
- down_moments: float32 [2, 1536, 384], P(None, 'head', 'batch'), may hold values from -9 to 31, as said below
- norm_moments: float32 [2, 1536], P(None, ('batch', 'head')), may hold values from -34 to 490, as said below
Outputs:
- block_out: bfloat16 [128, 640, 384], P(('batch', 'head'))
- input_grad: float32 [128, 640, 384], P(('batch', 'head'))
- grad_norm: float32 [], replicated
- qkv_next: float32 [384, 3, 384], P('batch', None, 'head')
- out_next: float32 [384, 384], P('head', 'batch')
- up_next: float32 [384, 1536], P('batch', 'head')
- down_next: float32 [1536, 384], P('head', 'batch')
- norm_next: float32 [1536], P(('batch', 'head'))
- qkv_states: float32 [2, 384, 3, 384], P(None, 'batch', None, 'head')
- out_states: float32 [2, 384, 384], P(None, 'head', 'batch')
- up_states: float32 [2, 384, 1536], P(None, 'batch', 'head')
- down_states: float32 [2, 1536, 384], P(None, 'head', 'batch')
- norm_states: float32 [2, 1536], P(None, ('batch', 'head'))
- norm_grads: float32 [1536], P(('batch', 'head'))
The draws below stay inside these ranges and needn't reach their ends.
Inputs may be any that keep to these rules, and one draw needn't show every extreme that they name: `lengths`: at least one sequence has 577 live rows. `qkv_moments`: first moments, then second moments (positive). `out_moments`: first moments, then second moments (positive). `up_moments`: first moments, then second moments (positive). `down_moments`: first moments, then second moments (positive). `norm_moments`: first moments, then second moments (positive).
All inputs are finite; a program needn't handle non-finite values. No bound on the sum of `lengths` or of `key_masks` on one device may be relied on, other than what follows from the above.
Results may differ from the reference program's by a relative error of at most 0.017.
Values may be sent and summed in bfloat16 or wider, within the bound.
No kernel may reach another device: no remote copies, remote signals or barrier semaphores. Data moves between devices by JAX's collectives and lax.ppermute only.
A program may use at most 192 MiB of HBM per device.

```python
import math
import jax
import jax.numpy as jnp
import numpy as np
from jax import lax

D = 384
H = 6
HD = 64
FF = 1536
LMAX = 577
LPAD = 640
STEP = 10
SEQS = 128


CLIP_NORM = 1000.0


def rising(width_of, highest):
    return 1.0 + (highest - 1.0) * jnp.arange(width_of, dtype=jnp.float32) / width_of


def entry_size():
    return CLIP_NORM / math.sqrt(4 * D * D + 2 * D * FF)


def moment_pair(key, dims_of, typical):
    first_key, second_key = jax.random.split(key)
    moment = typical * jnp.clip(jax.random.normal(first_key, dims_of, jnp.float32), -3.0, 3.0)
    spread = jnp.exp(jax.random.uniform(second_key, dims_of, jnp.float32, 0.0, math.log(4.0)))
    return jnp.stack([moment, typical * typical * spread])


def draw_cotangent(key, part):
    key = jax.random.fold_in(key, 11)
    normal_part = jnp.clip(jax.random.normal(key, (SEQS, LPAD, D), jnp.float32), -4.0, 4.0)
    column_scale = rising(D, 1.73)
    return (normal_part * column_scale).astype(jnp.bfloat16)


def draw_norm_master(key, part):
    key = jax.random.fold_in(key, 12)
    keys_list = jax.random.split(key, 4)
    highest = 1.73
    gain_one = rising(D, highest) * jax.random.uniform(keys_list[0], (D,), jnp.float32, 0.8, 1.2)
    bias_one = 0.4 * jnp.clip(jax.random.normal(keys_list[1], (D,), jnp.float32), -4.0, 4.0)
    gain_two = rising(D, highest) * jax.random.uniform(keys_list[2], (D,), jnp.float32, 0.8, 1.2)
    bias_two = 0.4 * jnp.clip(jax.random.normal(keys_list[3], (D,), jnp.float32), -4.0, 4.0)
    return jnp.concatenate([gain_one, bias_one, gain_two, bias_two])


def draw_qkv_moments(key, part):
    key = jax.random.fold_in(key, 21)
    return moment_pair(key, (D, 3, D), entry_size())


def draw_out_moments(key, part):
    key = jax.random.fold_in(key, 22)
    return moment_pair(key, (D, D), entry_size())


def draw_up_moments(key, part):
    key = jax.random.fold_in(key, 23)
    return moment_pair(key, (D, FF), entry_size())


def draw_down_moments(key, part):
    key = jax.random.fold_in(key, 24)
    return moment_pair(key, (FF, D), entry_size())


def draw_norm_moments(key, part):
    key = jax.random.fold_in(key, 25)
    return moment_pair(key, (4 * D,), 4.0 * entry_size())


def plant(drawn, rng, least, high):
    extent = drawn.shape
    place = [jax.random.randint(jax.random.fold_in(rng, axis), (), 0, extent[axis]) for axis in range(len(extent))]
    drawn = drawn.at[tuple(place)].set(least)
    longest = extent.index(max(extent))
    place[longest] = (place[longest] + 1) % extent[longest]
    return drawn.at[tuple(place)].set(high)


def levels(stream_key, extent, cuts, low, top_value):
    factor_of, own = 1.0, jax.random.fold_in(stream_key, 6)
    for position, parts in cuts:
        heights = jnp.exp(jax.random.uniform(jax.random.fold_in(own, position), (parts,), jnp.float32, low / len(cuts), top_value / len(cuts)))
        factor_of = factor_of * jnp.repeat(heights, extent[position] // parts).reshape([-1 if axis == position else 1 for axis in range(len(extent))])
    return factor_of


def profile(count, total, reach, skew):
    loads = [(1 << 20) // math.isqrt(grade ** skew) + 1 for grade in range(2, count + 1)]
    rest, given = total - reach - (count - 1), [1] * (count - 1)
    while rest > 0:
        free = [i for i in range(count - 1) if given[i] < reach]
        pool, remaining = sum([loads[i] for i in free]), rest
        for i in free:
            extra = min(reach - given[i], max(1, remaining * loads[i] // pool), rest)
            given[i] = given[i] + extra
            rest = rest - extra
    return np.array([reach] + given)


def uneven(stream_key, count, total, bound, slope):
    if count == 2:
        one = jax.random.randint(stream_key, (), max(1, total - bound), min(bound, total - 1) + 1)
        return jnp.stack([one, total - one])
    sizes = jnp.asarray(profile(count, total, bound, slope), jnp.int32)
    couples = (count - 1) // 2
    giver, taker = sizes[1:1 + 2 * couples:2], sizes[2:2 + 2 * couples:2]
    room = jnp.minimum(giver - 1, bound - taker)
    passed = jax.random.randint(jax.random.fold_in(stream_key, 1), (couples,), 0, 1 << 20) % (room + 1)
    sizes = sizes.at[1:1 + 2 * couples:2].set(giver - passed).at[2:2 + 2 * couples:2].set(taker + passed)
    return sizes[jax.random.permutation(jax.random.fold_in(stream_key, 2), count)]


def noise(key, shape, scale, limit, cuts=(), kind=jnp.bfloat16):
    loudness = levels(key, shape, cuts, -0.22, 0.18) if cuts else 1.0
    entries = jax.random.normal(key, shape, jnp.float32) * scale * loudness
    return jnp.minimum(jnp.maximum(entries, -limit), limit).astype(kind)


def setup_inputs(seed: int = 0) -> dict:
    splits = jax.random.split(jax.random.key(seed), 15)
    tokens = noise(splits[0], (SEQS, LPAD, D), 1.0, 6.0, ((0, 32),))
    cotangent = draw_cotangent(jax.random.fold_in(splits[14], 71), 0)
    lengths = uneven(splits[2], SEQS, SEQS * LMAX * 2 // 3, LMAX, 1).astype(jnp.int32)
    key_masks = plant((jax.random.randint(splits[3], (SEQS, LPAD), 0, 8) < 7).astype(jnp.int32), jax.random.fold_in(splits[3], 1), 0, 1)
    qkv_master = noise(splits[4], (D, 3, D), D ** -0.5, 0.3125, ((0, 16), (2, 2)), jnp.float32)
    out_master = noise(splits[5], (D, D), (D // 16) ** -0.5, 1.25, ((0, 2), (1, 16)), jnp.float32)
    up_master = noise(splits[6], (D, FF), D ** -0.5, 0.3125, ((0, 16), (1, 2)), jnp.float32)
    down_master = noise(splits[7], (FF, D), FF ** -0.5, 0.15625, ((0, 2), (1, 16)), jnp.float32)
    norm_master = draw_norm_master(jax.random.fold_in(splits[14], 71), 0)
    qkv_moments = draw_qkv_moments(jax.random.fold_in(splits[14], 71), 0)
    out_moments = draw_out_moments(jax.random.fold_in(splits[14], 71), 0)
    up_moments = draw_up_moments(jax.random.fold_in(splits[14], 71), 0)
    down_moments = draw_down_moments(jax.random.fold_in(splits[14], 71), 0)
    norm_moments = draw_norm_moments(jax.random.fold_in(splits[14], 71), 0)
    return dict(tokens=tokens, cotangent=cotangent, lengths=lengths, key_masks=key_masks, qkv_master=qkv_master, out_master=out_master, up_master=up_master, down_master=down_master, norm_master=norm_master, qkv_moments=qkv_moments, out_moments=out_moments, up_moments=up_moments, down_moments=down_moments, norm_moments=norm_moments)


@jax.custom_vjp
def low(v):
    return lax.optimization_barrier(v.astype(jnp.bfloat16)).astype(jnp.float32)

@jax.custom_vjp
def low_back(v):
    return v

def low_keep(v):
    return (low(v), None)

def low_pass(kept, grad):
    return (grad,)

def back_keep(v):
    return (v, None)

def back_low(kept, grad):
    return (low(grad),)
low.defvjp(low_keep, low_pass)
low_back.defvjp(back_keep, back_low)
NORM_EPS = 1e-06
CLIP_NORM = 1000.0
BETA_ONE = 0.5
BETA_TWO = 0.5
ADAM_EPS = 1e-08
RATE_LIST = (0.06, 0.25, 0.06, 0.03, 0.5)
DECAY_LIST = (0.04, 0.04, 0.04, 0.04, 0.0)

def layer_norm(values, norm_gain, norm_bias):
    row_mean = lax.optimization_barrier(jnp.mean(values, axis=-1, keepdims=True))
    centred = values - row_mean
    variance = lax.optimization_barrier(jnp.mean(centred * centred, axis=-1, keepdims=True))
    return centred * lax.rsqrt(variance + NORM_EPS) * norm_gain + norm_bias

def matmul(left, right):
    return jnp.dot(left, right, precision=lax.Precision.HIGHEST)

def exact_gelu(values):
    return jax.nn.gelu(values, approximate=False)

def forward(inputs, qkv_master, out_master, up_master, down_master, norm_master, visible):
    norms = norm_master.reshape(4, D)
    normed_one = low(layer_norm(inputs, norms[0], norms[1]))
    projected = jnp.einsum('ld,dce->lce', normed_one, low(qkv_master), precision=lax.Precision.HIGHEST)
    projected = low_back(low(projected))
    queries = projected[:, 0].reshape(LPAD, H, HD)
    key_rows = projected[:, 1].reshape(LPAD, H, HD)
    values = projected[:, 2].reshape(LPAD, H, HD)
    scores = jnp.einsum('qhe,khe->hqk', queries, key_rows, precision=lax.Precision.HIGHEST) * HD ** (-0.5)
    scores = low_back(scores)
    scores = jnp.where(visible[None, None, :], scores, -1e+30)
    row_top = lax.optimization_barrier(jnp.max(scores, axis=-1, keepdims=True))
    powers = jnp.exp(scores - row_top)
    attn_prob = powers / lax.optimization_barrier(jnp.sum(powers, axis=-1, keepdims=True))
    attended = jnp.einsum('hqk,khe->qhe', low(attn_prob), values, precision=lax.Precision.HIGHEST)
    attended = low_back(low(attended)).reshape(LPAD, D)
    middle = inputs + low_back(matmul(attended, low(out_master)))
    normed_two = low(layer_norm(middle, norms[2], norms[3]))
    hidden_rows = low_back(matmul(normed_two, low(up_master)))
    gelu_output = low(exact_gelu(hidden_rows))
    return middle + low_back(matmul(gelu_output, low(down_master)))

def adamw(master, gradient, moments, rate, decay):
    moment = BETA_ONE * moments[0] + (1.0 - BETA_ONE) * gradient
    second = BETA_TWO * moments[1] + (1.0 - BETA_TWO) * gradient * gradient
    step_size = moment / (1.0 - BETA_ONE ** STEP) / (jnp.sqrt(second / (1.0 - BETA_TWO ** STEP)) + ADAM_EPS)
    return (master - rate * (step_size + decay * master), jnp.stack([moment, second]))

def reference(tokens, cotangent, lengths, key_masks, qkv_master, out_master, up_master, down_master, norm_master, qkv_moments, out_moments, up_moments, down_moments, norm_moments):
    masters = (qkv_master, out_master, up_master, down_master, norm_master)
    positions = jnp.arange(LPAD, dtype=jnp.int32)

    def per_sequence(summed, member):
        inputs, upstream, length, key_mask = member
        visible = (positions < length) & ((key_mask == 1) | (positions == 0))
        live_rows = (positions < length).astype(jnp.float32)[:, None]

        def layer_fn(inputs_float, *params):
            return forward(inputs_float, *params, visible)
        result, pull_back = jax.vjp(layer_fn, inputs.astype(jnp.float32), *masters)
        gradients = pull_back(upstream.astype(jnp.float32) * live_rows)
        summed = tuple((running + fresh for running, fresh in zip(summed, gradients[1:])))
        return (summed, (result.astype(jnp.bfloat16), gradients[0]))
    zeros_all = tuple((jnp.zeros_like(master) for master in masters))
    totals, (block_out, input_grad) = lax.scan(per_sequence, zeros_all, (tokens, cotangent, lengths, key_masks))
    squares = sum((jnp.sum(gradient * gradient) for gradient in totals))
    grad_norm = jnp.sqrt(squares)
    factor = jnp.minimum(1.0, CLIP_NORM / (grad_norm + 1e-06))
    norm_grads = factor * totals[4]
    qkv_next, qkv_states = adamw(qkv_master, factor * totals[0], qkv_moments, RATE_LIST[0], DECAY_LIST[0])
    out_next, out_states = adamw(out_master, factor * totals[1], out_moments, RATE_LIST[1], DECAY_LIST[1])
    up_next, up_states = adamw(up_master, factor * totals[2], up_moments, RATE_LIST[2], DECAY_LIST[2])
    down_next, down_states = adamw(down_master, factor * totals[3], down_moments, RATE_LIST[3], DECAY_LIST[3])
    norm_next, norm_states = adamw(norm_master, norm_grads, norm_moments, RATE_LIST[4], DECAY_LIST[4])
    return (block_out, input_grad, grad_norm, qkv_next, out_next, up_next, down_next, norm_next, qkv_states, out_states, up_states, down_states, norm_states, norm_grads)
```

```python
import functools

import jax
import jax.numpy as jnp
from jax import lax
from jax.experimental import pallas as pl
from jax.experimental.pallas import tpu as pltpu
from jax.sharding import PartitionSpec as P

HD = 64
STEP = 10
NORM_EPS = 1e-06
CLIP_NORM = 1000.0
BETA_ONE = 0.5
BETA_TWO = 0.5
ADAM_EPS = 1e-08
RATE_LIST = (0.06, 0.25, 0.06, 0.03, 0.5)
DECAY_LIST = (0.04, 0.04, 0.04, 0.04, 0.0)

F32 = jnp.float32
BF16 = jnp.bfloat16
NN = (((1,), (0,)), ((), ()))
NT = (((1,), (1,)), ((), ()))
TN = (((0,), (0,)), ((), ()))
QB = 128
FB = 512
FC = 256
PAIR = 2 * HD
VMEM = pltpu.CompilerParams(vmem_limit_bytes=56 * 2**20)


def cost(microseconds):
    return pl.CostEstimate(flops=microseconds * 1_000_000_000, bytes_accessed=1_000_000, transcendentals=0)


def mm(left, right, dims=NN):
    return lax.dot_general(left, right, dims, preferred_element_type=F32)


def normalize(values):
    centred = values - jnp.mean(values, axis=-1, keepdims=True)
    variance = jnp.mean(centred * centred, axis=-1, keepdims=True)
    rs = lax.rsqrt(variance + NORM_EPS)
    return centred * rs, rs


def norm_backward(normal, rs, gained):
    inner = jnp.mean(gained * normal, axis=-1, keepdims=True)
    return rs * (gained - jnp.mean(gained, axis=-1, keepdims=True) - normal * inner)


def gelu_parts(h):
    gauss = jnp.exp(h * h * -0.5)
    t = 1.0 / (1.0 + (0.3275911 * 0.7071067811865476) * jnp.abs(h))
    poly = t * (
        0.127414796
        + t * (-0.142248368 + t * (0.7107068705 + t * (-0.7265760135 + t * 0.5307027145)))
    )
    tail = poly * gauss
    return jnp.where(h < 0.0, tail, 1.0 - tail), gauss


def split_pairs(own, other, per_pair):
    wide, narrow = 2 * per_pair, per_pair
    singles = []
    for part in range(per_pair // HD):
        cols = slice(wide + part * HD, wide + (part + 1) * HD)
        singles += [own[:, cols], other[:, cols]]
    return own[:, :wide], jnp.concatenate(singles, axis=1), other[:, :wide]


def join_pairs(first, second, third, per_pair):
    parts = [
        [second[:, p * PAIR + side * HD : p * PAIR + (side + 1) * HD] for p in range(per_pair // HD)]
        for side in range(2)
    ]
    return [first] + parts[0], [third] + parts[1]


def forward_kernel(
    tok_ref, bias_ref, own_ref, other_ref, norms_ref, n1t_ref, qkv_ref, att_ref, p_ref, w_ref
):
    rows, width = tok_ref.shape

    @pl.when(pl.program_id(0) == 0)
    def _():
        cols = 9 * HD
        for i, part in enumerate(split_pairs(own_ref[:, :cols], other_ref[:, :cols], 3 * HD)):
            w_ref[i] = part

    x = tok_ref[...].astype(F32)
    normal, _ = normalize(x)
    n1 = (normal * norms_ref[0:1, :] + norms_ref[1:2, :]).astype(BF16)
    n1t_ref[...] = n1.T
    bias = bias_ref[...]
    lane = lax.broadcasted_iota(jnp.int32, (QB, PAIR), 1)
    for pair in range(width // PAIR):
        part = mm(n1, w_ref[pair])
        qkv_ref[pair, :, :PAIR] = (part[:, :PAIR].astype(BF16).astype(F32) * (HD**-0.5)).astype(BF16)
        qkv_ref[pair, :, PAIR:] = part[:, PAIR:].astype(BF16)
        kp = qkv_ref[pair, :, PAIR : 2 * PAIR]
        vp = qkv_ref[pair, :, 2 * PAIR :]
        for qb in range(rows // QB):
            sl = slice(qb * QB, (qb + 1) * QB)
            qp = qkv_ref[pair, sl, :PAIR]
            outs = []
            for half in range(2):
                qm = jnp.where((lane < HD) == (half == 0), qp, jnp.zeros_like(qp))
                s = mm(qm, kp, NT) + bias
                e = jnp.exp(s - jnp.max(s, axis=-1, keepdims=True))
                p = (e * (1.0 / jnp.sum(e, axis=-1, keepdims=True))).astype(BF16)
                p_ref[pair * 2 + half, sl, :] = p
                outs.append(mm(p, vp))
            att_ref[sl, pair * PAIR : (pair + 1) * PAIR] = jnp.where(
                lane < HD, outs[0], outs[1]
            ).astype(BF16)


def forward(tokens, bias, own, other, norms):
    seqs, rows, width = tokens.shape
    heads, pairs = width // HD, width // PAIR
    sq = pl.squeezed
    shape = jax.ShapeDtypeStruct
    whole = lambda *dims: pl.BlockSpec(dims, lambda s: (0,) * len(dims))
    return pl.pallas_call(
        forward_kernel,
        grid=(seqs,),
        in_specs=[
            pl.BlockSpec((sq, rows, width), lambda s: (s, 0, 0)),
            pl.BlockSpec((sq, 1, rows), lambda s: (s, 0, 0)),
            whole(*own.shape),
            whole(*other.shape),
            whole(4, width),
        ],
        out_specs=[
            pl.BlockSpec((sq, width, rows), lambda s: (s, 0, 0)),
            pl.BlockSpec((sq, pairs, rows, 3 * PAIR), lambda s: (s, 0, 0, 0)),
            pl.BlockSpec((sq, rows, width), lambda s: (s, 0, 0)),
            pl.BlockSpec((sq, heads, rows, rows), lambda s: (s, 0, 0, 0)),
            whole(pairs, width, 3 * PAIR),
        ],
        out_shape=[
            shape((seqs, width, rows), BF16),
            shape((seqs, pairs, rows, 3 * PAIR), BF16),
            shape((seqs, rows, width), BF16),
            shape((seqs, heads, rows, rows), BF16),
            shape((pairs, width, 3 * PAIR), BF16),
        ],
        compiler_params=VMEM,
        cost_estimate=cost(50),
        name="attention_forward",
    )(tokens, bias, own, other, norms)


def middle_kernel(
    seq_rows, units, len_ref, tok_ref, cot_ref, att_ref, own_ref, other_ref, norms_ref,
    out_ref, gmid_ref, gatt_ref, gown_ref, gother_ref, gnorm_ref,
    wo_ref, gout_ref, gup_ref, gdown_ref,
):
    step = pl.program_id(0)
    rows, width = tok_ref.shape
    halves = (own_ref, other_ref)

    @pl.when(step == 0)
    def _():
        gout_ref[...] = jnp.zeros_like(gout_ref)
        gup_ref[...] = jnp.zeros_like(gup_ref)
        gdown_ref[...] = jnp.zeros_like(gdown_ref)
        gnorm_ref[...] = jnp.zeros_like(gnorm_ref)
        cols = slice(2 * units, 2 * units + 3 * HD)
        parts = split_pairs(own_ref[:, cols], other_ref[:, cols], HD)
        for i, part in enumerate(parts):
            wo_ref[:, i * PAIR : (i + 1) * PAIR] = part

    first = step * rows
    row = first + lax.broadcasted_iota(jnp.int32, (rows, 1), 0)
    live = row < 0
    last = len_ref.shape[0] - 1
    for near in range(-(-rows // seq_rows) + 1):
        s = first // seq_rows + near
        bound = jnp.where(s <= last, len_ref[jnp.minimum(s, last)], 0)
        live = live | ((row >= s * seq_rows) & (row < s * seq_rows + bound))

    x = tok_ref[...].astype(F32)
    att = att_ref[...]
    mid = x + mm(att, wo_ref[...], NT)
    normal, rs = normalize(mid)
    gain, shift = norms_ref[2:3, :], norms_ref[3:4, :]
    n2 = (normal * gain + shift).astype(BF16)
    n2t = n2.T
    up = jnp.where(live, cot_ref[...].astype(F32), 0.0)
    gb = up.astype(BF16)
    gbt = gb.T
    bo = mid
    gtwo = jnp.zeros_like(mid)
    for half in range(2):
        for c in range(units // FC):
            cols = slice(c * FC, (c + 1) * FC)
            wu = halves[half][:, c * FC : (c + 1) * FC]
            wd = halves[half][:, units + c * FC : units + (c + 1) * FC]
            h = mm(n2, wu)
            ga = mm(gb, wd)
            cdf, gauss = gelu_parts(h)
            act = (h * cdf).astype(BF16)
            gh = (ga * (cdf + h * (gauss * 0.3989422804014327))).astype(BF16)
            bo = bo + mm(act, wd, NT)
            gtwo = gtwo + mm(gh, wu, NT)
            gup_ref[half, :, cols] += mm(n2t, gh)
            gdown_ref[half, :, cols] += mm(gbt, act)
    out_ref[...] = bo.astype(BF16)
    gnorm_ref[0:8, :] += jnp.sum((gtwo * normal).reshape(rows // 8, 8, width), axis=0)
    gnorm_ref[8:16, :] += jnp.sum(gtwo.reshape(rows // 8, 8, width), axis=0)
    gmid = up + norm_backward(normal, rs, gtwo * gain)
    gmid_ref[...] = gmid
    gm = gmid.astype(BF16)
    gout_ref[...] += mm(gm, att, TN)
    gatt_ref[...] = mm(gm, wo_ref[...]).astype(BF16)

    @pl.when(step == pl.num_programs(0) - 1)
    def _():
        total = gout_ref[...]
        sides = join_pairs(
            total[:, :PAIR], total[:, PAIR : 2 * PAIR], total[:, 2 * PAIR :], HD
        )
        for half, ref in enumerate((gown_ref, gother_ref)):
            ref[:, :units] = gup_ref[half].astype(BF16)
            ref[:, units : 2 * units] = gdown_ref[half].astype(BF16)
            blank = jnp.zeros((total.shape[0], HD), F32)
            ref[:, 2 * units :] = jnp.concatenate(sides[half] + [blank], axis=1).astype(BF16)


def middle(lengths, tokens, cotangent, attended, own, other, norms):
    seqs, seq_rows, width = tokens.shape
    total = seqs * seq_rows
    packed = own.shape[1]
    units = (packed - 4 * HD) // 2
    flat = lambda a: a.reshape(total, width)
    rowspec = pl.BlockSpec((FB, width), lambda s: (s, 0))
    whole = lambda *dims: pl.BlockSpec(dims, lambda s: (0,) * len(dims))
    shape = jax.ShapeDtypeStruct
    return pl.pallas_call(
        functools.partial(middle_kernel, seq_rows, units),
        grid=(total // FB,),
        in_specs=[
            pl.BlockSpec(memory_space=pltpu.SMEM),
            rowspec,
            rowspec,
            rowspec,
            whole(*own.shape),
            whole(*other.shape),
            whole(4, width),
        ],
        out_specs=[rowspec] * 3 + [whole(*own.shape), whole(*own.shape), whole(16, width)],
        out_shape=[
            shape((total, width), BF16),
            shape((total, width), F32),
            shape((total, width), BF16),
            shape(own.shape, BF16),
            shape(own.shape, BF16),
            shape((16, width), F32),
        ],
        scratch_shapes=[
            pltpu.VMEM((width, width), BF16),
            pltpu.VMEM((width, width), F32),
            pltpu.VMEM((2, width, units), F32),
            pltpu.VMEM((2, width, units), F32),
        ],
        compiler_params=VMEM,
        cost_estimate=cost(50),
        name="feed_forward",
    )(lengths, flat(tokens), flat(cotangent), flat(attended), own, other, norms)


def backward_kernel(
    n1t_ref, qkv_ref, p_ref, gatt_ref, att_ref, gp_ref, gown_ref, gother_ref, gqkv_ref
):
    seq, pair = pl.program_id(0), pl.program_id(1)
    rows = qkv_ref.shape[0]
    qp, kp, vp = qkv_ref[:, :PAIR], qkv_ref[:, PAIR : 2 * PAIR], qkv_ref[:, 2 * PAIR :]
    ga = gatt_ref[...]
    prod = ga.astype(F32) * att_ref[...].astype(F32)
    lane = lax.broadcasted_iota(jnp.int32, (QB, PAIR), 1)
    gat, qt = ga.T, qp.T
    zero = jnp.zeros((QB, PAIR), BF16)
    gq = [[], []]
    gkt, gvt = [], []
    for half in range(2):
        ds_all = []
        mask = (lane < HD) == (half == 0)
        for qb in range(rows // QB):
            sl = slice(qb * QB, (qb + 1) * QB)
            dp = mm(jnp.where(mask, ga[sl], zero), vp, NT)
            inner = jnp.sum(jnp.where(mask, prod[sl], 0.0), axis=-1, keepdims=True)
            ds = (p_ref[half, sl, :].astype(F32) * (dp - inner)).astype(BF16)
            ds_all.append(ds)
            gq[half].append(mm(ds, kp))
        ds = jnp.concatenate(ds_all, axis=0)
        hs = slice(half * HD, half * HD + HD)
        gkt.append(mm(qt[hs], ds))
        gvt.append(mm(gat[hs], p_ref[half]))
    for qb in range(rows // QB):
        sl = slice(qb * QB, (qb + 1) * QB)
        joined = jnp.where(lane < HD, gq[0][qb], gq[1][qb])
        gp_ref[sl, :PAIR] = (joined * (HD**-0.5)).astype(BF16)
    gp_ref[:, PAIR : 2 * PAIR] = jnp.concatenate(gkt, axis=0).astype(BF16).T
    gp_ref[:, 2 * PAIR :] = jnp.concatenate(gvt, axis=0).astype(BF16).T
    new = mm(n1t_ref[...], gp_ref[...])

    @pl.when(seq == 0)
    def _():
        gqkv_ref[pair] = new

    @pl.when(seq > 0)
    def _():
        gqkv_ref[pair] += new

    @pl.when((seq == pl.num_programs(0) - 1) & (pair == pl.num_programs(1) - 1))
    def _():
        sides = join_pairs(gqkv_ref[0], gqkv_ref[1], gqkv_ref[2], 3 * HD)
        blank = jnp.zeros((gqkv_ref.shape[1], HD), F32)
        for columns, ref in zip(sides, (gown_ref, gother_ref)):
            ref[...] = jnp.concatenate(columns + [blank], axis=1).astype(BF16)


def backward(n1t, qkv, probs, gatt, attended):
    seqs, rows, width = attended.shape
    pairs = width // PAIR
    sq = pl.squeezed
    pairspec = pl.BlockSpec((sq, rows, PAIR), lambda s, p: (s, 0, p))
    groupspec = pl.BlockSpec((sq, sq, rows, 3 * PAIR), lambda s, p: (s, p, 0, 0))
    whole = lambda *dims: pl.BlockSpec(dims, lambda s, p: (0,) * len(dims))
    shape = jax.ShapeDtypeStruct
    packed = (width, 10 * HD)
    return pl.pallas_call(
        backward_kernel,
        grid=(seqs, pairs),
        in_specs=[
            pl.BlockSpec((sq, width, rows), lambda s, p: (s, 0, 0)),
            groupspec,
            pl.BlockSpec((sq, 2, rows, rows), lambda s, p: (s, p, 0, 0)),
            pairspec,
            pairspec,
        ],
        out_specs=[groupspec, whole(*packed), whole(*packed)],
        out_shape=[shape(qkv.shape, BF16), shape(packed, BF16), shape(packed, BF16)],
        scratch_shapes=[pltpu.VMEM((pairs, width, 3 * PAIR), F32)],
        compiler_params=VMEM,
        cost_estimate=cost(50),
        name="attention_backward",
    )(n1t, qkv, probs, gatt, attended)


def input_kernel(tok_ref, gp_ref, gmid_ref, w_ref, norms_ref, two_ref, gin_ref, terms_ref):
    rows, width = tok_ref.shape
    gone = mm(gp_ref[0], w_ref[0], NT)
    for pair in range(1, w_ref.shape[0]):
        gone = gone + mm(gp_ref[pair], w_ref[pair], NT)
    normal, rs = normalize(tok_ref[...].astype(F32))

    @pl.when(pl.program_id(0) == 0)
    def _():
        terms_ref[...] = jnp.zeros_like(terms_ref)
        terms_ref[2:3, :] = jnp.sum(two_ref[0:8, :], axis=0, keepdims=True)
        terms_ref[3:4, :] = jnp.sum(two_ref[8:16, :], axis=0, keepdims=True)

    terms_ref[0:1, :] += jnp.sum(gone * normal, axis=0, keepdims=True)
    terms_ref[1:2, :] += jnp.sum(gone, axis=0, keepdims=True)
    gin_ref[...] = gmid_ref[...] + norm_backward(normal, rs, gone * norms_ref[0:1, :])


def input_gradient(tokens, gp, gmid, wpairs, norms, gnorm_two):
    seqs, rows, width = tokens.shape
    pairs = width // PAIR
    sq = pl.squeezed
    full = pl.BlockSpec((sq, rows, width), lambda s: (s, 0, 0))
    whole = lambda *dims: pl.BlockSpec(dims, lambda s: (0,) * len(dims))
    shape = jax.ShapeDtypeStruct
    return pl.pallas_call(
        input_kernel,
        grid=(seqs,),
        in_specs=[
            full,
            pl.BlockSpec((sq, pairs, rows, 3 * PAIR), lambda s: (s, 0, 0, 0)),
            full,
            whole(pairs, width, 3 * PAIR),
            whole(4, width),
            whole(16, width),
        ],
        out_specs=[full, whole(8, width)],
        out_shape=[shape((seqs, rows, width), F32), shape((8, width), F32)],
        compiler_params=VMEM,
        cost_estimate=cost(12),
        name="input_gradient",
    )(tokens, gp, gmid, wpairs, norms, gnorm_two)


def pack_kernel(qkv_ref, out_ref, up_ref, down_ref, norm_ref, lead_ref, rest_ref):
    chips, rows, _ = lead_ref.shape
    part = norm_ref.shape[1]
    norm = norm_ref[...]
    high = norm.astype(BF16).astype(F32)
    row = lax.broadcasted_iota(jnp.int32, (rows, part), 0)
    extra = jnp.where(row == 0, high, jnp.where(row == 1, norm - high, 0.0))
    columns = [qkv_ref[c, :, :PAIR] for c in range(3)] + [qkv_ref[c, :, PAIR:] for c in range(3)]
    blank = jnp.zeros((rows, HD - part), F32)
    lead_ref[...] = jnp.broadcast_to(
        jnp.concatenate(columns + [extra, blank], axis=1).astype(BF16)[None], lead_ref.shape
    )
    blank = jnp.zeros((rows, HD), F32)
    rest_ref[...] = jnp.concatenate([up_ref[...], down_ref[...], out_ref[...], blank], axis=1).astype(BF16)


def sum_kernel(parts_ref, rest_ref, terms_ref, lead_ref, message_ref):
    parts = parts_ref[...].astype(F32)
    lead = jnp.sum(parts, axis=0)
    lead_ref[...] = lead
    rest = rest_ref[...].astype(F32)
    lanes = message_ref.shape[1]
    total = jnp.zeros((lead.shape[0], PAIR), F32)
    for values in (lead, rest):
        for start in range(0, values.shape[1], PAIR):
            piece = values[:, start : start + PAIR]
            total = total + piece * piece
    message_ref[...] = terms_ref[...]
    message_ref[4:5, :PAIR] = jnp.sum(total, axis=0, keepdims=True)


def adamw(master, gradient, moments, rate, decay):
    moment = BETA_ONE * moments[0] + (1.0 - BETA_ONE) * gradient
    second = BETA_TWO * moments[1] + (1.0 - BETA_TWO) * gradient * gradient
    step_size = (
        moment / (1.0 - BETA_ONE**STEP) / (jnp.sqrt(second / (1.0 - BETA_TWO**STEP)) + ADAM_EPS)
    )
    return master - rate * (step_size + decay * master), moment, second


def update_kernel(
    message_ref, mine_ref, lead_ref, rest_ref,
    qkv_ref, out_ref, up_ref, down_ref, norm_ref,
    qkv_m_ref, out_m_ref, up_m_ref, down_m_ref, norm_m_ref,
    gn_ref, qkv_n_ref, out_n_ref, up_n_ref, down_n_ref, norm_n_ref,
    qkv_s_ref, out_s_ref, up_s_ref, down_s_ref, norm_s_ref, grads_ref,
):
    units = up_ref.shape[1]
    terms = message_ref[0:4, :]
    squares = jnp.sum(terms * terms, axis=(0, 1), keepdims=True) + jnp.sum(
        message_ref[4:5, :], axis=(0, 1), keepdims=True
    )
    grad_norm = jnp.sqrt(squares)
    gn_ref[...] = grad_norm
    factor = jnp.minimum(1.0, CLIP_NORM / (grad_norm + 1e-06))
    for c in range(3):
        wide = lead_ref[:, c * PAIR : (c + 1) * PAIR]
        narrow = lead_ref[:, 3 * PAIR + c * HD : 3 * PAIR + (c + 1) * HD]
        for cols, grad in ((slice(0, PAIR), wide), (slice(PAIR, PAIR + HD), narrow)):
            new, moment, second = adamw(
                qkv_ref[c, :, cols], factor * grad, qkv_m_ref[:, c, :, cols], RATE_LIST[0], DECAY_LIST[0]
            )
            qkv_n_ref[c, :, cols] = new
            qkv_s_ref[0, c, :, cols] = moment
            qkv_s_ref[1, c, :, cols] = second
    norm_grads = factor * mine_ref[...]
    grads_ref[...] = norm_grads
    plain = (
        (out_ref, rest_ref[:, 2 * units : 2 * units + 3 * HD], out_m_ref, out_n_ref, out_s_ref, 1),
        (up_ref, rest_ref[:, :units], up_m_ref, up_n_ref, up_s_ref, 2),
        (down_ref, rest_ref[:, units : 2 * units], down_m_ref, down_n_ref, down_s_ref, 3),
    )
    for master, grad, moments, next_ref, state_ref, i in plain:
        next_ref[...], state_ref[0], state_ref[1] = adamw(
            master[...], factor * grad.astype(F32), moments[...], RATE_LIST[i], DECAY_LIST[i]
        )
    norm_n_ref[...], norm_s_ref[0:1, :], norm_s_ref[1:2, :] = adamw(
        norm_ref[...], norm_grads, (norm_m_ref[0:1, :], norm_m_ref[1:2, :]), RATE_LIST[4], DECAY_LIST[4]
    )


def small_call(kernel, name, out_shape, *operands):
    return pl.pallas_call(kernel, out_shape=out_shape, compiler_params=VMEM, cost_estimate=cost(3), name=name)(
        *operands
    )


def swap(values):
    return lax.ppermute(values, "head", [(0, 1), (1, 0)])


def per_device(
    groups,
    tokens,
    cotangent,
    lengths,
    key_masks,
    qkv_master,
    out_master,
    up_master,
    down_master,
    norm_master,
    qkv_moments,
    out_moments,
    up_moments,
    down_moments,
    norm_moments,
):
    seqs, slot_rows, width = tokens.shape
    chips = groups[2]
    shard_rows = qkv_master.shape[0]
    norm_part = norm_master.shape[0]
    units = up_master.shape[1]
    side = lax.axis_index("head")
    own_first = side == 0

    qkv_rows = qkv_master.transpose(1, 0, 2)
    masters = (qkv_rows, out_master.T, up_master, down_master.T, norm_master[None])
    shape = jax.ShapeDtypeStruct
    lead, rest = small_call(
        pack_kernel,
        "pack_weights",
        [shape((chips, shard_rows, 10 * HD), BF16), shape((shard_rows, 2 * units + 4 * HD), BF16)],
        *masters,
    )
    lead_own = lax.all_to_all(lead, "batch", 0, 0)
    rest_own = lax.all_gather(rest, "batch", axis=0, tiled=True)
    lead_other = swap(lead_own)

    def norms_of(gathered):
        parts = gathered[:, :2, 9 * HD : 9 * HD + norm_part].astype(F32)
        return parts[:, 0] + parts[:, 1]

    norms_own, norms_other = norms_of(lead_own), norms_of(lead_other)
    norms = jnp.stack(
        [jnp.where(own_first, norms_own, norms_other), jnp.where(own_first, norms_other, norms_own)], axis=1
    ).reshape(4, width)

    positions = jnp.arange(slot_rows, dtype=jnp.int32)
    own_lengths = lax.dynamic_slice_in_dim(lengths, side * seqs, seqs)
    own_masks = lax.dynamic_slice_in_dim(key_masks, side * seqs, seqs)
    visible = (positions[None, :] < own_lengths[:, None]) & ((own_masks == 1) | (positions[None, :] == 0))
    bias = jnp.where(visible, 0.0, -1e30).astype(F32)[:, None, :]

    flat = lambda a: a.reshape(chips * shard_rows, a.shape[-1])
    n1t, qkv, attended, probs, wpairs = forward(tokens, bias, flat(lead_own), flat(lead_other), norms)
    rest_own, attended = lax.optimization_barrier((rest_own, attended))
    rest_other = swap(rest_own)
    block_out, gmid, gatt, grest_own, grest_other, gnorm_two = middle(
        own_lengths, tokens, cotangent, attended, rest_own, rest_other, norms
    )
    per_seq = lambda a: a.reshape(seqs, slot_rows, width)
    rest_sum = (grest_own.astype(F32) + swap(grest_other).astype(F32)).astype(BF16)
    rest_part = lax.psum_scatter(
        rest_sum, "batch", scatter_dimension=0, tiled=True, axis_index_groups=groups[0]
    )
    gp, glead_own, glead_other = backward(n1t, qkv, probs, per_seq(gatt), attended)
    rest_part, glead_own, glead_other = lax.optimization_barrier((rest_part, glead_own, glead_other))
    rest_shard = lax.psum_scatter(
        rest_part, "batch", scatter_dimension=0, tiled=True, axis_index_groups=groups[1]
    )
    lead_sum = (glead_own.astype(F32) + swap(glead_other).astype(F32)).astype(BF16)
    lead_parts = lax.all_to_all(lead_sum.reshape(chips, shard_rows, 10 * HD), "batch", 0, 0)
    input_grad, terms = input_gradient(tokens, gp, per_seq(gmid), wpairs, norms, gnorm_two)
    lead_shard, message = small_call(
        sum_kernel,
        "sum_parts",
        [shape((shard_rows, 10 * HD), F32), shape(terms.shape, F32)],
        lead_parts,
        rest_shard,
        terms,
    )
    message = message + swap(message)
    stride = 1
    while stride < chips:
        message = message + lax.ppermute(message, "batch", [(i, i ^ stride) for i in range(chips)])
        stride *= 2
    place = (lax.axis_index("batch") * 2 + side) * norm_part
    mine = lax.dynamic_slice_in_dim(message[:4].reshape(1, 4 * width), place, norm_part, axis=1)
    like = lambda a: shape(a.shape, F32)
    moments = (
        qkv_moments.transpose(0, 2, 1, 3),
        out_moments.transpose(0, 2, 1),
        up_moments,
        down_moments.transpose(0, 2, 1),
        norm_moments,
    )
    results = small_call(
        update_kernel,
        "update_weights",
        [shape((1, 1), F32)] + [like(a) for a in masters + moments] + [like(mine)],
        message,
        mine,
        lead_shard,
        rest_shard,
        *masters,
        *moments,
    )
    grad_norm, qkv_next, out_next, up_next, down_next, norm_next = results[:6]
    qkv_states, out_states, up_states, down_states, norm_states, norm_grads = results[6:]
    return (
        per_seq(block_out),
        input_grad,
        grad_norm.reshape(()),
        qkv_next.transpose(1, 0, 2),
        out_next.T,
        up_next,
        down_next.T,
        norm_next[0],
        qkv_states.transpose(0, 2, 1, 3),
        out_states.transpose(0, 2, 1),
        up_states,
        down_states.transpose(0, 2, 1),
        norm_states,
        norm_grads[0],
    )


def solution(mesh):
    chips = mesh.shape["batch"]
    near = 4
    outer = [[c + near * z for z in range(chips // near)] for c in range(near)]
    inner = [[near * z + c for c in range(near)] for z in range(chips // near)]
    return jax.shard_map(
        functools.partial(per_device, (outer, inner, chips)),
        mesh=mesh,
        in_specs=(
            P(("batch", "head"), None, None),
            P(("batch", "head"), None, None),
            P("batch"),
            P("batch", None),
            P("batch", None, "head"),
            P("head", "batch"),
            P("batch", "head"),
            P("head", "batch"),
            P(("batch", "head")),
            P(None, "batch", None, "head"),
            P(None, "head", "batch"),
            P(None, "batch", "head"),
            P(None, "head", "batch"),
            P(None, ("batch", "head")),
        ),
        out_specs=(
            P(("batch", "head"), None, None),
            P(("batch", "head"), None, None),
            P(),
            P("batch", None, "head"),
            P("head", "batch"),
            P("batch", "head"),
            P("head", "batch"),
            P(("batch", "head")),
            P(None, "batch", None, "head"),
            P(None, "head", "batch"),
            P(None, "batch", "head"),
            P(None, "head", "batch"),
            P(None, ("batch", "head")),
            P(("batch", "head")),
        ),
        check_vma=False,
    )
```

```python
import functools

import jax
import jax.numpy as jnp
from jax import lax
from jax.experimental import pallas as pl
from jax.experimental.pallas import tpu as pltpu
from jax.sharding import PartitionSpec as P

HD = 64
STEP = 10
NORM_EPS = 1e-06
CLIP_NORM = 1000.0
BETA_ONE = 0.5
BETA_TWO = 0.5
ADAM_EPS = 1e-08
RATE_LIST = (0.06, 0.25, 0.06, 0.03, 0.5)
DECAY_LIST = (0.04, 0.04, 0.04, 0.04, 0.0)

F32 = jnp.float32
BF16 = jnp.bfloat16
NN = (((1,), (0,)), ((), ()))
NT = (((1,), (1,)), ((), ()))
TN = (((0,), (0,)), ((), ()))
QB = 128
FB = 512
FC = 256
PAIR = 2 * HD
VMEM = pltpu.CompilerParams(vmem_limit_bytes=56 * 2**20)


def cost(microseconds):
    return pl.CostEstimate(flops=microseconds * 1_000_000_000, bytes_accessed=1_000_000, transcendentals=0)


def mm(left, right, dims=NN):
    return lax.dot_general(left, right, dims, preferred_element_type=F32)


def normalize(values):
    centred = values - jnp.mean(values, axis=-1, keepdims=True)
    variance = jnp.mean(centred * centred, axis=-1, keepdims=True)
    rs = lax.rsqrt(variance + NORM_EPS)
    return centred * rs, rs


def norm_backward(normal, rs, gained):
    inner = jnp.mean(gained * normal, axis=-1, keepdims=True)
    return rs * (gained - jnp.mean(gained, axis=-1, keepdims=True) - normal * inner)


def gelu_parts(h):
    gauss = jnp.exp(h * h * -0.5)
    t = 1.0 / (1.0 + (0.3275911 * 0.7071067811865476) * jnp.abs(h))
    poly = t * (
        0.127414796
        + t * (-0.142248368 + t * (0.7107068705 + t * (-0.7265760135 + t * 0.5307027145)))
    )
    tail = poly * gauss
    return jnp.where(h < 0.0, tail, 1.0 - tail), gauss


def split_pairs(own, other, per_pair):
    wide, narrow = 2 * per_pair, per_pair
    singles = []
    for part in range(per_pair // HD):
        cols = slice(wide + part * HD, wide + (part + 1) * HD)
        singles += [own[:, cols], other[:, cols]]
    return own[:, :wide], jnp.concatenate(singles, axis=1), other[:, :wide]


def join_pairs(first, second, third, per_pair):
    parts = [
        [second[:, p * PAIR + side * HD : p * PAIR + (side + 1) * HD] for p in range(per_pair // HD)]
        for side in range(2)
    ]
    return [first] + parts[0], [third] + parts[1]


def forward_kernel(
    tok_ref, bias_ref, own_ref, other_ref, norms_ref, n1t_ref, qkv_ref, att_ref, p_ref, w_ref
):
    rows, width = tok_ref.shape

    @pl.when(pl.program_id(0) == 0)
    def _():
        cols = 9 * HD
        for i, part in enumerate(split_pairs(own_ref[:, :cols], other_ref[:, :cols], 3 * HD)):
            w_ref[i] = part

    x = tok_ref[...].astype(F32)
    normal, _ = normalize(x)
    n1 = (normal * norms_ref[0:1, :] + norms_ref[1:2, :]).astype(BF16)
    n1t_ref[...] = n1.T
    bias = bias_ref[...]
    lane = lax.broadcasted_iota(jnp.int32, (QB, PAIR), 1)
    for pair in range(width // PAIR):
        part = mm(n1, w_ref[pair])
        qkv_ref[pair, :, :PAIR] = (part[:, :PAIR].astype(BF16).astype(F32) * (HD**-0.5)).astype(BF16)
        qkv_ref[pair, :, PAIR:] = part[:, PAIR:].astype(BF16)
        kp = qkv_ref[pair, :, PAIR : 2 * PAIR]
        vp = qkv_ref[pair, :, 2 * PAIR :]
        for qb in range(rows // QB):
            sl = slice(qb * QB, (qb + 1) * QB)
            qp = qkv_ref[pair, sl, :PAIR]
            outs = []
            for half in range(2):
                qm = jnp.where((lane < HD) == (half == 0), qp, jnp.zeros_like(qp))
                s = mm(qm, kp, NT) + bias
                e = jnp.exp(s - jnp.max(s, axis=-1, keepdims=True))
                p = (e * (1.0 / jnp.sum(e, axis=-1, keepdims=True))).astype(BF16)
                p_ref[pair * 2 + half, sl, :] = p
                outs.append(mm(p, vp))
            att_ref[sl, pair * PAIR : (pair + 1) * PAIR] = jnp.where(
                lane < HD, outs[0], outs[1]
            ).astype(BF16)


def forward(tokens, bias, own, other, norms):
    seqs, rows, width = tokens.shape
    heads, pairs = width // HD, width // PAIR
    sq = pl.squeezed
    shape = jax.ShapeDtypeStruct
    whole = lambda *dims: pl.BlockSpec(dims, lambda s: (0,) * len(dims))
    return pl.pallas_call(
        forward_kernel,
        grid=(seqs,),
        in_specs=[
            pl.BlockSpec((sq, rows, width), lambda s: (s, 0, 0)),
            pl.BlockSpec((sq, 1, rows), lambda s: (s, 0, 0)),
            whole(*own.shape),
            whole(*other.shape),
            whole(4, width),
        ],
        out_specs=[
            pl.BlockSpec((sq, width, rows), lambda s: (s, 0, 0)),
            pl.BlockSpec((sq, pairs, rows, 3 * PAIR), lambda s: (s, 0, 0, 0)),
            pl.BlockSpec((sq, rows, width), lambda s: (s, 0, 0)),
            pl.BlockSpec((sq, heads, rows, rows), lambda s: (s, 0, 0, 0)),
            whole(pairs, width, 3 * PAIR),
        ],
        out_shape=[
            shape((seqs, width, rows), BF16),
            shape((seqs, pairs, rows, 3 * PAIR), BF16),
            shape((seqs, rows, width), BF16),
            shape((seqs, heads, rows, rows), BF16),
            shape((pairs, width, 3 * PAIR), BF16),
        ],
        compiler_params=VMEM,
        cost_estimate=cost(50),
        name="attention_forward",
    )(tokens, bias, own, other, norms)


def middle_kernel(
    seq_rows, units, len_ref, tok_ref, cot_ref, att_ref, own_ref, other_ref, norms_ref,
    out_ref, gmid_ref, gatt_ref, gown_ref, gother_ref, gnorm_ref,
    wo_ref, gout_ref, gup_ref, gdown_ref,
):
    step = pl.program_id(0)
    rows, width = tok_ref.shape
    halves = (own_ref, other_ref)

    @pl.when(step == 0)
    def _():
        gout_ref[...] = jnp.zeros_like(gout_ref)
        gup_ref[...] = jnp.zeros_like(gup_ref)
        gdown_ref[...] = jnp.zeros_like(gdown_ref)
        gnorm_ref[...] = jnp.zeros_like(gnorm_ref)
        cols = slice(2 * units, 2 * units + 3 * HD)
        parts = split_pairs(own_ref[:, cols], other_ref[:, cols], HD)
        for i, part in enumerate(parts):
            wo_ref[:, i * PAIR : (i + 1) * PAIR] = part

    first = step * rows
    row = first + lax.broadcasted_iota(jnp.int32, (rows, 1), 0)
    live = row < 0
    last = len_ref.shape[0] - 1
    for near in range(-(-rows // seq_rows) + 1):
        s = first // seq_rows + near
        bound = jnp.where(s <= last, len_ref[jnp.minimum(s, last)], 0)
        live = live | ((row >= s * seq_rows) & (row < s * seq_rows + bound))

    x = tok_ref[...].astype(F32)
    att = att_ref[...]
    mid = x + mm(att, wo_ref[...], NT)
    normal, rs = normalize(mid)
    gain, shift = norms_ref[2:3, :], norms_ref[3:4, :]
    n2 = (normal * gain + shift).astype(BF16)
    n2t = n2.T
    up = jnp.where(live, cot_ref[...].astype(F32), 0.0)
    gb = up.astype(BF16)
    gbt = gb.T
    bo = mid
    gtwo = jnp.zeros_like(mid)
    for half in range(2):
        for c in range(units // FC):
            cols = slice(c * FC, (c + 1) * FC)
            wu = halves[half][:, c * FC : (c + 1) * FC]
            wd = halves[half][:, units + c * FC : units + (c + 1) * FC]
            h = mm(n2, wu)
            ga = mm(gb, wd)
            cdf, gauss = gelu_parts(h)
            act = (h * cdf).astype(BF16)
            gh = (ga * (cdf + h * (gauss * 0.3989422804014327))).astype(BF16)
            bo = bo + mm(act, wd, NT)
            gtwo = gtwo + mm(gh, wu, NT)
            gup_ref[half, :, cols] += mm(n2t, gh)
            gdown_ref[half, :, cols] += mm(gbt, act)
    out_ref[...] = bo.astype(BF16)
    gnorm_ref[0:8, :] += jnp.sum((gtwo * normal).reshape(rows // 8, 8, width), axis=0)
    gnorm_ref[8:16, :] += jnp.sum(gtwo.reshape(rows // 8, 8, width), axis=0)
    gmid = up + norm_backward(normal, rs, gtwo * gain)
    gmid_ref[...] = gmid
    gm = gmid.astype(BF16)
    gout_ref[...] += mm(gm, att, TN)
    gatt_ref[...] = mm(gm, wo_ref[...]).astype(BF16)

    @pl.when(step == pl.num_programs(0) - 1)
    def _():
        total = gout_ref[...]
        sides = join_pairs(
            total[:, :PAIR], total[:, PAIR : 2 * PAIR], total[:, 2 * PAIR :], HD
        )
        for half, ref in enumerate((gown_ref, gother_ref)):
            ref[:, :units] = gup_ref[half].astype(BF16)
            ref[:, units : 2 * units] = gdown_ref[half].astype(BF16)
            blank = jnp.zeros((total.shape[0], HD), F32)
            ref[:, 2 * units :] = jnp.concatenate(sides[half] + [blank], axis=1).astype(BF16)


def middle(lengths, tokens, cotangent, attended, own, other, norms):
    seqs, seq_rows, width = tokens.shape
    total = seqs * seq_rows
    packed = own.shape[1]
    units = (packed - 4 * HD) // 2
    flat = lambda a: a.reshape(total, width)
    rowspec = pl.BlockSpec((FB, width), lambda s: (s, 0))
    whole = lambda *dims: pl.BlockSpec(dims, lambda s: (0,) * len(dims))
    shape = jax.ShapeDtypeStruct
    return pl.pallas_call(
        functools.partial(middle_kernel, seq_rows, units),
        grid=(total // FB,),
        in_specs=[
            pl.BlockSpec(memory_space=pltpu.SMEM),
            rowspec,
            rowspec,
            rowspec,
            whole(*own.shape),
            whole(*other.shape),
            whole(4, width),
        ],
        out_specs=[rowspec] * 3 + [whole(*own.shape), whole(*own.shape), whole(16, width)],
        out_shape=[
            shape((total, width), BF16),
            shape((total, width), F32),
            shape((total, width), BF16),
            shape(own.shape, BF16),
            shape(own.shape, BF16),
            shape((16, width), F32),
        ],
        scratch_shapes=[
            pltpu.VMEM((width, width), BF16),
            pltpu.VMEM((width, width), F32),
            pltpu.VMEM((2, width, units), F32),
            pltpu.VMEM((2, width, units), F32),
        ],
        compiler_params=VMEM,
        cost_estimate=cost(50),
        name="feed_forward",
    )(lengths, flat(tokens), flat(cotangent), flat(attended), own, other, norms)


def backward_kernel(
    n1t_ref, qkv_ref, p_ref, gatt_ref, att_ref, gp_ref, gown_ref, gother_ref, gqkv_ref
):
    seq, pair = pl.program_id(0), pl.program_id(1)
    rows = qkv_ref.shape[0]
    qp, kp, vp = qkv_ref[:, :PAIR], qkv_ref[:, PAIR : 2 * PAIR], qkv_ref[:, 2 * PAIR :]
    ga = gatt_ref[...]
    prod = ga.astype(F32) * att_ref[...].astype(F32)
    lane = lax.broadcasted_iota(jnp.int32, (QB, PAIR), 1)
    gat, qt = ga.T, qp.T
    zero = jnp.zeros((QB, PAIR), BF16)
    gq = [[], []]
    gkt, gvt = [], []
    for half in range(2):
        ds_all = []
        mask = (lane < HD) == (half == 0)
        for qb in range(rows // QB):
            sl = slice(qb * QB, (qb + 1) * QB)
            dp = mm(jnp.where(mask, ga[sl], zero), vp, NT)
            inner = jnp.sum(jnp.where(mask, prod[sl], 0.0), axis=-1, keepdims=True)
            ds = (p_ref[half, sl, :].astype(F32) * (dp - inner)).astype(BF16)
            ds_all.append(ds)
            gq[half].append(mm(ds, kp))
        ds = jnp.concatenate(ds_all, axis=0)
        hs = slice(half * HD, half * HD + HD)
        gkt.append(mm(qt[hs], ds))
        gvt.append(mm(gat[hs], p_ref[half]))
    for qb in range(rows // QB):
        sl = slice(qb * QB, (qb + 1) * QB)
        joined = jnp.where(lane < HD, gq[0][qb], gq[1][qb])
        gp_ref[sl, :PAIR] = (joined * (HD**-0.5)).astype(BF16)
    gp_ref[:, PAIR : 2 * PAIR] = jnp.concatenate(gkt, axis=0).astype(BF16).T
    gp_ref[:, 2 * PAIR :] = jnp.concatenate(gvt, axis=0).astype(BF16).T
    new = mm(n1t_ref[...], gp_ref[...])

    @pl.when(seq == 0)
    def _():
        gqkv_ref[pair] = new

    @pl.when(seq > 0)
    def _():
        gqkv_ref[pair] += new

    @pl.when((seq == pl.num_programs(0) - 1) & (pair == pl.num_programs(1) - 1))
    def _():
        sides = join_pairs(gqkv_ref[0], gqkv_ref[1], gqkv_ref[2], 3 * HD)
        blank = jnp.zeros((gqkv_ref.shape[1], HD), F32)
        for columns, ref in zip(sides, (gown_ref, gother_ref)):
            ref[...] = jnp.concatenate(columns + [blank], axis=1).astype(BF16)


def backward(n1t, qkv, probs, gatt, attended):
    seqs, rows, width = attended.shape
    pairs = width // PAIR
    sq = pl.squeezed
    pairspec = pl.BlockSpec((sq, rows, PAIR), lambda s, p: (s, 0, p))
    groupspec = pl.BlockSpec((sq, sq, rows, 3 * PAIR), lambda s, p: (s, p, 0, 0))
    whole = lambda *dims: pl.BlockSpec(dims, lambda s, p: (0,) * len(dims))
    shape = jax.ShapeDtypeStruct
    packed = (width, 10 * HD)
    return pl.pallas_call(
        backward_kernel,
        grid=(seqs, pairs),
        in_specs=[
            pl.BlockSpec((sq, width, rows), lambda s, p: (s, 0, 0)),
            groupspec,
            pl.BlockSpec((sq, 2, rows, rows), lambda s, p: (s, p, 0, 0)),
            pairspec,
            pairspec,
        ],
        out_specs=[groupspec, whole(*packed), whole(*packed)],
        out_shape=[shape(qkv.shape, BF16), shape(packed, BF16), shape(packed, BF16)],
        scratch_shapes=[pltpu.VMEM((pairs, width, 3 * PAIR), F32)],
        compiler_params=VMEM,
        cost_estimate=cost(50),
        name="attention_backward",
    )(n1t, qkv, probs, gatt, attended)


def input_kernel(tok_ref, gp_ref, gmid_ref, w_ref, norms_ref, two_ref, gin_ref, terms_ref):
    rows, width = tok_ref.shape
    gone = mm(gp_ref[0], w_ref[0], NT)
    for pair in range(1, w_ref.shape[0]):
        gone = gone + mm(gp_ref[pair], w_ref[pair], NT)
    normal, rs = normalize(tok_ref[...].astype(F32))

    @pl.when(pl.program_id(0) == 0)
    def _():
        terms_ref[...] = jnp.zeros_like(terms_ref)
        terms_ref[2:3, :] = jnp.sum(two_ref[0:8, :], axis=0, keepdims=True)
        terms_ref[3:4, :] = jnp.sum(two_ref[8:16, :], axis=0, keepdims=True)

    terms_ref[0:1, :] += jnp.sum(gone * normal, axis=0, keepdims=True)
    terms_ref[1:2, :] += jnp.sum(gone, axis=0, keepdims=True)
    gin_ref[...] = gmid_ref[...] + norm_backward(normal, rs, gone * norms_ref[0:1, :])


def input_gradient(tokens, gp, gmid, wpairs, norms, gnorm_two):
    seqs, rows, width = tokens.shape
    pairs = width // PAIR
    sq = pl.squeezed
    full = pl.BlockSpec((sq, rows, width), lambda s: (s, 0, 0))
    whole = lambda *dims: pl.BlockSpec(dims, lambda s: (0,) * len(dims))
    shape = jax.ShapeDtypeStruct
    return pl.pallas_call(
        input_kernel,
        grid=(seqs,),
        in_specs=[
            full,
            pl.BlockSpec((sq, pairs, rows, 3 * PAIR), lambda s: (s, 0, 0, 0)),
            full,
            whole(pairs, width, 3 * PAIR),
            whole(4, width),
            whole(16, width),
        ],
        out_specs=[full, whole(8, width)],
        out_shape=[shape((seqs, rows, width), F32), shape((8, width), F32)],
        compiler_params=VMEM,
        cost_estimate=cost(12),
        name="input_gradient",
    )(tokens, gp, gmid, wpairs, norms, gnorm_two)


def pack_kernel(qkv_ref, out_ref, up_ref, down_ref, norm_ref, lead_ref, rest_ref):
    chips, rows, _ = lead_ref.shape
    part = norm_ref.shape[1]
    norm = norm_ref[...]
    high = norm.astype(BF16).astype(F32)
    row = lax.broadcasted_iota(jnp.int32, (rows, part), 0)
    extra = jnp.where(row == 0, high, jnp.where(row == 1, norm - high, 0.0))
    columns = [qkv_ref[c, :, :PAIR] for c in range(3)] + [qkv_ref[c, :, PAIR:] for c in range(3)]
    blank = jnp.zeros((rows, HD - part), F32)
    lead_ref[...] = jnp.broadcast_to(
        jnp.concatenate(columns + [extra, blank], axis=1).astype(BF16)[None], lead_ref.shape
    )
    blank = jnp.zeros((rows, HD), F32)
    rest_ref[...] = jnp.broadcast_to(
        jnp.concatenate([up_ref[...], down_ref[...], out_ref[...], blank], axis=1).astype(BF16)[None], rest_ref.shape
    )


def sum_kernel(lead_parts_ref, rest_parts_ref, terms_ref, lead_ref, rest_ref, message_ref):
    total = jnp.zeros((lead_ref.shape[0], PAIR), F32)
    for parts_ref, ref in ((lead_parts_ref, lead_ref), (rest_parts_ref, rest_ref)):
        for start in range(0, ref.shape[1], PAIR):
            cols = slice(start, start + PAIR)
            piece = jnp.sum(parts_ref[:, :, cols].astype(F32), axis=0)
            ref[:, cols] = piece
            total = total + piece * piece
    message_ref[...] = terms_ref[...]
    message_ref[4:5, :PAIR] = jnp.sum(total, axis=0, keepdims=True)


def adamw(master, gradient, moments, rate, decay):
    moment = BETA_ONE * moments[0] + (1.0 - BETA_ONE) * gradient
    second = BETA_TWO * moments[1] + (1.0 - BETA_TWO) * gradient * gradient
    step_size = (
        moment / (1.0 - BETA_ONE**STEP) / (jnp.sqrt(second / (1.0 - BETA_TWO**STEP)) + ADAM_EPS)
    )
    return master - rate * (step_size + decay * master), moment, second


def update_kernel(
    message_ref, mine_ref, lead_ref, rest_ref,
    qkv_ref, out_ref, up_ref, down_ref, norm_ref,
    qkv_m_ref, out_m_ref, up_m_ref, down_m_ref, norm_m_ref,
    gn_ref, qkv_n_ref, out_n_ref, up_n_ref, down_n_ref, norm_n_ref,
    qkv_s_ref, out_s_ref, up_s_ref, down_s_ref, norm_s_ref, grads_ref,
):
    units = up_ref.shape[1]
    terms = message_ref[0:4, :]
    squares = jnp.sum(terms * terms, axis=(0, 1), keepdims=True) + jnp.sum(
        message_ref[4:5, :], axis=(0, 1), keepdims=True
    )
    grad_norm = jnp.sqrt(squares)
    gn_ref[...] = grad_norm
    factor = jnp.minimum(1.0, CLIP_NORM / (grad_norm + 1e-06))
    for c in range(3):
        wide = lead_ref[:, c * PAIR : (c + 1) * PAIR]
        narrow = lead_ref[:, 3 * PAIR + c * HD : 3 * PAIR + (c + 1) * HD]
        for cols, grad in ((slice(0, PAIR), wide), (slice(PAIR, PAIR + HD), narrow)):
            new, moment, second = adamw(
                qkv_ref[c, :, cols], factor * grad, qkv_m_ref[:, c, :, cols], RATE_LIST[0], DECAY_LIST[0]
            )
            qkv_n_ref[c, :, cols] = new
            qkv_s_ref[0, c, :, cols] = moment
            qkv_s_ref[1, c, :, cols] = second
    norm_grads = factor * mine_ref[...]
    grads_ref[...] = norm_grads
    plain = (
        (out_ref, rest_ref[:, 2 * units : 2 * units + 3 * HD], out_m_ref, out_n_ref, out_s_ref, 1),
        (up_ref, rest_ref[:, :units], up_m_ref, up_n_ref, up_s_ref, 2),
        (down_ref, rest_ref[:, units : 2 * units], down_m_ref, down_n_ref, down_s_ref, 3),
    )
    for master, grad, moments, next_ref, state_ref, i in plain:
        next_ref[...], state_ref[0], state_ref[1] = adamw(
            master[...], factor * grad, moments[...], RATE_LIST[i], DECAY_LIST[i]
        )
    norm_n_ref[...], norm_s_ref[0:1, :], norm_s_ref[1:2, :] = adamw(
        norm_ref[...], norm_grads, (norm_m_ref[0:1, :], norm_m_ref[1:2, :]), RATE_LIST[4], DECAY_LIST[4]
    )


def small_call(kernel, name, out_shape, *operands):
    return pl.pallas_call(kernel, out_shape=out_shape, compiler_params=VMEM, cost_estimate=cost(3), name=name)(
        *operands
    )


def swap(values):
    return lax.ppermute(values, "head", [(0, 1), (1, 0)])


def per_device(
    chips,
    tokens,
    cotangent,
    lengths,
    key_masks,
    qkv_master,
    out_master,
    up_master,
    down_master,
    norm_master,
    qkv_moments,
    out_moments,
    up_moments,
    down_moments,
    norm_moments,
):
    seqs, slot_rows, width = tokens.shape
    shard_rows = qkv_master.shape[0]
    norm_part = norm_master.shape[0]
    units = up_master.shape[1]
    side = lax.axis_index("head")
    own_first = side == 0

    qkv_rows = qkv_master.transpose(1, 0, 2)
    masters = (qkv_rows, out_master.T, up_master, down_master.T, norm_master[None])
    shape = jax.ShapeDtypeStruct
    lead, rest = small_call(
        pack_kernel,
        "pack_weights",
        [shape((chips, shard_rows, 10 * HD), BF16), shape((chips, shard_rows, 2 * units + 4 * HD), BF16)],
        *masters,
    )
    lead_own = lax.all_to_all(lead, "batch", 0, 0)
    lead_own, rest = lax.optimization_barrier((lead_own, rest))
    rest_own = lax.all_to_all(rest, "batch", 0, 0)
    lead_other = swap(lead_own)

    def norms_of(gathered):
        parts = gathered[:, :2, 9 * HD : 9 * HD + norm_part].astype(F32)
        return parts[:, 0] + parts[:, 1]

    norms_own, norms_other = norms_of(lead_own), norms_of(lead_other)
    norms = jnp.stack(
        [jnp.where(own_first, norms_own, norms_other), jnp.where(own_first, norms_other, norms_own)], axis=1
    ).reshape(4, width)

    positions = jnp.arange(slot_rows, dtype=jnp.int32)
    own_lengths = lax.dynamic_slice_in_dim(lengths, side * seqs, seqs)
    own_masks = lax.dynamic_slice_in_dim(key_masks, side * seqs, seqs)
    visible = (positions[None, :] < own_lengths[:, None]) & ((own_masks == 1) | (positions[None, :] == 0))
    bias = jnp.where(visible, 0.0, -1e30).astype(F32)[:, None, :]

    flat = lambda a: a.reshape(chips * shard_rows, a.shape[-1])
    n1t, qkv, attended, probs, wpairs = forward(tokens, bias, flat(lead_own), flat(lead_other), norms)
    rest_own, attended = lax.optimization_barrier((rest_own, attended))
    rest_other = swap(rest_own)
    block_out, gmid, gatt, grest_own, grest_other, gnorm_two = middle(
        own_lengths, tokens, cotangent, attended, flat(rest_own), flat(rest_other), norms
    )
    per_seq = lambda a: a.reshape(seqs, slot_rows, width)
    rest_sum = (grest_own.astype(F32) + swap(grest_other).astype(F32)).astype(BF16)
    rest_parts = lax.all_to_all(rest_sum.reshape(rest.shape), "batch", 0, 0)
    gp, glead_own, glead_other = backward(n1t, qkv, probs, per_seq(gatt), attended)
    lead_sum = (glead_own.astype(F32) + swap(glead_other).astype(F32)).astype(BF16)
    lead_parts = lax.all_to_all(lead_sum.reshape(chips, shard_rows, 10 * HD), "batch", 0, 0)
    input_grad, terms = input_gradient(tokens, gp, per_seq(gmid), wpairs, norms, gnorm_two)
    lead_shard, rest_shard, message = small_call(
        sum_kernel,
        "sum_parts",
        [shape(lead.shape[1:], F32), shape(rest.shape[1:], F32), shape(terms.shape, F32)],
        lead_parts,
        rest_parts,
        terms,
    )
    message = message + swap(message)
    stride = 1
    while stride < chips:
        message = message + lax.ppermute(message, "batch", [(i, i ^ stride) for i in range(chips)])
        stride *= 2
    place = (lax.axis_index("batch") * 2 + side) * norm_part
    mine = lax.dynamic_slice_in_dim(message[:4].reshape(1, 4 * width), place, norm_part, axis=1)
    like = lambda a: shape(a.shape, F32)
    moments = (
        qkv_moments.transpose(0, 2, 1, 3),
        out_moments.transpose(0, 2, 1),
        up_moments,
        down_moments.transpose(0, 2, 1),
        norm_moments,
    )
    results = small_call(
        update_kernel,
        "update_weights",
        [shape((1, 1), F32)] + [like(a) for a in masters + moments] + [like(mine)],
        message,
        mine,
        lead_shard,
        rest_shard,
        *masters,
        *moments,
    )
    grad_norm, qkv_next, out_next, up_next, down_next, norm_next = results[:6]
    qkv_states, out_states, up_states, down_states, norm_states, norm_grads = results[6:]
    return (
        per_seq(block_out),
        input_grad,
        grad_norm.reshape(()),
        qkv_next.transpose(1, 0, 2),
        out_next.T,
        up_next,
        down_next.T,
        norm_next[0],
        qkv_states.transpose(0, 2, 1, 3),
        out_states.transpose(0, 2, 1),
        up_states,
        down_states.transpose(0, 2, 1),
        norm_states,
        norm_grads[0],
    )


def solution(mesh):
    chips = mesh.shape["batch"]
    return jax.shard_map(
        functools.partial(per_device, chips),
        mesh=mesh,
        in_specs=(
            P(("batch", "head"), None, None),
            P(("batch", "head"), None, None),
            P("batch"),
            P("batch", None),
            P("batch", None, "head"),
            P("head", "batch"),
            P("batch", "head"),
            P("head", "batch"),
            P(("batch", "head")),
            P(None, "batch", None, "head"),
            P(None, "head", "batch"),
            P(None, "batch", "head"),
            P(None, "head", "batch"),
            P(None, ("batch", "head")),
        ),
        out_specs=(
            P(("batch", "head"), None, None),
            P(("batch", "head"), None, None),
            P(),
            P("batch", None, "head"),
            P("head", "batch"),
            P("batch", "head"),
            P("head", "batch"),
            P(("batch", "head")),
            P(None, "batch", None, "head"),
            P(None, "head", "batch"),
            P(None, "batch", "head"),
            P(None, "head", "batch"),
            P(None, ("batch", "head")),
            P(("batch", "head")),
        ),
        check_vma=False,
    )
```

```python
import functools

import jax
import jax.numpy as jnp
from jax import lax
from jax.experimental import pallas as pl
from jax.experimental.pallas import tpu as pltpu
from jax.sharding import PartitionSpec as P

HD = 64
STEP = 10
NORM_EPS = 1e-06
CLIP_NORM = 1000.0
BETA_ONE = 0.5
BETA_TWO = 0.5
ADAM_EPS = 1e-08
RATE_LIST = (0.06, 0.25, 0.06, 0.03, 0.5)
DECAY_LIST = (0.04, 0.04, 0.04, 0.04, 0.0)

F32 = jnp.float32
BF16 = jnp.bfloat16
NN = (((1,), (0,)), ((), ()))
NT = (((1,), (1,)), ((), ()))
TN = (((0,), (0,)), ((), ()))
QB = 128
FB = 512
FC = 256
PAIR = 2 * HD
VMEM = pltpu.CompilerParams(vmem_limit_bytes=56 * 2**20)


def cost(microseconds):
    return pl.CostEstimate(flops=microseconds * 1_000_000_000, bytes_accessed=1_000_000, transcendentals=0)


def mm(left, right, dims=NN):
    return lax.dot_general(left, right, dims, preferred_element_type=F32)


def normalize(values):
    centred = values - jnp.mean(values, axis=-1, keepdims=True)
    variance = jnp.mean(centred * centred, axis=-1, keepdims=True)
    rs = lax.rsqrt(variance + NORM_EPS)
    return centred * rs, rs


def norm_backward(normal, rs, gained):
    inner = jnp.mean(gained * normal, axis=-1, keepdims=True)
    return rs * (gained - jnp.mean(gained, axis=-1, keepdims=True) - normal * inner)


def gelu_parts(h):
    gauss = jnp.exp(h * h * -0.5)
    t = 1.0 / (1.0 + (0.3275911 * 0.7071067811865476) * jnp.abs(h))
    poly = t * (
        0.127414796
        + t * (-0.142248368 + t * (0.7107068705 + t * (-0.7265760135 + t * 0.5307027145)))
    )
    tail = poly * gauss
    return jnp.where(h < 0.0, tail, 1.0 - tail), gauss


def split_pairs(own, other, per_pair):
    wide, narrow = 2 * per_pair, per_pair
    singles = []
    for part in range(per_pair // HD):
        cols = slice(wide + part * HD, wide + (part + 1) * HD)
        singles += [own[:, cols], other[:, cols]]
    return own[:, :wide], jnp.concatenate(singles, axis=1), other[:, :wide]


def join_pairs(first, second, third, per_pair):
    parts = [
        [second[:, p * PAIR + side * HD : p * PAIR + (side + 1) * HD] for p in range(per_pair // HD)]
        for side in range(2)
    ]
    return [first] + parts[0], [third] + parts[1]


def forward_kernel(
    tok_ref, bias_ref, own_ref, other_ref, norms_ref, n1t_ref, qkv_ref, att_ref, p_ref, w_ref
):
    rows, width = tok_ref.shape

    @pl.when(pl.program_id(0) == 0)
    def _():
        cols = 9 * HD
        for i, part in enumerate(split_pairs(own_ref[:, :cols], other_ref[:, :cols], 3 * HD)):
            w_ref[i] = part

    x = tok_ref[...].astype(F32)
    normal, _ = normalize(x)
    n1 = (normal * norms_ref[0:1, :] + norms_ref[1:2, :]).astype(BF16)
    n1t_ref[...] = n1.T
    bias = bias_ref[...]
    lane = lax.broadcasted_iota(jnp.int32, (QB, PAIR), 1)
    for pair in range(width // PAIR):
        part = mm(n1, w_ref[pair])
        qkv_ref[pair, :, :PAIR] = (part[:, :PAIR].astype(BF16).astype(F32) * (HD**-0.5)).astype(BF16)
        qkv_ref[pair, :, PAIR:] = part[:, PAIR:].astype(BF16)
        kp = qkv_ref[pair, :, PAIR : 2 * PAIR]
        vp = qkv_ref[pair, :, 2 * PAIR :]
        for qb in range(rows // QB):
            sl = slice(qb * QB, (qb + 1) * QB)
            qp = qkv_ref[pair, sl, :PAIR]
            outs = []
            for half in range(2):
                qm = jnp.where((lane < HD) == (half == 0), qp, jnp.zeros_like(qp))
                s = mm(qm, kp, NT) + bias
                e = jnp.exp(s - jnp.max(s, axis=-1, keepdims=True))
                p = (e * (1.0 / jnp.sum(e, axis=-1, keepdims=True))).astype(BF16)
                p_ref[pair * 2 + half, sl, :] = p
                outs.append(mm(p, vp))
            att_ref[sl, pair * PAIR : (pair + 1) * PAIR] = jnp.where(
                lane < HD, outs[0], outs[1]
            ).astype(BF16)


def forward(tokens, bias, own, other, norms):
    seqs, rows, width = tokens.shape
    heads, pairs = width // HD, width // PAIR
    sq = pl.squeezed
    shape = jax.ShapeDtypeStruct
    whole = lambda *dims: pl.BlockSpec(dims, lambda s: (0,) * len(dims))
    return pl.pallas_call(
        forward_kernel,
        grid=(seqs,),
        in_specs=[
            pl.BlockSpec((sq, rows, width), lambda s: (s, 0, 0)),
            pl.BlockSpec((sq, 1, rows), lambda s: (s, 0, 0)),
            whole(*own.shape),
            whole(*other.shape),
            whole(4, width),
        ],
        out_specs=[
            pl.BlockSpec((sq, width, rows), lambda s: (s, 0, 0)),
            pl.BlockSpec((sq, pairs, rows, 3 * PAIR), lambda s: (s, 0, 0, 0)),
            pl.BlockSpec((sq, rows, width), lambda s: (s, 0, 0)),
            pl.BlockSpec((sq, heads, rows, rows), lambda s: (s, 0, 0, 0)),
            whole(pairs, width, 3 * PAIR),
        ],
        out_shape=[
            shape((seqs, width, rows), BF16),
            shape((seqs, pairs, rows, 3 * PAIR), BF16),
            shape((seqs, rows, width), BF16),
            shape((seqs, heads, rows, rows), BF16),
            shape((pairs, width, 3 * PAIR), BF16),
        ],
        compiler_params=VMEM,
        cost_estimate=cost(50),
        name="attention_forward",
    )(tokens, bias, own, other, norms)


def middle_kernel(
    seq_rows, units, len_ref, tok_ref, cot_ref, att_ref, own_ref, other_ref, norms_ref,
    out_ref, gmid_ref, gatt_ref, gown_ref, gother_ref, gnorm_ref,
    wo_ref, gout_ref, gup_ref, gdown_ref,
):
    step = pl.program_id(0)
    rows, width = tok_ref.shape
    halves = (own_ref, other_ref)

    @pl.when(step == 0)
    def _():
        gout_ref[...] = jnp.zeros_like(gout_ref)
        gup_ref[...] = jnp.zeros_like(gup_ref)
        gdown_ref[...] = jnp.zeros_like(gdown_ref)
        gnorm_ref[...] = jnp.zeros_like(gnorm_ref)
        cols = slice(2 * units, 2 * units + 3 * HD)
        parts = split_pairs(own_ref[:, cols], other_ref[:, cols], HD)
        for i, part in enumerate(parts):
            wo_ref[:, i * PAIR : (i + 1) * PAIR] = part

    first = step * rows
    row = first + lax.broadcasted_iota(jnp.int32, (rows, 1), 0)
    live = row < 0
    last = len_ref.shape[0] - 1
    for near in range(-(-rows // seq_rows) + 1):
        s = first // seq_rows + near
        bound = jnp.where(s <= last, len_ref[jnp.minimum(s, last)], 0)
        live = live | ((row >= s * seq_rows) & (row < s * seq_rows + bound))

    x = tok_ref[...].astype(F32)
    att = att_ref[...]
    mid = x + mm(att, wo_ref[...], NT)
    normal, rs = normalize(mid)
    gain, shift = norms_ref[2:3, :], norms_ref[3:4, :]
    n2 = (normal * gain + shift).astype(BF16)
    n2t = n2.T
    up = jnp.where(live, cot_ref[...].astype(F32), 0.0)
    gb = up.astype(BF16)
    gbt = gb.T
    bo = mid
    gtwo = jnp.zeros_like(mid)
    for half in range(2):
        for c in range(units // FC):
            cols = slice(c * FC, (c + 1) * FC)
            wu = halves[half][:, c * FC : (c + 1) * FC]
            wd = halves[half][:, units + c * FC : units + (c + 1) * FC]
            h = mm(n2, wu)
            ga = mm(gb, wd)
            cdf, gauss = gelu_parts(h)
            act = (h * cdf).astype(BF16)
            gh = (ga * (cdf + h * (gauss * 0.3989422804014327))).astype(BF16)
            bo = bo + mm(act, wd, NT)
            gtwo = gtwo + mm(gh, wu, NT)
            gup_ref[half, :, cols] += mm(n2t, gh)
            gdown_ref[half, :, cols] += mm(gbt, act)
    out_ref[...] = bo.astype(BF16)
    gnorm_ref[0:8, :] += jnp.sum((gtwo * normal).reshape(rows // 8, 8, width), axis=0)
    gnorm_ref[8:16, :] += jnp.sum(gtwo.reshape(rows // 8, 8, width), axis=0)
    gmid = up + norm_backward(normal, rs, gtwo * gain)
    gmid_ref[...] = gmid
    gm = gmid.astype(BF16)
    gout_ref[...] += mm(gm, att, TN)
    gatt_ref[...] = mm(gm, wo_ref[...]).astype(BF16)

    @pl.when(step == pl.num_programs(0) - 1)
    def _():
        total = gout_ref[...]
        sides = join_pairs(
            total[:, :PAIR], total[:, PAIR : 2 * PAIR], total[:, 2 * PAIR :], HD
        )
        for half, ref in enumerate((gown_ref, gother_ref)):
            ref[:, :units] = gup_ref[half].astype(BF16)
            ref[:, units : 2 * units] = gdown_ref[half].astype(BF16)
            blank = jnp.zeros((total.shape[0], HD), F32)
            ref[:, 2 * units :] = jnp.concatenate(sides[half] + [blank], axis=1).astype(BF16)


def middle(lengths, tokens, cotangent, attended, own, other, norms):
    seqs, seq_rows, width = tokens.shape
    total = seqs * seq_rows
    packed = own.shape[1]
    units = (packed - 4 * HD) // 2
    flat = lambda a: a.reshape(total, width)
    rowspec = pl.BlockSpec((FB, width), lambda s: (s, 0))
    whole = lambda *dims: pl.BlockSpec(dims, lambda s: (0,) * len(dims))
    shape = jax.ShapeDtypeStruct
    return pl.pallas_call(
        functools.partial(middle_kernel, seq_rows, units),
        grid=(total // FB,),
        in_specs=[
            pl.BlockSpec(memory_space=pltpu.SMEM),
            rowspec,
            rowspec,
            rowspec,
            whole(*own.shape),
            whole(*other.shape),
            whole(4, width),
        ],
        out_specs=[rowspec] * 3 + [whole(*own.shape), whole(*own.shape), whole(16, width)],
        out_shape=[
            shape((total, width), BF16),
            shape((total, width), F32),
            shape((total, width), BF16),
            shape(own.shape, BF16),
            shape(own.shape, BF16),
            shape((16, width), F32),
        ],
        scratch_shapes=[
            pltpu.VMEM((width, width), BF16),
            pltpu.VMEM((width, width), F32),
            pltpu.VMEM((2, width, units), F32),
            pltpu.VMEM((2, width, units), F32),
        ],
        compiler_params=VMEM,
        cost_estimate=cost(50),
        name="feed_forward",
    )(lengths, flat(tokens), flat(cotangent), flat(attended), own, other, norms)


def backward_kernel(
    n1t_ref, qkv_ref, p_ref, gatt_ref, att_ref, gp_ref, gown_ref, gother_ref, gqkv_ref
):
    seq, pair = pl.program_id(0), pl.program_id(1)
    rows = qkv_ref.shape[0]
    qp, kp, vp = qkv_ref[:, :PAIR], qkv_ref[:, PAIR : 2 * PAIR], qkv_ref[:, 2 * PAIR :]
    ga = gatt_ref[...]
    prod = ga.astype(F32) * att_ref[...].astype(F32)
    lane = lax.broadcasted_iota(jnp.int32, (QB, PAIR), 1)
    gat, qt = ga.T, qp.T
    zero = jnp.zeros((QB, PAIR), BF16)
    gq = [[], []]
    gkt, gvt = [], []
    for half in range(2):
        ds_all = []
        mask = (lane < HD) == (half == 0)
        for qb in range(rows // QB):
            sl = slice(qb * QB, (qb + 1) * QB)
            dp = mm(jnp.where(mask, ga[sl], zero), vp, NT)
            inner = jnp.sum(jnp.where(mask, prod[sl], 0.0), axis=-1, keepdims=True)
            ds = (p_ref[half, sl, :].astype(F32) * (dp - inner)).astype(BF16)
            ds_all.append(ds)
            gq[half].append(mm(ds, kp))
        ds = jnp.concatenate(ds_all, axis=0)
        hs = slice(half * HD, half * HD + HD)
        gkt.append(mm(qt[hs], ds))
        gvt.append(mm(gat[hs], p_ref[half]))
    for qb in range(rows // QB):
        sl = slice(qb * QB, (qb + 1) * QB)
        joined = jnp.where(lane < HD, gq[0][qb], gq[1][qb])
        gp_ref[sl, :PAIR] = (joined * (HD**-0.5)).astype(BF16)
    gp_ref[:, PAIR : 2 * PAIR] = jnp.concatenate(gkt, axis=0).astype(BF16).T
    gp_ref[:, 2 * PAIR :] = jnp.concatenate(gvt, axis=0).astype(BF16).T
    new = mm(n1t_ref[...], gp_ref[...])

    @pl.when(seq == 0)
    def _():
        gqkv_ref[pair] = new

    @pl.when(seq > 0)
    def _():
        gqkv_ref[pair] += new

    @pl.when((seq == pl.num_programs(0) - 1) & (pair == pl.num_programs(1) - 1))
    def _():
        sides = join_pairs(gqkv_ref[0], gqkv_ref[1], gqkv_ref[2], 3 * HD)
        blank = jnp.zeros((gqkv_ref.shape[1], HD), F32)
        for columns, ref in zip(sides, (gown_ref, gother_ref)):
            ref[...] = jnp.concatenate(columns + [blank], axis=1).astype(BF16)


def backward(n1t, qkv, probs, gatt, attended):
    seqs, rows, width = attended.shape
    pairs = width // PAIR
    sq = pl.squeezed
    pairspec = pl.BlockSpec((sq, rows, PAIR), lambda s, p: (s, 0, p))
    groupspec = pl.BlockSpec((sq, sq, rows, 3 * PAIR), lambda s, p: (s, p, 0, 0))
    whole = lambda *dims: pl.BlockSpec(dims, lambda s, p: (0,) * len(dims))
    shape = jax.ShapeDtypeStruct
    packed = (width, 10 * HD)
    return pl.pallas_call(
        backward_kernel,
        grid=(seqs, pairs),
        in_specs=[
            pl.BlockSpec((sq, width, rows), lambda s, p: (s, 0, 0)),
            groupspec,
            pl.BlockSpec((sq, 2, rows, rows), lambda s, p: (s, p, 0, 0)),
            pairspec,
            pairspec,
        ],
        out_specs=[groupspec, whole(*packed), whole(*packed)],
        out_shape=[shape(qkv.shape, BF16), shape(packed, BF16), shape(packed, BF16)],
        scratch_shapes=[pltpu.VMEM((pairs, width, 3 * PAIR), F32)],
        compiler_params=VMEM,
        cost_estimate=cost(50),
        name="attention_backward",
    )(n1t, qkv, probs, gatt, attended)


def input_kernel(tok_ref, gp_ref, gmid_ref, w_ref, norms_ref, two_ref, gin_ref, terms_ref):
    rows, width = tok_ref.shape
    gone = mm(gp_ref[0], w_ref[0], NT)
    for pair in range(1, w_ref.shape[0]):
        gone = gone + mm(gp_ref[pair], w_ref[pair], NT)
    normal, rs = normalize(tok_ref[...].astype(F32))

    @pl.when(pl.program_id(0) == 0)
    def _():
        terms_ref[...] = jnp.zeros_like(terms_ref)
        terms_ref[2:3, :] = jnp.sum(two_ref[0:8, :], axis=0, keepdims=True)
        terms_ref[3:4, :] = jnp.sum(two_ref[8:16, :], axis=0, keepdims=True)

    terms_ref[0:1, :] += jnp.sum(gone * normal, axis=0, keepdims=True)
    terms_ref[1:2, :] += jnp.sum(gone, axis=0, keepdims=True)
    gin_ref[...] = gmid_ref[...] + norm_backward(normal, rs, gone * norms_ref[0:1, :])


def input_gradient(tokens, gp, gmid, wpairs, norms, gnorm_two):
    seqs, rows, width = tokens.shape
    pairs = width // PAIR
    sq = pl.squeezed
    full = pl.BlockSpec((sq, rows, width), lambda s: (s, 0, 0))
    whole = lambda *dims: pl.BlockSpec(dims, lambda s: (0,) * len(dims))
    shape = jax.ShapeDtypeStruct
    return pl.pallas_call(
        input_kernel,
        grid=(seqs,),
        in_specs=[
            full,
            pl.BlockSpec((sq, pairs, rows, 3 * PAIR), lambda s: (s, 0, 0, 0)),
            full,
            whole(pairs, width, 3 * PAIR),
            whole(4, width),
            whole(16, width),
        ],
        out_specs=[full, whole(8, width)],
        out_shape=[shape((seqs, rows, width), F32), shape((8, width), F32)],
        compiler_params=VMEM,
        cost_estimate=cost(12),
        name="input_gradient",
    )(tokens, gp, gmid, wpairs, norms, gnorm_two)


def pack_kernel(qkv_ref, out_ref, up_ref, down_ref, norm_ref, lead_ref, rest_ref):
    chips, rows, _ = lead_ref.shape
    part = norm_ref.shape[1]
    norm = norm_ref[...]
    high = norm.astype(BF16).astype(F32)
    row = lax.broadcasted_iota(jnp.int32, (rows, part), 0)
    extra = jnp.where(row == 0, high, jnp.where(row == 1, norm - high, 0.0))
    columns = [qkv_ref[c, :, :PAIR] for c in range(3)] + [qkv_ref[c, :, PAIR:] for c in range(3)]
    blank = jnp.zeros((rows, HD - part), F32)
    lead_ref[...] = jnp.broadcast_to(
        jnp.concatenate(columns + [extra, blank], axis=1).astype(BF16)[None], lead_ref.shape
    )
    blank = jnp.zeros((rows, HD), F32)
    rest_ref[...] = jnp.broadcast_to(
        jnp.concatenate([up_ref[...], down_ref[...], out_ref[...], blank], axis=1).astype(BF16)[None], rest_ref.shape
    )


def sum_kernel(lead_parts_ref, rest_parts_ref, terms_ref, lead_ref, rest_ref, message_ref):
    total = jnp.zeros((lead_ref.shape[0], PAIR), F32)
    for parts_ref, ref in ((lead_parts_ref, lead_ref), (rest_parts_ref, rest_ref)):
        for start in range(0, ref.shape[1], PAIR):
            cols = slice(start, start + PAIR)
            piece = jnp.sum(parts_ref[:, :, cols].astype(F32), axis=0)
            ref[:, cols] = piece
            total = total + piece * piece
    message_ref[...] = terms_ref[...]
    message_ref[4:5, :PAIR] = jnp.sum(total, axis=0, keepdims=True)


def adamw(master, gradient, moments, rate, decay):
    moment = BETA_ONE * moments[0] + (1.0 - BETA_ONE) * gradient
    second = BETA_TWO * moments[1] + (1.0 - BETA_TWO) * gradient * gradient
    step_size = (
        moment / (1.0 - BETA_ONE**STEP) / (jnp.sqrt(second / (1.0 - BETA_TWO**STEP)) + ADAM_EPS)
    )
    return master - rate * (step_size + decay * master), moment, second


def update_kernel(
    message_ref, mine_ref, lead_ref, rest_ref,
    qkv_ref, out_ref, up_ref, down_ref, norm_ref,
    qkv_m_ref, out_m_ref, up_m_ref, down_m_ref, norm_m_ref,
    gn_ref, qkv_n_ref, out_n_ref, up_n_ref, down_n_ref, norm_n_ref,
    qkv_s_ref, out_s_ref, up_s_ref, down_s_ref, norm_s_ref, grads_ref,
):
    units = up_ref.shape[1]
    terms = message_ref[0:4, :]
    squares = jnp.sum(terms * terms, axis=(0, 1), keepdims=True) + jnp.sum(
        message_ref[4:5, :], axis=(0, 1), keepdims=True
    )
    grad_norm = jnp.sqrt(squares)
    gn_ref[...] = grad_norm
    factor = jnp.minimum(1.0, CLIP_NORM / (grad_norm + 1e-06))
    for c in range(3):
        wide = lead_ref[:, c * PAIR : (c + 1) * PAIR]
        narrow = lead_ref[:, 3 * PAIR + c * HD : 3 * PAIR + (c + 1) * HD]
        for cols, grad in ((slice(0, PAIR), wide), (slice(PAIR, PAIR + HD), narrow)):
            new, moment, second = adamw(
                qkv_ref[c, :, cols], factor * grad, qkv_m_ref[:, c, :, cols], RATE_LIST[0], DECAY_LIST[0]
            )
            qkv_n_ref[c, :, cols] = new
            qkv_s_ref[0, c, :, cols] = moment
            qkv_s_ref[1, c, :, cols] = second
    norm_grads = factor * mine_ref[...]
    grads_ref[...] = norm_grads
    plain = (
        (out_ref, rest_ref[:, 2 * units : 2 * units + 3 * HD], out_m_ref, out_n_ref, out_s_ref, 1),
        (up_ref, rest_ref[:, :units], up_m_ref, up_n_ref, up_s_ref, 2),
        (down_ref, rest_ref[:, units : 2 * units], down_m_ref, down_n_ref, down_s_ref, 3),
    )
    for master, grad, moments, next_ref, state_ref, i in plain:
        next_ref[...], state_ref[0], state_ref[1] = adamw(
            master[...], factor * grad, moments[...], RATE_LIST[i], DECAY_LIST[i]
        )
    norm_n_ref[...], norm_s_ref[0:1, :], norm_s_ref[1:2, :] = adamw(
        norm_ref[...], norm_grads, (norm_m_ref[0:1, :], norm_m_ref[1:2, :]), RATE_LIST[4], DECAY_LIST[4]
    )


def small_call(kernel, name, out_shape, *operands):
    return pl.pallas_call(kernel, out_shape=out_shape, compiler_params=VMEM, cost_estimate=cost(3), name=name)(
        *operands
    )


def swap(values):
    return lax.ppermute(values, "head", [(0, 1), (1, 0)])


def per_device(
    chips,
    tokens,
    cotangent,
    lengths,
    key_masks,
    qkv_master,
    out_master,
    up_master,
    down_master,
    norm_master,
    qkv_moments,
    out_moments,
    up_moments,
    down_moments,
    norm_moments,
):
    seqs, slot_rows, width = tokens.shape
    shard_rows = qkv_master.shape[0]
    norm_part = norm_master.shape[0]
    units = up_master.shape[1]
    side = lax.axis_index("head")
    own_first = side == 0

    qkv_rows = qkv_master.transpose(1, 0, 2)
    masters = (qkv_rows, out_master.T, up_master, down_master.T, norm_master[None])
    shape = jax.ShapeDtypeStruct
    lead, rest = small_call(
        pack_kernel,
        "pack_weights",
        [shape((chips, shard_rows, 10 * HD), BF16), shape((chips, shard_rows, 2 * units + 4 * HD), BF16)],
        *masters,
    )
    lead_own = lax.all_to_all(lead, "batch", 0, 0)
    lead_own, rest = lax.optimization_barrier((lead_own, rest))
    rest_own = lax.all_to_all(rest, "batch", 0, 0)
    lead_other = swap(lead_own)

    def norms_of(gathered):
        parts = gathered[:, :2, 9 * HD : 9 * HD + norm_part].astype(F32)
        return parts[:, 0] + parts[:, 1]

    norms_own, norms_other = norms_of(lead_own), norms_of(lead_other)
    norms = jnp.stack(
        [jnp.where(own_first, norms_own, norms_other), jnp.where(own_first, norms_other, norms_own)], axis=1
    ).reshape(4, width)

    positions = jnp.arange(slot_rows, dtype=jnp.int32)
    own_lengths = lax.dynamic_slice_in_dim(lengths, side * seqs, seqs)
    own_masks = lax.dynamic_slice_in_dim(key_masks, side * seqs, seqs)
    visible = (positions[None, :] < own_lengths[:, None]) & ((own_masks == 1) | (positions[None, :] == 0))
    bias = jnp.where(visible, 0.0, -1e30).astype(F32)[:, None, :]

    flat = lambda a: a.reshape(chips * shard_rows, a.shape[-1])
    n1t, qkv, attended, probs, wpairs = forward(tokens, bias, flat(lead_own), flat(lead_other), norms)
    rest_own, attended = lax.optimization_barrier((rest_own, attended))
    rest_other = swap(rest_own)
    block_out, gmid, gatt, grest_own, grest_other, gnorm_two = middle(
        own_lengths, tokens, cotangent, attended, flat(rest_own), flat(rest_other), norms
    )
    per_seq = lambda a: a.reshape(seqs, slot_rows, width)
    rest_sum = (grest_own.astype(F32) + swap(grest_other).astype(F32)).astype(BF16)
    rest_sum, gatt = lax.optimization_barrier((rest_sum, gatt))
    rest_parts = lax.all_to_all(rest_sum.reshape(rest.shape), "batch", 0, 0)
    gp, glead_own, glead_other = backward(n1t, qkv, probs, per_seq(gatt), attended)
    lead_sum = (glead_own.astype(F32) + swap(glead_other).astype(F32)).astype(BF16)
    lead_sum, rest_parts = lax.optimization_barrier((lead_sum, rest_parts))
    lead_parts = lax.all_to_all(lead_sum.reshape(chips, shard_rows, 10 * HD), "batch", 0, 0)
    input_grad, terms = input_gradient(tokens, gp, per_seq(gmid), wpairs, norms, gnorm_two)
    lead_shard, rest_shard, message = small_call(
        sum_kernel,
        "sum_parts",
        [shape(lead.shape[1:], F32), shape(rest.shape[1:], F32), shape(terms.shape, F32)],
        lead_parts,
        rest_parts,
        terms,
    )
    message = message + swap(message)
    stride = 1
    while stride < chips:
        message = message + lax.ppermute(message, "batch", [(i, i ^ stride) for i in range(chips)])
        stride *= 2
    place = (lax.axis_index("batch") * 2 + side) * norm_part
    mine = lax.dynamic_slice_in_dim(message[:4].reshape(1, 4 * width), place, norm_part, axis=1)
    like = lambda a: shape(a.shape, F32)
    moments = (
        qkv_moments.transpose(0, 2, 1, 3),
        out_moments.transpose(0, 2, 1),
        up_moments,
        down_moments.transpose(0, 2, 1),
        norm_moments,
    )
    results = small_call(
        update_kernel,
        "update_weights",
        [shape((1, 1), F32)] + [like(a) for a in masters + moments] + [like(mine)],
        message,
        mine,
        lead_shard,
        rest_shard,
        *masters,
        *moments,
    )
    grad_norm, qkv_next, out_next, up_next, down_next, norm_next = results[:6]
    qkv_states, out_states, up_states, down_states, norm_states, norm_grads = results[6:]
    return (
        per_seq(block_out),
        input_grad,
        grad_norm.reshape(()),
        qkv_next.transpose(1, 0, 2),
        out_next.T,
        up_next,
        down_next.T,
        norm_next[0],
        qkv_states.transpose(0, 2, 1, 3),
        out_states.transpose(0, 2, 1),
        up_states,
        down_states.transpose(0, 2, 1),
        norm_states,
        norm_grads[0],
    )


def solution(mesh):
    chips = mesh.shape["batch"]
    return jax.shard_map(
        functools.partial(per_device, chips),
        mesh=mesh,
        in_specs=(
            P(("batch", "head"), None, None),
            P(("batch", "head"), None, None),
            P("batch"),
            P("batch", None),
            P("batch", None, "head"),
            P("head", "batch"),
            P("batch", "head"),
            P("head", "batch"),
            P(("batch", "head")),
            P(None, "batch", None, "head"),
            P(None, "head", "batch"),
            P(None, "batch", "head"),
            P(None, "head", "batch"),
            P(None, ("batch", "head")),
        ),
        out_specs=(
            P(("batch", "head"), None, None),
            P(("batch", "head"), None, None),
            P(),
            P("batch", None, "head"),
            P("head", "batch"),
            P("batch", "head"),
            P("head", "batch"),
            P(("batch", "head")),
            P(None, "batch", None, "head"),
            P(None, "head", "batch"),
            P(None, "batch", "head"),
            P(None, "head", "batch"),
            P(None, ("batch", "head")),
            P(("batch", "head")),
        ),
        check_vma=False,
    )
```

```python
import functools

import jax
import jax.numpy as jnp
from jax import lax
from jax.experimental import pallas as pl
from jax.experimental.pallas import tpu as pltpu
from jax.sharding import PartitionSpec as P

HD = 64
STEP = 10
NORM_EPS = 1e-06
CLIP_NORM = 1000.0
BETA_ONE = 0.5
BETA_TWO = 0.5
ADAM_EPS = 1e-08
RATE_LIST = (0.06, 0.25, 0.06, 0.03, 0.5)
DECAY_LIST = (0.04, 0.04, 0.04, 0.04, 0.0)

F32 = jnp.float32
BF16 = jnp.bfloat16
NN = (((1,), (0,)), ((), ()))
NT = (((1,), (1,)), ((), ()))
TN = (((0,), (0,)), ((), ()))
QB = 320
FB = 512
FC = 256
PAIR = 2 * HD
VMEM = pltpu.CompilerParams(vmem_limit_bytes=60 * 2**20)


def cost(microseconds):
    return pl.CostEstimate(flops=microseconds * 1_000_000_000, bytes_accessed=1_000_000, transcendentals=0)


def mm(left, right, dims=NN):
    return lax.dot_general(left, right, dims, preferred_element_type=F32)


def normalize(values):
    centred = values - jnp.mean(values, axis=-1, keepdims=True)
    variance = jnp.mean(centred * centred, axis=-1, keepdims=True)
    rs = lax.rsqrt(variance + NORM_EPS)
    return centred * rs, rs


def norm_backward(normal, rs, gained):
    inner = jnp.mean(gained * normal, axis=-1, keepdims=True)
    return rs * (gained - jnp.mean(gained, axis=-1, keepdims=True) - normal * inner)


def gelu_both(h, gradient):
    cdf = 0.5 + 0.5 * lax.erf(h * 0.7071067811865476)
    density = jnp.exp(h * h * -0.5) * 0.3989422804014327
    return (h * cdf).astype(BF16), (gradient * (cdf + h * density)).astype(BF16)


def split_pairs(own, other, per_pair):
    wide, narrow = 2 * per_pair, per_pair
    singles = []
    for part in range(per_pair // HD):
        cols = slice(wide + part * HD, wide + (part + 1) * HD)
        singles += [own[:, cols], other[:, cols]]
    return own[:, :wide], jnp.concatenate(singles, axis=1), other[:, :wide]


def join_pairs(first, second, third, per_pair):
    parts = [
        [second[:, p * PAIR + side * HD : p * PAIR + (side + 1) * HD] for p in range(per_pair // HD)]
        for side in range(2)
    ]
    return [first] + parts[0], [third] + parts[1]


def gathered_norms(first, second, chips, part, width):
    shard_rows = first.shape[0] // chips
    cols = slice(9 * HD, 9 * HD + part)
    pieces = []
    for chip in range(chips):
        row = chip * shard_rows
        for values in (first, second):
            pieces.append(values[row : row + 1, cols] + values[row + 1 : row + 2, cols])
    per_row = width // part
    return [jnp.concatenate(pieces[i * per_row : (i + 1) * per_row], axis=1) for i in range(4)]


def forward_kernel(
    chips, part, side_ref, len_ref, tok_ref, mask_ref, own_ref, other_ref,
    n1t_ref, qkv_ref, att_ref, linv_ref, p_ref, w_ref, norms_ref,
):
    rows, width = tok_ref.shape
    pairs = width // PAIR
    side, seq = side_ref[0], pl.program_id(0)

    @pl.when(seq == 0)
    def _():
        own, other = own_ref[...], other_ref[...]
        for i, weights in enumerate(split_pairs(own[:, : 9 * HD], other[:, : 9 * HD], 3 * HD)):
            w_ref[i] = weights
        tail = slice(8 * HD, 10 * HD)
        mine, theirs = own[:, tail].astype(F32), other[:, tail].astype(F32)
        pad = jnp.zeros((own.shape[0], 8 * HD), F32)
        first = jnp.concatenate([pad, jnp.where(side == 0, mine, theirs)], axis=1)
        second = jnp.concatenate([pad, jnp.where(side == 0, theirs, mine)], axis=1)
        for i, row in enumerate(gathered_norms(first, second, chips, part, width)):
            norms_ref[i : i + 1, :] = row

    member = side * pl.num_programs(0) + seq
    position = lax.broadcasted_iota(jnp.int32, (1, rows), 1)
    mask = mask_ref[pl.ds(member, 1), :]
    visible = (position < len_ref[member]) & ((mask == 1) | (position == 0))
    hidden = jnp.where(visible, 0.0, -1e30)
    hidden = jnp.broadcast_to(hidden, (PAIR, rows)).T.astype(BF16)

    normal, _ = normalize(tok_ref[...].astype(F32))
    n1 = (normal * norms_ref[0:1, :] + norms_ref[1:2, :]).astype(BF16)
    n1t_ref[...] = n1.T
    lane = lax.broadcasted_iota(jnp.int32, (QB, PAIR), 1)
    key_lane = lax.broadcasted_iota(jnp.int32, (rows, PAIR), 1)
    ones = jnp.ones((rows, PAIR), BF16)
    ready = {}

    def project(pair):
        out = mm(n1, w_ref[pair])
        queries = (out[:, :PAIR].astype(BF16).astype(F32) * (HD**-0.5)).astype(BF16)
        others = out[:, PAIR:].astype(BF16)
        qkv_ref[pair, :, :PAIR] = queries
        qkv_ref[pair, :, PAIR:] = others
        keys = [jnp.where(key_lane == HD * (1 - half), hidden, others[:, :PAIR]) for half in range(2)]
        return queries, keys, jnp.concatenate([others[:, PAIR:], ones], axis=1)

    def scores(pair, block, half):
        if pair not in ready:
            ready[pair] = project(pair)
        queries, keys, _ = ready[pair]
        spot = jnp.where(lane == HD * (1 - half), 1.0, 0.0).astype(BF16)
        part_queries = jnp.where((lane < HD) == (half == 0), queries[block * QB : (block + 1) * QB], spot)
        return mm(part_queries, keys[half], NT)

    outs = {}

    def finish(pair, block, half, s):
        sl = slice(block * QB, (block + 1) * QB)
        p = jnp.exp(s - jnp.max(s, axis=-1, keepdims=True)).astype(BF16)
        p_ref[pair * 2 + half, sl, :] = p
        out = mm(p, ready[pair][2])
        inverse = 1.0 / out[:, PAIR:]
        outs[half] = (out[:, :PAIR] * inverse, inverse)
        if half == 1:
            cols = slice(pair * PAIR, (pair + 1) * PAIR)
            att_ref[sl, cols] = jnp.where(lane < HD, outs[0][0], outs[1][0]).astype(BF16)
            linv_ref[sl, cols] = jnp.where(lane < HD, outs[0][1], outs[1][1])

    pending = None
    for pair in range(pairs):
        for block in range(rows // QB):
            for half in range(2):
                fresh = (pair, block, half, scores(pair, block, half))
                if pending is not None:
                    finish(*pending)
                pending = fresh
    finish(*pending)


def forward(chips, part, side, lengths, tokens, key_masks, own, other):
    seqs, rows, width = tokens.shape
    heads, pairs = width // HD, width // PAIR
    sq = pl.squeezed
    shape = jax.ShapeDtypeStruct
    whole = lambda *dims: pl.BlockSpec(dims, lambda s: (0,) * len(dims))
    row_spec = pl.BlockSpec((sq, rows, width), lambda s: (s, 0, 0))
    scalars = pl.BlockSpec(memory_space=pltpu.SMEM)
    return pl.pallas_call(
        functools.partial(forward_kernel, chips, part),
        grid=(seqs,),
        in_specs=[scalars, scalars, row_spec, whole(*key_masks.shape), whole(*own.shape), whole(*other.shape)],
        out_specs=[
            pl.BlockSpec((sq, width, rows), lambda s: (s, 0, 0)),
            pl.BlockSpec((sq, pairs, rows, 3 * PAIR), lambda s: (s, 0, 0, 0)),
            row_spec,
            row_spec,
            pl.BlockSpec((sq, heads, rows, rows), lambda s: (s, 0, 0, 0)),
            whole(pairs, width, 3 * PAIR),
            whole(4, width),
        ],
        out_shape=[
            shape((seqs, width, rows), BF16),
            shape((seqs, pairs, rows, 3 * PAIR), BF16),
            shape((seqs, rows, width), BF16),
            shape((seqs, rows, width), F32),
            shape((seqs, heads, rows, rows), BF16),
            shape((pairs, width, 3 * PAIR), BF16),
            shape((4, width), F32),
        ],
        compiler_params=VMEM,
        cost_estimate=cost(24),
        name="attention_forward",
    )(side, lengths, tokens, key_masks, own, other)


def middle_kernel(
    seq_rows, units, side_ref, len_ref, tok_ref, cot_ref, att_ref, linv_ref, own_ref, other_ref, norms_ref,
    out_ref, gmid_ref, gatt_ref, gown_ref, gother_ref, gnorm_ref,
    wo_ref, gout_ref, gup_ref, gdown_ref,
):
    step = pl.program_id(0)
    rows, width = tok_ref.shape
    halves = (own_ref, other_ref)

    @pl.when(step == 0)
    def _():
        gout_ref[...] = jnp.zeros_like(gout_ref)
        gup_ref[...] = jnp.zeros_like(gup_ref)
        gdown_ref[...] = jnp.zeros_like(gdown_ref)
        gnorm_ref[...] = jnp.zeros_like(gnorm_ref)
        cols = slice(2 * units, 2 * units + 3 * HD)
        parts = split_pairs(own_ref[:, cols], other_ref[:, cols], HD)
        for i, part in enumerate(parts):
            wo_ref[:, i * PAIR : (i + 1) * PAIR] = part

    first = step * rows
    row = first + lax.broadcasted_iota(jnp.int32, (rows, 1), 0)
    live = row < 0
    seqs = rows * pl.num_programs(0) // seq_rows
    for near in range(-(-rows // seq_rows) + 1):
        s = first // seq_rows + near
        bound = jnp.where(s < seqs, len_ref[side_ref[0] * seqs + jnp.minimum(s, seqs - 1)], 0)
        live = live | ((row >= s * seq_rows) & (row < s * seq_rows + bound))

    x = tok_ref[...].astype(F32)
    att = att_ref[...]
    mid = x + mm(att, wo_ref[...], NT)
    normal, rs = normalize(mid)
    gain, shift = norms_ref[2:3, :], norms_ref[3:4, :]
    n2 = (normal * gain + shift).astype(BF16)
    n2t = n2.T
    up = jnp.where(live, cot_ref[...].astype(F32), 0.0)
    gb = up.astype(BF16)
    gbt = gb.T
    sums = [mid, jnp.zeros_like(mid)]

    def begin(half, c):
        wu = halves[half][:, c * FC : (c + 1) * FC]
        wd = halves[half][:, units + c * FC : units + (c + 1) * FC]
        return half, c, wu, wd, mm(n2, wu), mm(gb, wd)

    def finish(half, c, wu, wd, h, ga):
        cols = slice(c * FC, (c + 1) * FC)
        act, gh = gelu_both(h, ga)
        sums[0] = sums[0] + mm(act, wd, NT)
        sums[1] = sums[1] + mm(gh, wu, NT)
        gup_ref[half, :, cols] += mm(n2t, gh)
        gdown_ref[half, :, cols] += mm(gbt, act)

    pending = None
    for half in range(2):
        for c in range(units // FC):
            fresh = begin(half, c)
            if pending is not None:
                finish(*pending)
            pending = fresh
    finish(*pending)
    bo, gtwo = sums
    out_ref[...] = bo.astype(BF16)
    gnorm_ref[0:8, :] += jnp.sum((gtwo * normal).reshape(rows // 8, 8, width), axis=0)
    gnorm_ref[8:16, :] += jnp.sum(gtwo.reshape(rows // 8, 8, width), axis=0)
    gmid = up + norm_backward(normal, rs, gtwo * gain)
    gmid_ref[...] = gmid
    gm = gmid.astype(BF16)
    gout_ref[...] += mm(gm, att, TN)
    gatt_ref[...] = (mm(gm, wo_ref[...]) * linv_ref[...]).astype(BF16)

    @pl.when(step == pl.num_programs(0) - 1)
    def _():
        total = gout_ref[...]
        sides = join_pairs(
            total[:, :PAIR], total[:, PAIR : 2 * PAIR], total[:, 2 * PAIR :], HD
        )
        for half, ref in enumerate((gown_ref, gother_ref)):
            ref[:, :units] = gup_ref[half].astype(BF16)
            ref[:, units : 2 * units] = gdown_ref[half].astype(BF16)
            blank = jnp.zeros((total.shape[0], HD), F32)
            ref[:, 2 * units :] = jnp.concatenate(sides[half] + [blank], axis=1).astype(BF16)


def middle(side, lengths, tokens, cotangent, attended, linv, own, other, norms):
    seqs, seq_rows, width = tokens.shape
    total = seqs * seq_rows
    packed = own.shape[1]
    units = (packed - 4 * HD) // 2
    flat = lambda a: a.reshape(total, width)
    rowspec = pl.BlockSpec((FB, width), lambda s: (s, 0))
    whole = lambda *dims: pl.BlockSpec(dims, lambda s: (0,) * len(dims))
    shape = jax.ShapeDtypeStruct
    return pl.pallas_call(
        functools.partial(middle_kernel, seq_rows, units),
        grid=(total // FB,),
        in_specs=[
            pl.BlockSpec(memory_space=pltpu.SMEM),
            pl.BlockSpec(memory_space=pltpu.SMEM),
            rowspec,
            rowspec,
            rowspec,
            rowspec,
            whole(*own.shape),
            whole(*other.shape),
            whole(4, width),
        ],
        out_specs=[rowspec] * 3 + [whole(*own.shape), whole(*own.shape), whole(16, width)],
        out_shape=[
            shape((total, width), BF16),
            shape((total, width), F32),
            shape((total, width), BF16),
            shape(own.shape, BF16),
            shape(own.shape, BF16),
            shape((16, width), F32),
        ],
        scratch_shapes=[
            pltpu.VMEM((width, width), BF16),
            pltpu.VMEM((width, width), F32),
            pltpu.VMEM((2, width, units), F32),
            pltpu.VMEM((2, width, units), F32),
        ],
        compiler_params=VMEM,
        cost_estimate=cost(36),
        name="feed_forward",
    )(side, lengths, flat(tokens), flat(cotangent), flat(attended), flat(linv), own, other, norms)


def backward_kernel(n1t_ref, qkv_ref, p_ref, gatt_ref, att_ref, gp_ref, gown_ref, gother_ref, gqkv_ref):
    seq = pl.program_id(0)
    pairs, rows = qkv_ref.shape[:2]

    @pl.when(seq == 0)
    def _():
        gqkv_ref[...] = jnp.zeros_like(gqkv_ref)

    lane = lax.broadcasted_iota(jnp.int32, (rows, PAIR), 1)
    zero = jnp.zeros((rows, PAIR), BF16)
    state = {}

    def begin(pair, half):
        if half == 0:
            cols = slice(pair * PAIR, (pair + 1) * PAIR)
            ga = gatt_ref[:, cols]
            state[pair] = dict(
                ga=ga,
                inner=ga.astype(F32) * att_ref[:, cols].astype(F32),
                gat=ga.T,
                qt=qkv_ref[pair, :, :PAIR].T,
                gq=[],
                gkt=[],
                gvt=[],
            )
        mask = (lane < HD) == (half == 0)
        return pair, half, mask, mm(jnp.where(mask, state[pair]["ga"], zero), qkv_ref[pair, :, 2 * PAIR :], NT)

    def finish(pair, half, mask, dp):
        mine = state[pair]
        hs = slice(half * HD, half * HD + HD)
        p = p_ref[pair * 2 + half]
        mine["gvt"].append(mm(mine["gat"][hs], p))
        inner = jnp.sum(jnp.where(mask, mine["inner"], 0.0), axis=-1, keepdims=True)
        ds = (p.astype(F32) * (dp - inner)).astype(BF16)
        mine["gq"].append(mm(ds, qkv_ref[pair, :, PAIR : 2 * PAIR]))
        mine["gkt"].append(mm(mine["qt"][hs], ds))
        if half == 1:
            joined = jnp.where(lane < HD, mine["gq"][0], mine["gq"][1])
            gp_ref[pair, :, :PAIR] = (joined * (HD**-0.5)).astype(BF16)
            gp_ref[pair, :, PAIR : 2 * PAIR] = jnp.concatenate(mine["gkt"], axis=0).astype(BF16).T
            gp_ref[pair, :, 2 * PAIR :] = jnp.concatenate(mine["gvt"], axis=0).astype(BF16).T
            gqkv_ref[pair] += mm(n1t_ref[...], gp_ref[pair])

    pending = None
    for pair in range(pairs):
        for half in range(2):
            fresh = begin(pair, half)
            if pending is not None:
                finish(*pending)
            pending = fresh
    finish(*pending)

    @pl.when(seq == pl.num_programs(0) - 1)
    def _():
        sides = join_pairs(gqkv_ref[0], gqkv_ref[1], gqkv_ref[2], 3 * HD)
        blank = jnp.zeros((gqkv_ref.shape[1], HD), F32)
        for columns, ref in zip(sides, (gown_ref, gother_ref)):
            ref[...] = jnp.concatenate(columns + [blank], axis=1).astype(BF16)


def backward(n1t, qkv, probs, gatt, attended):
    seqs, rows, width = attended.shape
    pairs = width // PAIR
    sq = pl.squeezed
    rowspec = pl.BlockSpec((sq, rows, width), lambda s: (s, 0, 0))
    groupspec = pl.BlockSpec((sq, pairs, rows, 3 * PAIR), lambda s: (s, 0, 0, 0))
    whole = lambda *dims: pl.BlockSpec(dims, lambda s: (0,) * len(dims))
    shape = jax.ShapeDtypeStruct
    packed = (width, 10 * HD)
    return pl.pallas_call(
        backward_kernel,
        grid=(seqs,),
        in_specs=[
            pl.BlockSpec((sq, width, rows), lambda s: (s, 0, 0)),
            groupspec,
            pl.BlockSpec((sq, 2 * pairs, rows, rows), lambda s: (s, 0, 0, 0)),
            rowspec,
            rowspec,
        ],
        out_specs=[groupspec, whole(*packed), whole(*packed)],
        out_shape=[shape(qkv.shape, BF16), shape(packed, BF16), shape(packed, BF16)],
        scratch_shapes=[pltpu.VMEM((pairs, width, 3 * PAIR), F32)],
        compiler_params=VMEM,
        cost_estimate=cost(27),
        name="attention_backward",
    )(n1t, qkv, probs, gatt, attended)


def input_kernel(tok_ref, gp_ref, gmid_ref, w_ref, norms_ref, two_ref, gin_ref, terms_ref):
    rows, width = tok_ref.shape
    gone = mm(gp_ref[0], w_ref[0], NT)
    for pair in range(1, w_ref.shape[0]):
        gone = gone + mm(gp_ref[pair], w_ref[pair], NT)
    normal, rs = normalize(tok_ref[...].astype(F32))

    @pl.when(pl.program_id(0) == 0)
    def _():
        terms_ref[...] = jnp.zeros_like(terms_ref)
        terms_ref[2:3, :] = jnp.sum(two_ref[0:8, :], axis=0, keepdims=True)
        terms_ref[3:4, :] = jnp.sum(two_ref[8:16, :], axis=0, keepdims=True)

    terms_ref[0:1, :] += jnp.sum(gone * normal, axis=0, keepdims=True)
    terms_ref[1:2, :] += jnp.sum(gone, axis=0, keepdims=True)
    gin_ref[...] = gmid_ref[...] + norm_backward(normal, rs, gone * norms_ref[0:1, :])


def input_gradient(tokens, gp, gmid, wpairs, norms, gnorm_two):
    seqs, rows, width = tokens.shape
    pairs = width // PAIR
    sq = pl.squeezed
    full = pl.BlockSpec((sq, rows, width), lambda s: (s, 0, 0))
    whole = lambda *dims: pl.BlockSpec(dims, lambda s: (0,) * len(dims))
    shape = jax.ShapeDtypeStruct
    return pl.pallas_call(
        input_kernel,
        grid=(seqs,),
        in_specs=[
            full,
            pl.BlockSpec((sq, pairs, rows, 3 * PAIR), lambda s: (s, 0, 0, 0)),
            full,
            whole(pairs, width, 3 * PAIR),
            whole(4, width),
            whole(16, width),
        ],
        out_specs=[full, whole(8, width)],
        out_shape=[shape((seqs, rows, width), F32), shape((8, width), F32)],
        compiler_params=VMEM,
        cost_estimate=cost(12),
        name="input_gradient",
    )(tokens, gp, gmid, wpairs, norms, gnorm_two)


def pack_kernel(qkv_ref, out_ref, up_ref, down_ref, norm_ref, lead_ref, rest_ref):
    chips, rows, _ = lead_ref.shape
    part = norm_ref.shape[1]
    norm = norm_ref[...]
    high = norm.astype(BF16).astype(F32)
    row = lax.broadcasted_iota(jnp.int32, (rows, part), 0)
    extra = jnp.where(row == 0, high, jnp.where(row == 1, norm - high, 0.0))
    columns = [qkv_ref[c, :, :PAIR] for c in range(3)] + [qkv_ref[c, :, PAIR:] for c in range(3)]
    blank = jnp.zeros((rows, HD - part), F32)
    lead_ref[...] = jnp.broadcast_to(
        jnp.concatenate(columns + [extra, blank], axis=1).astype(BF16)[None], lead_ref.shape
    )
    blank = jnp.zeros((rows, HD), F32)
    rest_ref[...] = jnp.broadcast_to(
        jnp.concatenate([up_ref[...], down_ref[...], out_ref[...], blank], axis=1).astype(BF16)[None], rest_ref.shape
    )


def sum_kernel(lead_parts_ref, rest_parts_ref, terms_ref, lead_ref, rest_ref, message_ref):
    total = jnp.zeros((lead_ref.shape[0], PAIR), F32)
    for parts_ref, ref in ((lead_parts_ref, lead_ref), (rest_parts_ref, rest_ref)):
        for start in range(0, ref.shape[1], PAIR):
            cols = slice(start, start + PAIR)
            piece = jnp.sum(parts_ref[:, :, cols].astype(F32), axis=0)
            ref[:, cols] = piece
            total = total + piece * piece
    message_ref[...] = terms_ref[...]
    message_ref[4:5, :PAIR] = jnp.sum(total, axis=0, keepdims=True)


def adamw(master, gradient, moments, rate, decay):
    moment = BETA_ONE * moments[0] + (1.0 - BETA_ONE) * gradient
    second = BETA_TWO * moments[1] + (1.0 - BETA_TWO) * gradient * gradient
    step_size = (
        moment / (1.0 - BETA_ONE**STEP) / (jnp.sqrt(second / (1.0 - BETA_TWO**STEP)) + ADAM_EPS)
    )
    return master - rate * (step_size + decay * master), moment, second


def update_kernel(
    message_ref, mine_ref, lead_ref, rest_ref,
    qkv_ref, out_ref, up_ref, down_ref, norm_ref,
    qkv_m_ref, out_m_ref, up_m_ref, down_m_ref, norm_m_ref,
    gn_ref, qkv_n_ref, out_n_ref, up_n_ref, down_n_ref, norm_n_ref,
    qkv_s_ref, out_s_ref, up_s_ref, down_s_ref, norm_s_ref, grads_ref,
):
    units = up_ref.shape[1]
    terms = message_ref[0:4, :]
    squares = jnp.sum(terms * terms, axis=(0, 1), keepdims=True) + jnp.sum(
        message_ref[4:5, :], axis=(0, 1), keepdims=True
    )
    grad_norm = jnp.sqrt(squares)
    gn_ref[...] = grad_norm
    factor = jnp.minimum(1.0, CLIP_NORM / (grad_norm + 1e-06))
    for c in range(3):
        wide = lead_ref[:, c * PAIR : (c + 1) * PAIR]
        narrow = lead_ref[:, 3 * PAIR + c * HD : 3 * PAIR + (c + 1) * HD]
        for cols, grad in ((slice(0, PAIR), wide), (slice(PAIR, PAIR + HD), narrow)):
            new, moment, second = adamw(
                qkv_ref[c, :, cols], factor * grad, qkv_m_ref[:, c, :, cols], RATE_LIST[0], DECAY_LIST[0]
            )
            qkv_n_ref[c, :, cols] = new
            qkv_s_ref[0, c, :, cols] = moment
            qkv_s_ref[1, c, :, cols] = second
    norm_grads = factor * mine_ref[...]
    grads_ref[...] = norm_grads
    plain = (
        (out_ref, rest_ref[:, 2 * units : 2 * units + 3 * HD], out_m_ref, out_n_ref, out_s_ref, 1),
        (up_ref, rest_ref[:, :units], up_m_ref, up_n_ref, up_s_ref, 2),
        (down_ref, rest_ref[:, units : 2 * units], down_m_ref, down_n_ref, down_s_ref, 3),
    )
    for master, grad, moments, next_ref, state_ref, i in plain:
        next_ref[...], state_ref[0], state_ref[1] = adamw(
            master[...], factor * grad, moments[...], RATE_LIST[i], DECAY_LIST[i]
        )
    norm_n_ref[...], norm_s_ref[0:1, :], norm_s_ref[1:2, :] = adamw(
        norm_ref[...], norm_grads, (norm_m_ref[0:1, :], norm_m_ref[1:2, :]), RATE_LIST[4], DECAY_LIST[4]
    )


def small_call(kernel, name, out_shape, *operands):
    return pl.pallas_call(kernel, out_shape=out_shape, compiler_params=VMEM, cost_estimate=cost(3), name=name)(
        *operands
    )


def swap(values):
    return lax.ppermute(values, "head", [(0, 1), (1, 0)])


def per_device(
    chips,
    tokens,
    cotangent,
    lengths,
    key_masks,
    qkv_master,
    out_master,
    up_master,
    down_master,
    norm_master,
    qkv_moments,
    out_moments,
    up_moments,
    down_moments,
    norm_moments,
):
    seqs, slot_rows, width = tokens.shape
    shard_rows = qkv_master.shape[0]
    norm_part = norm_master.shape[0]
    units = up_master.shape[1]
    side = lax.axis_index("head")

    qkv_rows = qkv_master.transpose(1, 0, 2)
    masters = (qkv_rows, out_master.T, up_master, down_master.T, norm_master[None])
    shape = jax.ShapeDtypeStruct
    lead, rest = small_call(
        pack_kernel,
        "pack_weights",
        [shape((chips, shard_rows, 10 * HD), BF16), shape((chips, shard_rows, 2 * units + 4 * HD), BF16)],
        *masters,
    )
    lead_own = lax.all_to_all(lead, "batch", 0, 0)
    rest_own = lax.all_to_all(rest, "batch", 0, 0)
    lead_other = swap(lead_own)
    flat = lambda a: a.reshape(chips * shard_rows, a.shape[-1])
    place = side.astype(jnp.int32).reshape(1)
    n1t, qkv, attended, linv, probs, wpairs, norms = forward(
        chips, norm_part, place, lengths, tokens, key_masks, flat(lead_own), flat(lead_other)
    )
    rest_own, attended = lax.optimization_barrier((rest_own, attended))
    rest_other = swap(rest_own)
    block_out, gmid, gatt, grest_own, grest_other, gnorm_two = middle(
        place, lengths, tokens, cotangent, attended, linv, flat(rest_own), flat(rest_other), norms
    )
    per_seq = lambda a: a.reshape(seqs, slot_rows, width)
    rest_sum = (grest_own.astype(F32) + swap(grest_other).astype(F32)).astype(BF16)
    rest_sum, gatt = lax.optimization_barrier((rest_sum, gatt))
    rest_parts = lax.all_to_all(rest_sum.reshape(rest.shape), "batch", 0, 0)
    gp, glead_own, glead_other = backward(n1t, qkv, probs, per_seq(gatt), attended)
    lead_sum = (glead_own.astype(F32) + swap(glead_other).astype(F32)).astype(BF16)
    lead_sum, rest_parts = lax.optimization_barrier((lead_sum, rest_parts))
    lead_parts = lax.all_to_all(lead_sum.reshape(chips, shard_rows, 10 * HD), "batch", 0, 0)
    input_grad, terms = input_gradient(tokens, gp, per_seq(gmid), wpairs, norms, gnorm_two)
    lead_shard, rest_shard, message = small_call(
        sum_kernel,
        "sum_parts",
        [shape(lead.shape[1:], F32), shape(rest.shape[1:], F32), shape(terms.shape, F32)],
        lead_parts,
        rest_parts,
        terms,
    )
    message = message + swap(message)
    stride = 1
    while stride < chips:
        message = message + lax.ppermute(message, "batch", [(i, i ^ stride) for i in range(chips)])
        stride *= 2
    start = (lax.axis_index("batch") * 2 + side) * norm_part
    mine = lax.dynamic_slice_in_dim(message[:4].reshape(1, 4 * width), start, norm_part, axis=1)
    like = lambda a: shape(a.shape, F32)
    moments = (
        qkv_moments.transpose(0, 2, 1, 3),
        out_moments.transpose(0, 2, 1),
        up_moments,
        down_moments.transpose(0, 2, 1),
        norm_moments,
    )
    results = small_call(
        update_kernel,
        "update_weights",
        [shape((1, 1), F32)] + [like(a) for a in masters + moments] + [like(mine)],
        message,
        mine,
        lead_shard,
        rest_shard,
        *masters,
        *moments,
    )
    grad_norm, qkv_next, out_next, up_next, down_next, norm_next = results[:6]
    qkv_states, out_states, up_states, down_states, norm_states, norm_grads = results[6:]
    return (
        per_seq(block_out),
        input_grad,
        grad_norm.reshape(()),
        qkv_next.transpose(1, 0, 2),
        out_next.T,
        up_next,
        down_next.T,
        norm_next[0],
        qkv_states.transpose(0, 2, 1, 3),
        out_states.transpose(0, 2, 1),
        up_states,
        down_states.transpose(0, 2, 1),
        norm_states,
        norm_grads[0],
    )


def solution(mesh):
    chips = mesh.shape["batch"]
    return jax.shard_map(
        functools.partial(per_device, chips),
        mesh=mesh,
        in_specs=(
            P(("batch", "head"), None, None),
            P(("batch", "head"), None, None),
            P("batch"),
            P("batch", None),
            P("batch", None, "head"),
            P("head", "batch"),
            P("batch", "head"),
            P("head", "batch"),
            P(("batch", "head")),
            P(None, "batch", None, "head"),
            P(None, "head", "batch"),
            P(None, "batch", "head"),
            P(None, "head", "batch"),
            P(None, ("batch", "head")),
        ),
        out_specs=(
            P(("batch", "head"), None, None),
            P(("batch", "head"), None, None),
            P(),
            P("batch", None, "head"),
            P("head", "batch"),
            P("batch", "head"),
            P("head", "batch"),
            P(("batch", "head")),
            P(None, "batch", None, "head"),
            P(None, "head", "batch"),
            P(None, "batch", "head"),
            P(None, "head", "batch"),
            P(None, ("batch", "head")),
            P(("batch", "head")),
        ),
        check_vma=False,
    )
```

```python
import functools

import jax
import jax.numpy as jnp
from jax import lax
from jax.experimental import pallas as pl
from jax.experimental.pallas import tpu as pltpu
from jax.sharding import PartitionSpec as P

HD = 64
STEP = 10
NORM_EPS = 1e-06
CLIP_NORM = 1000.0
BETA_ONE = 0.5
BETA_TWO = 0.5
ADAM_EPS = 1e-08
RATE_LIST = (0.06, 0.25, 0.06, 0.03, 0.5)
DECAY_LIST = (0.04, 0.04, 0.04, 0.04, 0.0)

F32 = jnp.float32
BF16 = jnp.bfloat16
NN = (((1,), (0,)), ((), ()))
NT = (((1,), (1,)), ((), ()))
TN = (((0,), (0,)), ((), ()))
QB = 320
FB = 512
FC = 256
PAIR = 2 * HD
LIMIT_A, LIMIT_B, LIMIT_C, LIMIT_D, LIMIT_S = (
    pltpu.CompilerParams(vmem_limit_bytes=m * 2**20) for m in (56, 46, 52, 52, 16)
)
IN_VMEM = pl.BlockSpec(memory_space=pltpu.VMEM)
IN_SMEM = pl.BlockSpec(memory_space=pltpu.SMEM)


def cost(microseconds):
    return pl.CostEstimate(flops=microseconds * 1_000_000_000, bytes_accessed=1_000_000, transcendentals=0)


def mm(left, right, dims=NN):
    return lax.dot_general(left, right, dims, preferred_element_type=F32)


def normalize(values):
    centred = values - jnp.mean(values, axis=-1, keepdims=True)
    variance = jnp.mean(centred * centred, axis=-1, keepdims=True)
    rs = lax.rsqrt(variance + NORM_EPS)
    return centred * rs, rs


def norm_backward(normal, rs, gained):
    inner = jnp.mean(gained * normal, axis=-1, keepdims=True)
    return rs * (gained - jnp.mean(gained, axis=-1, keepdims=True) - normal * inner)


def gelu_both(h, gradient):
    cdf = 0.5 + 0.5 * lax.erf(h * 0.7071067811865476)
    density = jnp.exp(h * h * -0.5) * 0.3989422804014327
    return (h * cdf).astype(BF16), (gradient * (cdf + h * density)).astype(BF16)


def split_pairs(own, other, per_pair):
    wide, narrow = 2 * per_pair, per_pair
    singles = []
    for part in range(per_pair // HD):
        cols = slice(wide + part * HD, wide + (part + 1) * HD)
        singles += [own[:, cols], other[:, cols]]
    return own[:, :wide], jnp.concatenate(singles, axis=1), other[:, :wide]


def join_pairs(first, second, third, per_pair):
    parts = [
        [second[:, p * PAIR + side * HD : p * PAIR + (side + 1) * HD] for p in range(per_pair // HD)]
        for side in range(2)
    ]
    return [first] + parts[0], [third] + parts[1]


def gathered_norms(first, second, chips, part, width):
    shard_rows = first.shape[0] // chips
    cols = slice(9 * HD, 9 * HD + part)
    pieces = []
    for chip in range(chips):
        row = chip * shard_rows
        for values in (first, second):
            pieces.append(values[row : row + 1, cols] + values[row + 1 : row + 2, cols])
    per_row = width // part
    return [jnp.concatenate(pieces[i * per_row : (i + 1) * per_row], axis=1) for i in range(4)]


def forward_kernel(
    chips, part, side_ref, len_ref, tok_ref, mask_ref, own_ref, other_ref,
    n1t_ref, qkv_ref, att_ref, linv_ref, p_ref, w_ref, norms_ref,
):
    rows, width = tok_ref.shape
    pairs = width // PAIR
    side, seq = side_ref[0], pl.program_id(0)

    @pl.when(seq == 0)
    def _():
        own, other = own_ref[...], other_ref[...]
        for i, weights in enumerate(split_pairs(own[:, : 9 * HD], other[:, : 9 * HD], 3 * HD)):
            w_ref[i] = weights
        tail = slice(8 * HD, 10 * HD)
        mine, theirs = own[:, tail].astype(F32), other[:, tail].astype(F32)
        pad = jnp.zeros((own.shape[0], 8 * HD), F32)
        first = jnp.concatenate([pad, jnp.where(side == 0, mine, theirs)], axis=1)
        second = jnp.concatenate([pad, jnp.where(side == 0, theirs, mine)], axis=1)
        for i, row in enumerate(gathered_norms(first, second, chips, part, width)):
            norms_ref[i : i + 1, :] = row

    member = side * pl.num_programs(0) + seq
    position = lax.broadcasted_iota(jnp.int32, (1, rows), 1)
    mask = mask_ref[pl.ds(member, 1), :]
    visible = (position < len_ref[member]) & ((mask == 1) | (position == 0))
    hidden = jnp.where(visible, 0.0, -1e30)
    hidden = jnp.broadcast_to(hidden, (PAIR, rows)).T.astype(BF16)

    normal, _ = normalize(tok_ref[...].astype(F32))
    n1 = (normal * norms_ref[0:1, :] + norms_ref[1:2, :]).astype(BF16)
    n1t_ref[...] = n1.T
    lane = lax.broadcasted_iota(jnp.int32, (QB, PAIR), 1)
    key_lane = lax.broadcasted_iota(jnp.int32, (rows, PAIR), 1)
    ones = jnp.ones((rows, PAIR), BF16)
    ready = {}

    def project(pair):
        out = mm(n1, w_ref[pair])
        queries = (out[:, :PAIR].astype(BF16).astype(F32) * (HD**-0.5)).astype(BF16)
        others = out[:, PAIR:].astype(BF16)
        qkv_ref[pair, :, :PAIR] = queries
        qkv_ref[pair, :, PAIR:] = others
        keys = [jnp.where(key_lane == HD * (1 - half), hidden, others[:, :PAIR]) for half in range(2)]
        return queries, keys, jnp.concatenate([others[:, PAIR:], ones], axis=1)

    def scores(pair, block, half):
        if pair not in ready:
            ready[pair] = project(pair)
        queries, keys, _ = ready[pair]
        spot = jnp.where(lane == HD * (1 - half), 1.0, 0.0).astype(BF16)
        part_queries = jnp.where((lane < HD) == (half == 0), queries[block * QB : (block + 1) * QB], spot)
        return mm(part_queries, keys[half], NT)

    outs = {}

    def finish(pair, block, half, s):
        sl = slice(block * QB, (block + 1) * QB)
        p = jnp.exp(s - jnp.max(s, axis=-1, keepdims=True)).astype(BF16)
        p_ref[pair * 2 + half, sl, :] = p
        out = mm(p, ready[pair][2])
        inverse = 1.0 / out[:, PAIR:]
        outs[half] = (out[:, :PAIR] * inverse, inverse)
        if half == 1:
            cols = slice(pair * PAIR, (pair + 1) * PAIR)
            att_ref[sl, cols] = jnp.where(lane < HD, outs[0][0], outs[1][0]).astype(BF16)
            linv_ref[sl, cols] = jnp.where(lane < HD, outs[0][1], outs[1][1])

    pending = None
    for pair in range(pairs):
        for block in range(rows // QB):
            for half in range(2):
                fresh = (pair, block, half, scores(pair, block, half))
                if pending is not None:
                    finish(*pending)
                pending = fresh
    finish(*pending)


def forward(chips, part, side, lengths, tokens, key_masks, own, other):
    seqs, rows, width = tokens.shape
    heads, pairs = width // HD, width // PAIR
    sq = pl.squeezed
    shape = jax.ShapeDtypeStruct
    whole = lambda *dims: pl.BlockSpec(dims, lambda s: (0,) * len(dims))
    row_spec = pl.BlockSpec((sq, rows, width), lambda s: (s, 0, 0))
    return pl.pallas_call(
        functools.partial(forward_kernel, chips, part),
        grid=(seqs,),
        in_specs=[IN_SMEM, IN_SMEM, row_spec, IN_VMEM, IN_VMEM, IN_VMEM],
        out_specs=[
            pl.BlockSpec((sq, width, rows), lambda s: (s, 0, 0)),
            pl.BlockSpec((sq, pairs, rows, 3 * PAIR), lambda s: (s, 0, 0, 0)),
            row_spec,
            row_spec,
            pl.BlockSpec((sq, heads, rows, rows), lambda s: (s, 0, 0, 0)),
            whole(pairs, width, 3 * PAIR),
            whole(4, width),
        ],
        out_shape=[
            shape((seqs, width, rows), BF16),
            shape((seqs, pairs, rows, 3 * PAIR), BF16),
            shape((seqs, rows, width), BF16),
            shape((seqs, rows, width), F32),
            shape((seqs, heads, rows, rows), BF16),
            shape((pairs, width, 3 * PAIR), BF16),
            shape((4, width), F32),
        ],
        compiler_params=LIMIT_A,
        cost_estimate=cost(24),
        name="attention_forward",
    )(side, lengths, tokens, key_masks, own, other)


def middle_kernel(
    seq_rows, units, side_ref, len_ref, tok_ref, cot_ref, att_ref, linv_ref, own_ref, other_ref, norms_ref,
    out_ref, gmid_ref, gatt_ref, gown_ref, gother_ref, gnorm_ref,
    halves, wo_ref, gout_ref, gup_ref, gdown_ref,
):
    step = pl.program_id(0)
    rows, width = tok_ref.shape

    @pl.when(step == 0)
    def _():
        gout_ref[...] = jnp.zeros_like(gout_ref)
        gup_ref[...] = jnp.zeros_like(gup_ref)
        gdown_ref[...] = jnp.zeros_like(gdown_ref)
        gnorm_ref[...] = jnp.zeros_like(gnorm_ref)
        for half, ref in enumerate((own_ref, other_ref)):
            halves[half] = ref[...]
        cols = slice(2 * units, 2 * units + 3 * HD)
        parts = split_pairs(halves[0, :, cols], halves[1, :, cols], HD)
        for i, part in enumerate(parts):
            wo_ref[:, i * PAIR : (i + 1) * PAIR] = part

    first = step * rows
    row = first + lax.broadcasted_iota(jnp.int32, (rows, 1), 0)
    live = row < 0
    seqs = rows * pl.num_programs(0) // seq_rows
    for near in range(-(-rows // seq_rows) + 1):
        s = first // seq_rows + near
        bound = jnp.where(s < seqs, len_ref[side_ref[0] * seqs + jnp.minimum(s, seqs - 1)], 0)
        live = live | ((row >= s * seq_rows) & (row < s * seq_rows + bound))

    x = tok_ref[...].astype(F32)
    att = att_ref[...]
    mid = x + mm(att, wo_ref[...], NT)
    normal, rs = normalize(mid)
    gain, shift = norms_ref[2:3, :], norms_ref[3:4, :]
    n2 = (normal * gain + shift).astype(BF16)
    n2t = n2.T
    up = jnp.where(live, cot_ref[...].astype(F32), 0.0)
    gb = up.astype(BF16)
    gbt = gb.T
    sums = [mid, jnp.zeros_like(mid)]

    def begin(half, c):
        wu = halves[half, :, c * FC : (c + 1) * FC]
        wd = halves[half, :, units + c * FC : units + (c + 1) * FC]
        return half, c, wu, wd, mm(n2, wu), mm(gb, wd)

    def finish(half, c, wu, wd, h, ga):
        cols = slice(c * FC, (c + 1) * FC)
        act, gh = gelu_both(h, ga)
        sums[0] = sums[0] + mm(act, wd, NT)
        sums[1] = sums[1] + mm(gh, wu, NT)
        gup_ref[half, :, cols] += mm(n2t, gh)
        gdown_ref[half, :, cols] += mm(gbt, act)

    pending = None
    for half in range(2):
        for c in range(units // FC):
            fresh = begin(half, c)
            if pending is not None:
                finish(*pending)
            pending = fresh
    finish(*pending)
    bo, gtwo = sums
    out_ref[...] = bo.astype(BF16)
    gnorm_ref[0:8, :] += jnp.sum((gtwo * normal).reshape(rows // 8, 8, width), axis=0)
    gnorm_ref[8:16, :] += jnp.sum(gtwo.reshape(rows // 8, 8, width), axis=0)
    gmid = up + norm_backward(normal, rs, gtwo * gain)
    gmid_ref[...] = gmid
    gm = gmid.astype(BF16)
    gout_ref[...] += mm(gm, att, TN)
    gatt_ref[...] = (mm(gm, wo_ref[...]) * linv_ref[...]).astype(BF16)

    @pl.when(step == pl.num_programs(0) - 1)
    def _():
        total = gout_ref[...]
        sides = join_pairs(
            total[:, :PAIR], total[:, PAIR : 2 * PAIR], total[:, 2 * PAIR :], HD
        )
        for half, ref in enumerate((gown_ref, gother_ref)):
            ref[:, :units] = gup_ref[half].astype(BF16)
            ref[:, units : 2 * units] = gdown_ref[half].astype(BF16)
            blank = jnp.zeros((total.shape[0], HD), F32)
            ref[:, 2 * units :] = jnp.concatenate(sides[half] + [blank], axis=1).astype(BF16)


def middle(side, lengths, tokens, cotangent, attended, linv, own, other, norms):
    seqs, seq_rows, width = tokens.shape
    total = seqs * seq_rows
    packed = own.shape[-1]
    units = (packed - 4 * HD) // 2
    flat = lambda a: a.reshape(total, width)
    rowspec = pl.BlockSpec((FB, width), lambda s: (s, 0))
    whole = lambda *dims: pl.BlockSpec(dims, lambda s: (0,) * len(dims))
    shape = jax.ShapeDtypeStruct
    return pl.pallas_call(
        functools.partial(middle_kernel, seq_rows, units),
        grid=(total // FB,),
        in_specs=[
            IN_SMEM,
            IN_SMEM,
            rowspec,
            rowspec,
            rowspec,
            rowspec,
            IN_VMEM,
            IN_VMEM,
            whole(4, width),
        ],
        out_specs=[rowspec] * 3 + [IN_VMEM, IN_VMEM, whole(16, width)],
        out_shape=[
            shape((total, width), BF16),
            shape((total, width), F32),
            shape((total, width), BF16),
            shape((width, packed), BF16),
            shape((width, packed), BF16),
            shape((16, width), F32),
        ],
        scratch_shapes=[
            pltpu.VMEM((2, width, packed), BF16),
            pltpu.VMEM((width, width), BF16),
            pltpu.VMEM((width, width), F32),
            pltpu.VMEM((2, width, units), F32),
            pltpu.VMEM((2, width, units), F32),
        ],
        compiler_params=LIMIT_B,
        cost_estimate=cost(36),
        name="feed_forward",
    )(side, lengths, flat(tokens), flat(cotangent), flat(attended), flat(linv), own, other, norms)


def backward_kernel(n1t_ref, qkv_ref, p_ref, gatt_ref, att_ref, gp_ref, gown_ref, gother_ref, gqkv_ref):
    seq = pl.program_id(0)
    pairs, rows = qkv_ref.shape[:2]

    @pl.when(seq == 0)
    def _():
        gqkv_ref[...] = jnp.zeros_like(gqkv_ref)

    lane = lax.broadcasted_iota(jnp.int32, (rows, PAIR), 1)
    zero = jnp.zeros((rows, PAIR), BF16)
    state = {}

    def begin(pair, half):
        if half == 0:
            cols = slice(pair * PAIR, (pair + 1) * PAIR)
            ga = gatt_ref[:, cols]
            state[pair] = dict(
                ga=ga,
                inner=ga.astype(F32) * att_ref[:, cols].astype(F32),
                gat=ga.T,
                qt=qkv_ref[pair, :, :PAIR].T,
                gq=[],
                gkt=[],
                gvt=[],
            )
        mask = (lane < HD) == (half == 0)
        return pair, half, mask, mm(jnp.where(mask, state[pair]["ga"], zero), qkv_ref[pair, :, 2 * PAIR :], NT)

    def finish(pair, half, mask, dp):
        mine = state[pair]
        hs = slice(half * HD, half * HD + HD)
        p = p_ref[pair * 2 + half]
        mine["gvt"].append(mm(mine["gat"][hs], p))
        inner = jnp.sum(jnp.where(mask, mine["inner"], 0.0), axis=-1, keepdims=True)
        ds = (p.astype(F32) * (dp - inner)).astype(BF16)
        mine["gq"].append(mm(ds, qkv_ref[pair, :, PAIR : 2 * PAIR]))
        mine["gkt"].append(mm(mine["qt"][hs], ds))
        if half == 1:
            joined = jnp.where(lane < HD, mine["gq"][0], mine["gq"][1])
            gp_ref[pair, :, :PAIR] = (joined * (HD**-0.5)).astype(BF16)
            gp_ref[pair, :, PAIR : 2 * PAIR] = jnp.concatenate(mine["gkt"], axis=0).astype(BF16).T
            gp_ref[pair, :, 2 * PAIR :] = jnp.concatenate(mine["gvt"], axis=0).astype(BF16).T
            gqkv_ref[pair] += mm(n1t_ref[...], gp_ref[pair])

    pending = None
    for pair in range(pairs):
        for half in range(2):
            fresh = begin(pair, half)
            if pending is not None:
                finish(*pending)
            pending = fresh
    finish(*pending)

    @pl.when(seq == pl.num_programs(0) - 1)
    def _():
        sides = join_pairs(gqkv_ref[0], gqkv_ref[1], gqkv_ref[2], 3 * HD)
        blank = jnp.zeros((gqkv_ref.shape[1], HD), F32)
        for columns, ref in zip(sides, (gown_ref, gother_ref)):
            ref[...] = jnp.concatenate(columns + [blank], axis=1).astype(BF16)


def backward(n1t, qkv, probs, gatt, attended):
    seqs, rows, width = attended.shape
    pairs = width // PAIR
    sq = pl.squeezed
    rowspec = pl.BlockSpec((sq, rows, width), lambda s: (s, 0, 0))
    groupspec = pl.BlockSpec((sq, pairs, rows, 3 * PAIR), lambda s: (s, 0, 0, 0))
    shape = jax.ShapeDtypeStruct
    packed = (width, 10 * HD)
    return pl.pallas_call(
        backward_kernel,
        grid=(seqs,),
        in_specs=[
            pl.BlockSpec((sq, width, rows), lambda s: (s, 0, 0)),
            groupspec,
            pl.BlockSpec((sq, 2 * pairs, rows, rows), lambda s: (s, 0, 0, 0)),
            rowspec,
            rowspec,
        ],
        out_specs=[groupspec, IN_VMEM, IN_VMEM],
        out_shape=[shape(qkv.shape, BF16), shape(packed, BF16), shape(packed, BF16)],
        scratch_shapes=[pltpu.VMEM((pairs, width, 3 * PAIR), F32)],
        compiler_params=LIMIT_C,
        cost_estimate=cost(27),
        name="attention_backward",
    )(n1t, qkv, probs, gatt, attended)


def input_kernel(tok_ref, gp_ref, gmid_ref, w_ref, norms_ref, two_ref, gin_ref, terms_ref):
    rows, width = tok_ref.shape
    gone = mm(gp_ref[0], w_ref[0], NT)
    for pair in range(1, w_ref.shape[0]):
        gone = gone + mm(gp_ref[pair], w_ref[pair], NT)
    normal, rs = normalize(tok_ref[...].astype(F32))

    @pl.when(pl.program_id(0) == 0)
    def _():
        terms_ref[...] = jnp.zeros_like(terms_ref)
        terms_ref[2:3, :] = jnp.sum(two_ref[0:8, :], axis=0, keepdims=True)
        terms_ref[3:4, :] = jnp.sum(two_ref[8:16, :], axis=0, keepdims=True)

    terms_ref[0:1, :] += jnp.sum(gone * normal, axis=0, keepdims=True)
    terms_ref[1:2, :] += jnp.sum(gone, axis=0, keepdims=True)
    gin_ref[...] = gmid_ref[...] + norm_backward(normal, rs, gone * norms_ref[0:1, :])


def input_gradient(tokens, gp, gmid, wpairs, norms, gnorm_two):
    seqs, rows, width = tokens.shape
    pairs = width // PAIR
    sq = pl.squeezed
    full = pl.BlockSpec((sq, rows, width), lambda s: (s, 0, 0))
    whole = lambda *dims: pl.BlockSpec(dims, lambda s: (0,) * len(dims))
    shape = jax.ShapeDtypeStruct
    return pl.pallas_call(
        input_kernel,
        grid=(seqs,),
        in_specs=[
            full,
            pl.BlockSpec((sq, pairs, rows, 3 * PAIR), lambda s: (s, 0, 0, 0)),
            full,
            whole(pairs, width, 3 * PAIR),
            whole(4, width),
            whole(16, width),
        ],
        out_specs=[full, whole(8, width)],
        out_shape=[shape((seqs, rows, width), F32), shape((8, width), F32)],
        compiler_params=LIMIT_D,
        cost_estimate=cost(12),
        name="input_gradient",
    )(tokens, gp, gmid, wpairs, norms, gnorm_two)


def pack_lead_kernel(qkv_ref, norm_ref, lead_ref):
    chips, rows, _ = lead_ref.shape
    part = norm_ref.shape[1]
    norm = norm_ref[...]
    high = norm.astype(BF16).astype(F32)
    row = lax.broadcasted_iota(jnp.int32, (rows, part), 0)
    extra = jnp.where(row == 0, high, jnp.where(row == 1, norm - high, 0.0))
    columns = [qkv_ref[c, :, :PAIR] for c in range(3)] + [qkv_ref[c, :, PAIR:] for c in range(3)]
    blank = jnp.zeros((rows, HD - part), F32)
    packed = jnp.concatenate(columns + [extra, blank], axis=1).astype(BF16)
    lead_ref[...] = jnp.broadcast_to(packed[None], lead_ref.shape)


def pack_rest_kernel(out_ref, up_ref, down_ref, rest_ref):
    blank = jnp.zeros((out_ref.shape[0], HD), F32)
    packed = jnp.concatenate([up_ref[...], down_ref[...], out_ref[...], blank], axis=1).astype(BF16)
    rest_ref[...] = jnp.broadcast_to(packed[None], rest_ref.shape)


def add_kernel(left_ref, right_ref, out_ref):
    out_ref[...] = (left_ref[...].astype(F32) + right_ref[...].astype(F32)).astype(BF16)


def sum_parts(parts_ref, out_ref):
    total = jnp.zeros((out_ref.shape[0], PAIR), F32)
    for start in range(0, out_ref.shape[1], PAIR):
        cols = slice(start, start + PAIR)
        piece = jnp.sum(parts_ref[:, :, cols].astype(F32), axis=0)
        out_ref[:, cols] = piece
        total = total + piece * piece
    return jnp.sum(total, axis=0, keepdims=True)


def sum_rest_kernel(parts_ref, out_ref, squares_ref):
    squares_ref[...] = sum_parts(parts_ref, out_ref)


def sum_lead_kernel(parts_ref, squares_ref, terms_ref, out_ref, message_ref):
    message_ref[...] = terms_ref[...]
    message_ref[4:5, :PAIR] = sum_parts(parts_ref, out_ref) + squares_ref[...]


def adamw(master, gradient, moments, rate, decay):
    moment = BETA_ONE * moments[0] + (1.0 - BETA_ONE) * gradient
    second = BETA_TWO * moments[1] + (1.0 - BETA_TWO) * gradient * gradient
    step_size = (
        moment / (1.0 - BETA_ONE**STEP) / (jnp.sqrt(second / (1.0 - BETA_TWO**STEP)) + ADAM_EPS)
    )
    return master - rate * (step_size + decay * master), moment, second


def update_kernel(
    index_ref, message_ref, lead_ref, rest_ref,
    qkv_ref, out_ref, up_ref, down_ref, norm_ref,
    qkv_m_ref, out_m_ref, up_m_ref, down_m_ref, norm_m_ref,
    gn_ref, qkv_n_ref, out_n_ref, up_n_ref, down_n_ref, norm_n_ref,
    qkv_s_ref, out_s_ref, up_s_ref, down_s_ref, norm_s_ref, grads_ref,
):
    units = up_ref.shape[1]
    terms = message_ref[0:4, :]
    squares = jnp.sum(terms * terms, axis=(0, 1), keepdims=True) + jnp.sum(
        message_ref[4:5, :], axis=(0, 1), keepdims=True
    )
    grad_norm = jnp.sqrt(squares)
    gn_ref[...] = grad_norm
    factor = jnp.minimum(1.0, CLIP_NORM / (grad_norm + 1e-06))
    for c in range(3):
        wide = lead_ref[:, c * PAIR : (c + 1) * PAIR]
        narrow = lead_ref[:, 3 * PAIR + c * HD : 3 * PAIR + (c + 1) * HD]
        for cols, grad in ((slice(0, PAIR), wide), (slice(PAIR, PAIR + HD), narrow)):
            new, moment, second = adamw(
                qkv_ref[c, :, cols], factor * grad, qkv_m_ref[:, c, :, cols], RATE_LIST[0], DECAY_LIST[0]
            )
            qkv_n_ref[c, :, cols] = new
            qkv_s_ref[0, c, :, cols] = moment
            qkv_s_ref[1, c, :, cols] = second
    part = norm_ref.shape[1]
    per_row = terms.shape[1] // part
    row = message_ref[pl.ds(index_ref[0] // per_row, 1), :]
    mine = pltpu.roll(row, lax.rem(per_row - lax.rem(index_ref[0], per_row), per_row) * part, 1)[:, :part]
    norm_grads = factor * mine
    grads_ref[...] = norm_grads
    plain = (
        (out_ref, rest_ref[:, 2 * units : 2 * units + 3 * HD], out_m_ref, out_n_ref, out_s_ref, 1),
        (up_ref, rest_ref[:, :units], up_m_ref, up_n_ref, up_s_ref, 2),
        (down_ref, rest_ref[:, units : 2 * units], down_m_ref, down_n_ref, down_s_ref, 3),
    )
    for master, grad, moments, next_ref, state_ref, i in plain:
        next_ref[...], state_ref[0], state_ref[1] = adamw(
            master[...], factor * grad, moments[...], RATE_LIST[i], DECAY_LIST[i]
        )
    norm_n_ref[...], norm_s_ref[0:1, :], norm_s_ref[1:2, :] = adamw(
        norm_ref[...], norm_grads, (norm_m_ref[0:1, :], norm_m_ref[1:2, :]), RATE_LIST[4], DECAY_LIST[4]
    )


def small_call(kernel, name, out_shape, *operands, in_spec=IN_VMEM):
    return pl.pallas_call(
        kernel,
        in_specs=[IN_SMEM if a.dtype == jnp.int32 else in_spec for a in operands],
        out_specs=jax.tree.map(lambda a: IN_VMEM, out_shape),
        out_shape=out_shape,
        compiler_params=LIMIT_S,
        cost_estimate=cost(2),
        name=name,
    )(*operands)


def swap(values):
    return lax.ppermute(values, "head", [(0, 1), (1, 0)])


def per_device(
    chips,
    tokens,
    cotangent,
    lengths,
    key_masks,
    qkv_master,
    out_master,
    up_master,
    down_master,
    norm_master,
    qkv_moments,
    out_moments,
    up_moments,
    down_moments,
    norm_moments,
):
    seqs, slot_rows, width = tokens.shape
    shard_rows = qkv_master.shape[0]
    norm_part = norm_master.shape[0]
    units = up_master.shape[1]
    side = lax.axis_index("head")

    qkv_rows = qkv_master.transpose(1, 0, 2)
    masters = (qkv_rows, out_master.T, up_master, down_master.T, norm_master[None])
    shape = jax.ShapeDtypeStruct
    lead = small_call(
        pack_lead_kernel,
        "pack_lead",
        shape((chips, shard_rows, 10 * HD), BF16),
        qkv_rows,
        norm_master[None],
        in_spec=pl.BlockSpec(),
    )
    rest = small_call(
        pack_rest_kernel, "pack_rest", shape((chips, shard_rows, 2 * units + 4 * HD), BF16), masters[1], *masters[2:4]
    )
    lead_own = lax.all_to_all(lead, "batch", 0, 0)
    lead_own, rest = lax.optimization_barrier((lead_own, rest))
    rest_own = lax.all_to_all(rest, "batch", 0, 0)
    lead_other = swap(lead_own)
    flat = lambda a: a.reshape(chips * shard_rows, a.shape[-1])
    place = side.astype(jnp.int32).reshape(1)
    n1t, qkv, attended, linv, probs, wpairs, norms = forward(
        chips, norm_part, place, lengths, tokens, key_masks, flat(lead_own), flat(lead_other)
    )
    rest_own, attended = lax.optimization_barrier((rest_own, attended))
    rest_other = swap(rest_own)
    block_out, gmid, gatt, grest_own, grest_other, gnorm_two = middle(
        place, lengths, tokens, cotangent, attended, linv, flat(rest_own), flat(rest_other), norms
    )
    per_seq = lambda a: a.reshape(seqs, slot_rows, width)
    plus = lambda name, a, b: small_call(add_kernel, name, shape(a.shape, BF16), a, b)
    rest_sum = plus("add_rest", grest_own, swap(grest_other))
    rest_sum, gatt = lax.optimization_barrier((rest_sum, gatt))
    rest_parts = lax.all_to_all(rest_sum.reshape(rest.shape), "batch", 0, 0)
    gp, glead_own, glead_other = backward(n1t, qkv, probs, per_seq(gatt), attended)
    lead_sum = plus("add_lead", glead_own, swap(glead_other))
    lead_sum, rest_parts = lax.optimization_barrier((lead_sum, rest_parts))
    lead_parts = lax.all_to_all(lead_sum.reshape(chips, shard_rows, 10 * HD), "batch", 0, 0)
    input_grad, terms = input_gradient(tokens, gp, per_seq(gmid), wpairs, norms, gnorm_two)
    rest_shard, squares = small_call(
        sum_rest_kernel, "sum_rest", [shape(rest.shape[1:], F32), shape((1, PAIR), F32)], rest_parts
    )
    lead_shard, message = small_call(
        sum_lead_kernel,
        "sum_lead",
        [shape(lead.shape[1:], F32), shape(terms.shape, F32)],
        lead_parts,
        squares,
        terms,
    )
    message = message + swap(message)
    stride = 1
    while stride < chips:
        message = message + lax.ppermute(message, "batch", [(i, i ^ stride) for i in range(chips)])
        stride *= 2
    like = lambda a: shape(a.shape, F32)
    moments = (
        qkv_moments.transpose(0, 2, 1, 3),
        out_moments.transpose(0, 2, 1),
        up_moments,
        down_moments.transpose(0, 2, 1),
        norm_moments,
    )
    results = small_call(
        update_kernel,
        "update_weights",
        [shape((1, 1), F32)] + [like(a) for a in masters + moments] + [shape((1, norm_part), F32)],
        (lax.axis_index("batch") * 2 + side).astype(jnp.int32).reshape(1),
        message,
        lead_shard,
        rest_shard,
        *masters,
        *moments,
    )
    grad_norm, qkv_next, out_next, up_next, down_next, norm_next = results[:6]
    qkv_states, out_states, up_states, down_states, norm_states, norm_grads = results[6:]
    return (
        per_seq(block_out),
        input_grad,
        grad_norm.reshape(()),
        qkv_next.transpose(1, 0, 2),
        out_next.T,
        up_next,
        down_next.T,
        norm_next[0],
        qkv_states.transpose(0, 2, 1, 3),
        out_states.transpose(0, 2, 1),
        up_states,
        down_states.transpose(0, 2, 1),
        norm_states,
        norm_grads[0],
    )


def solution(mesh):
    chips = mesh.shape["batch"]
    return jax.shard_map(
        functools.partial(per_device, chips),
        mesh=mesh,
        in_specs=(
            P(("batch", "head"), None, None),
            P(("batch", "head"), None, None),
            P("batch"),
            P("batch", None),
            P("batch", None, "head"),
            P("head", "batch"),
            P("batch", "head"),
            P("head", "batch"),
            P(("batch", "head")),
            P(None, "batch", None, "head"),
            P(None, "head", "batch"),
            P(None, "batch", "head"),
            P(None, "head", "batch"),
            P(None, ("batch", "head")),
        ),
        out_specs=(
            P(("batch", "head"), None, None),
            P(("batch", "head"), None, None),
            P(),
            P("batch", None, "head"),
            P("head", "batch"),
            P("batch", "head"),
            P("head", "batch"),
            P(("batch", "head")),
            P(None, "batch", None, "head"),
            P(None, "head", "batch"),
            P(None, "batch", "head"),
            P(None, "head", "batch"),
            P(None, ("batch", "head")),
            P(("batch", "head")),
        ),
        check_vma=False,
    )
```

```python
import functools

import jax
import jax.numpy as jnp
from jax import lax
from jax.experimental import pallas as pl
from jax.experimental.pallas import tpu as pltpu
from jax.sharding import PartitionSpec as P

HD = 64
STEP = 10
NORM_EPS = 1e-06
CLIP_NORM = 1000.0
BETA_ONE = 0.5
BETA_TWO = 0.5
ADAM_EPS = 1e-08
RATE_LIST = (0.06, 0.25, 0.06, 0.03, 0.5)
DECAY_LIST = (0.04, 0.04, 0.04, 0.04, 0.0)

F32 = jnp.float32
BF16 = jnp.bfloat16
NN = (((1,), (0,)), ((), ()))
NT = (((1,), (1,)), ((), ()))
TN = (((0,), (0,)), ((), ()))
QB = 320
FB = 512
FC = 256
PAIR = 2 * HD
LIMIT_A, LIMIT_B, LIMIT_C, LIMIT_D, LIMIT_S, LIMIT_P = (
    pltpu.CompilerParams(vmem_limit_bytes=m * 2**20) for m in (52, 46, 52, 52, 16, 62)
)
IN_VMEM = pl.BlockSpec(memory_space=pltpu.VMEM)
IN_SMEM = pl.BlockSpec(memory_space=pltpu.SMEM)


def cost(microseconds):
    return pl.CostEstimate(flops=microseconds * 1_000_000_000, bytes_accessed=1_000_000, transcendentals=0)


def mm(left, right, dims=NN):
    return lax.dot_general(left, right, dims, preferred_element_type=F32)


def normalize(values):
    centred = values - jnp.mean(values, axis=-1, keepdims=True)
    variance = jnp.mean(centred * centred, axis=-1, keepdims=True)
    rs = lax.rsqrt(variance + NORM_EPS)
    return centred * rs, rs


def norm_backward(normal, rs, gained):
    inner = jnp.mean(gained * normal, axis=-1, keepdims=True)
    return rs * (gained - jnp.mean(gained, axis=-1, keepdims=True) - normal * inner)


def gelu_both(h, gradient):
    cdf = 0.5 + 0.5 * lax.erf(h * 0.7071067811865476)
    density = jnp.exp(h * h * -0.5) * 0.3989422804014327
    return (h * cdf).astype(BF16), (gradient * (cdf + h * density)).astype(BF16)


def split_pairs(own, other, per_pair):
    wide, narrow = 2 * per_pair, per_pair
    singles = []
    for part in range(per_pair // HD):
        cols = slice(wide + part * HD, wide + (part + 1) * HD)
        singles += [own[:, cols], other[:, cols]]
    return own[:, :wide], jnp.concatenate(singles, axis=1), other[:, :wide]


def join_pairs(first, second, third, per_pair):
    parts = [
        [second[:, p * PAIR + side * HD : p * PAIR + (side + 1) * HD] for p in range(per_pair // HD)]
        for side in range(2)
    ]
    return [first] + parts[0], [third] + parts[1]


def gathered_norms(first, second, chips, part, width):
    shard_rows = first.shape[0] // chips
    cols = slice(9 * HD, 9 * HD + part)
    pieces = []
    for chip in range(chips):
        row = chip * shard_rows
        for values in (first, second):
            pieces.append(values[row : row + 1, cols] + values[row + 1 : row + 2, cols])
    per_row = width // part
    return [jnp.concatenate(pieces[i * per_row : (i + 1) * per_row], axis=1) for i in range(4)]


def prepare_kernel(seq_rows, side_ref, len_ref, tok_ref, cot_ref, normal_ref, masked_ref, masked_t_ref):
    step = pl.program_id(0)
    rows = tok_ref.shape[0]
    first = step * rows
    row = first + lax.broadcasted_iota(jnp.int32, (rows, 1), 0)
    live = row < 0
    seqs = rows * pl.num_programs(0) // seq_rows
    for near in range(-(-rows // seq_rows) + 1):
        s = first // seq_rows + near
        bound = jnp.where(s < seqs, len_ref[side_ref[0] * seqs + jnp.minimum(s, seqs - 1)], 0)
        live = live | ((row >= s * seq_rows) & (row < s * seq_rows + bound))

    normal_ref[...], _ = normalize(tok_ref[...].astype(F32))
    masked = jnp.where(live, cot_ref[...].astype(F32), 0.0).astype(BF16)
    masked_ref[...] = masked
    masked_t_ref[...] = masked.T


def prepare(side, lengths, tokens, cotangent):
    seqs, seq_rows, width = tokens.shape
    total = seqs * seq_rows
    flat = lambda a: a.reshape(total, width)
    rowspec = pl.BlockSpec((FB, width), lambda s: (s, 0))
    shape = jax.ShapeDtypeStruct
    return pl.pallas_call(
        functools.partial(prepare_kernel, seq_rows),
        grid=(total // FB,),
        in_specs=[IN_SMEM, IN_SMEM, rowspec, rowspec],
        out_specs=[rowspec, rowspec, pl.BlockSpec((width, FB), lambda s: (0, s))],
        out_shape=[shape((total, width), F32), shape((total, width), BF16), shape((width, total), BF16)],
        compiler_params=LIMIT_P,
        cost_estimate=cost(5),
        name="prepare",
    )(side, lengths, flat(tokens), flat(cotangent))


def key_limits(rows):
    return [*range(256, rows, 256), rows]


def forward_kernel(
    chips, part, side_ref, len_ref, normal_ref, mask_ref, own_ref, other_ref,
    n1t_ref, qkv_ref, att_ref, linv_ref, p_ref, w_ref, norms_ref,
):
    rows, width = normal_ref.shape
    pairs = width // PAIR
    side, seq = side_ref[0], pl.program_id(0)

    @pl.when(seq == 0)
    def _():
        own, other = own_ref[...], other_ref[...]
        for i, weights in enumerate(split_pairs(own[:, : 9 * HD], other[:, : 9 * HD], 3 * HD)):
            w_ref[i] = weights
        tail = slice(8 * HD, 10 * HD)
        mine, theirs = own[:, tail].astype(F32), other[:, tail].astype(F32)
        pad = jnp.zeros((own.shape[0], 8 * HD), F32)
        first = jnp.concatenate([pad, jnp.where(side == 0, mine, theirs)], axis=1)
        second = jnp.concatenate([pad, jnp.where(side == 0, theirs, mine)], axis=1)
        for i, row in enumerate(gathered_norms(first, second, chips, part, width)):
            norms_ref[i : i + 1, :] = row

    member = side * pl.num_programs(0) + seq
    position = lax.broadcasted_iota(jnp.int32, (1, rows), 1)
    mask = mask_ref[pl.ds(member, 1), :]
    visible = (position < len_ref[member]) & ((mask == 1) | (position == 0))
    hidden = jnp.where(visible, 0.0, -1e30)
    hidden = jnp.broadcast_to(hidden, (PAIR, rows)).T.astype(BF16)

    low = 0
    for keys in key_limits(rows):
        pl.when((len_ref[member] > low) & (len_ref[member] <= keys))(
            functools.partial(
                attend, keys, hidden, normal_ref, norms_ref, w_ref, n1t_ref, qkv_ref, att_ref, linv_ref, p_ref
            )
        )
        low = keys


def attend(count, hidden, normal_ref, norms_ref, w_ref, n1t_ref, qkv_ref, att_ref, linv_ref, p_ref):
    rows, width = normal_ref.shape
    pairs = width // PAIR
    n1 = (normal_ref[...] * norms_ref[0:1, :] + norms_ref[1:2, :]).astype(BF16)
    n1t_ref[...] = n1.T
    lane = lax.broadcasted_iota(jnp.int32, (QB, PAIR), 1)
    key_lane = lax.broadcasted_iota(jnp.int32, (count, PAIR), 1)
    ones = jnp.ones((count, PAIR), BF16)
    hidden = hidden[:count]
    ready = {}

    def project(pair):
        out = mm(n1, w_ref[pair])
        queries = (out[:, :PAIR].astype(BF16).astype(F32) * (HD**-0.5)).astype(BF16)
        others = out[:, PAIR:].astype(BF16)
        qkv_ref[pair, :, :PAIR] = queries
        qkv_ref[pair, :, PAIR:] = others
        keys = [jnp.where(key_lane == HD * (1 - half), hidden, others[:count, :PAIR]) for half in range(2)]
        return queries, keys, jnp.concatenate([others[:count, PAIR:], ones], axis=1)

    def scores(pair, block, half):
        if pair not in ready:
            ready[pair] = project(pair)
        queries, keys, _ = ready[pair]
        spot = jnp.where(lane == HD * (1 - half), 1.0, 0.0).astype(BF16)
        part_queries = jnp.where((lane < HD) == (half == 0), queries[block * QB : (block + 1) * QB], spot)
        return mm(part_queries, keys[half], NT)

    outs = {}

    def finish(pair, block, half, s):
        sl = slice(block * QB, (block + 1) * QB)
        p = jnp.exp(s - jnp.max(s, axis=-1, keepdims=True)).astype(BF16)
        p_ref[pair * 2 + half, sl, :count] = p
        out = mm(p, ready[pair][2])
        inverse = 1.0 / out[:, PAIR:]
        outs[half] = (out[:, :PAIR] * inverse, inverse)
        if half == 1:
            cols = slice(pair * PAIR, (pair + 1) * PAIR)
            att_ref[sl, cols] = jnp.where(lane < HD, outs[0][0], outs[1][0]).astype(BF16)
            linv_ref[sl, cols] = jnp.where(lane < HD, outs[0][1], outs[1][1])

    pending = None
    for pair in range(pairs):
        for block in range(rows // QB):
            for half in range(2):
                fresh = (pair, block, half, scores(pair, block, half))
                if pending is not None:
                    finish(*pending)
                pending = fresh
    finish(*pending)


def forward(chips, part, side, lengths, normal, key_masks, own, other):
    seqs, rows, width = normal.shape
    heads, pairs = width // HD, width // PAIR
    sq = pl.squeezed
    shape = jax.ShapeDtypeStruct
    whole = lambda *dims: pl.BlockSpec(dims, lambda s: (0,) * len(dims))
    row_spec = pl.BlockSpec((sq, rows, width), lambda s: (s, 0, 0))
    return pl.pallas_call(
        functools.partial(forward_kernel, chips, part),
        grid=(seqs,),
        in_specs=[IN_SMEM, IN_SMEM, row_spec, IN_VMEM, IN_VMEM, IN_VMEM],
        out_specs=[
            pl.BlockSpec((sq, width, rows), lambda s: (s, 0, 0)),
            pl.BlockSpec((sq, pairs, rows, 3 * PAIR), lambda s: (s, 0, 0, 0)),
            row_spec,
            row_spec,
            pl.BlockSpec((sq, heads, rows, rows), lambda s: (s, 0, 0, 0)),
            whole(pairs, width, 3 * PAIR),
            IN_VMEM,
        ],
        out_shape=[
            shape((seqs, width, rows), BF16),
            shape((seqs, pairs, rows, 3 * PAIR), BF16),
            shape((seqs, rows, width), BF16),
            shape((seqs, rows, width), F32),
            shape((seqs, heads, rows, rows), BF16),
            shape((pairs, width, 3 * PAIR), BF16),
            shape((4, width), F32),
        ],
        compiler_params=LIMIT_A,
        cost_estimate=cost(24),
        name="attention_forward",
    )(side, lengths, normal, key_masks, own, other)


def middle_kernel(
    units, tok_ref, gb_ref, gbt_ref, att_ref, linv_ref, own_ref, other_ref, norms_ref,
    out_ref, gmid_ref, gatt_ref, gown_ref, gother_ref, gnorm_ref,
    halves, wo_ref, gout_ref, gup_ref, gdown_ref,
):
    step = pl.program_id(0)
    rows, width = tok_ref.shape

    @pl.when(step == 0)
    def _():
        gout_ref[...] = jnp.zeros_like(gout_ref)
        gup_ref[...] = jnp.zeros_like(gup_ref)
        gdown_ref[...] = jnp.zeros_like(gdown_ref)
        gnorm_ref[...] = jnp.zeros_like(gnorm_ref)
        members, sides, part, _ = own_ref.shape
        for half, ref in enumerate((own_ref, other_ref)):
            for place in range(members * sides):
                halves[half, place * part : (place + 1) * part, :] = ref[place % members, place // members]
        cols = slice(2 * units, 2 * units + 3 * HD)
        parts = split_pairs(halves[0, :, cols], halves[1, :, cols], HD)
        for i, part in enumerate(parts):
            wo_ref[:, i * PAIR : (i + 1) * PAIR] = part

    x = tok_ref[...].astype(F32)
    att = att_ref[...]
    mid = x + mm(att, wo_ref[...], NT)
    normal, rs = normalize(mid)
    gain, shift = norms_ref[2:3, :], norms_ref[3:4, :]
    n2 = (normal * gain + shift).astype(BF16)
    n2t = n2.T
    gb, gbt = gb_ref[...], gbt_ref[...]
    sums = [mid, jnp.zeros_like(mid)]

    def begin(half, c):
        wu = halves[half, :, c * FC : (c + 1) * FC]
        wd = halves[half, :, units + c * FC : units + (c + 1) * FC]
        return half, c, wu, wd, mm(n2, wu), mm(gb, wd)

    def finish(half, c, wu, wd, h, ga):
        cols = slice(c * FC, (c + 1) * FC)
        act, gh = gelu_both(h, ga)
        sums[0] = sums[0] + mm(act, wd, NT)
        sums[1] = sums[1] + mm(gh, wu, NT)
        gup_ref[half, :, cols] += mm(n2t, gh)
        gdown_ref[half, :, cols] += mm(gbt, act)

    pending = None
    for half in range(2):
        for c in range(units // FC):
            fresh = begin(half, c)
            if pending is not None:
                finish(*pending)
            pending = fresh
    finish(*pending)
    bo, gtwo = sums
    out_ref[...] = bo.astype(BF16)
    gnorm_ref[0:8, :] += jnp.sum((gtwo * normal).reshape(rows // 8, 8, width), axis=0)
    gnorm_ref[8:16, :] += jnp.sum(gtwo.reshape(rows // 8, 8, width), axis=0)
    gmid = gb.astype(F32) + norm_backward(normal, rs, gtwo * gain)
    gmid_ref[...] = gmid
    gm = gmid.astype(BF16)
    gout_ref[...] += mm(gm, att, TN)
    gatt_ref[...] = (mm(gm, wo_ref[...]) * linv_ref[...]).astype(BF16)

    @pl.when(step == pl.num_programs(0) - 1)
    def _():
        total = gout_ref[...]
        sides = join_pairs(
            total[:, :PAIR], total[:, PAIR : 2 * PAIR], total[:, 2 * PAIR :], HD
        )
        for half, ref in enumerate((gown_ref, gother_ref)):
            ref[:, :units] = gup_ref[half].astype(BF16)
            ref[:, units : 2 * units] = gdown_ref[half].astype(BF16)
            blank = jnp.zeros((total.shape[0], HD), F32)
            ref[:, 2 * units :] = jnp.concatenate(sides[half] + [blank], axis=1).astype(BF16)


def middle(tokens, masked, masked_t, attended, linv, own, other, norms):
    seqs, seq_rows, width = tokens.shape
    total = seqs * seq_rows
    packed = own.shape[-1]
    units = (packed - 4 * HD) // 2
    flat = lambda a: a.reshape(total, width)
    rowspec = pl.BlockSpec((FB, width), lambda s: (s, 0))
    whole = lambda *dims: pl.BlockSpec(dims, lambda s: (0,) * len(dims))
    shape = jax.ShapeDtypeStruct
    return pl.pallas_call(
        functools.partial(middle_kernel, units),
        grid=(total // FB,),
        in_specs=[
            rowspec,
            rowspec,
            pl.BlockSpec((width, FB), lambda s: (0, s)),
            rowspec,
            rowspec,
            IN_VMEM,
            IN_VMEM,
            IN_VMEM,
        ],
        out_specs=[rowspec] * 3 + [IN_VMEM, IN_VMEM, whole(16, width)],
        out_shape=[
            shape((total, width), BF16),
            shape((total, width), F32),
            shape((total, width), BF16),
            shape((width, packed), BF16),
            shape((width, packed), BF16),
            shape((16, width), F32),
        ],
        scratch_shapes=[
            pltpu.VMEM((2, width, packed), BF16),
            pltpu.VMEM((width, width), BF16),
            pltpu.VMEM((width, width), F32),
            pltpu.VMEM((2, width, units), F32),
            pltpu.VMEM((2, width, units), F32),
        ],
        compiler_params=LIMIT_B,
        cost_estimate=cost(36),
        name="feed_forward",
    )(flat(tokens), masked, masked_t, flat(attended), flat(linv), own, other, norms)


def backward_kernel(
    side_ref, len_ref, n1t_ref, qkv_ref, p_ref, gatt_ref, att_ref, gp_ref, gown_ref, gother_ref, gqkv_ref
):
    seq = pl.program_id(0)
    rows = qkv_ref.shape[1]

    @pl.when(seq == 0)
    def _():
        gqkv_ref[...] = jnp.zeros_like(gqkv_ref)

    length = len_ref[side_ref[0] * pl.num_programs(0) + seq]
    low = 0
    for count in key_limits(rows):
        pl.when((length > low) & (length <= count))(
            functools.partial(attend_backward, count, n1t_ref, qkv_ref, p_ref, gatt_ref, att_ref, gp_ref, gqkv_ref)
        )
        low = count

    @pl.when(seq == pl.num_programs(0) - 1)
    def _():
        sides = join_pairs(gqkv_ref[0], gqkv_ref[1], gqkv_ref[2], 3 * HD)
        blank = jnp.zeros((gqkv_ref.shape[1], HD), F32)
        for columns, ref in zip(sides, (gown_ref, gother_ref)):
            ref[...] = jnp.concatenate(columns + [blank], axis=1).astype(BF16)


def attend_backward(count, n1t_ref, qkv_ref, p_ref, gatt_ref, att_ref, gp_ref, gqkv_ref):
    pairs, rows = qkv_ref.shape[:2]
    lane = lax.broadcasted_iota(jnp.int32, (count, PAIR), 1)
    zero = jnp.zeros((count, PAIR), BF16)
    state = {}

    def begin(pair, half):
        if half == 0:
            cols = slice(pair * PAIR, (pair + 1) * PAIR)
            ga = gatt_ref[:count, cols]
            state[pair] = dict(
                ga=ga,
                inner=ga.astype(F32) * att_ref[:count, cols].astype(F32),
                gat=ga.T,
                qt=qkv_ref[pair, :count, :PAIR].T,
                gq=[],
                gkt=[],
                gvt=[],
            )
        mask = (lane < HD) == (half == 0)
        values = qkv_ref[pair, :count, 2 * PAIR :]
        return pair, half, mask, mm(jnp.where(mask, state[pair]["ga"], zero), values, NT)

    def finish(pair, half, mask, dp):
        mine = state[pair]
        hs = slice(half * HD, half * HD + HD)
        p = p_ref[pair * 2 + half, :count, :count]
        mine["gvt"].append(mm(mine["gat"][hs], p))
        inner = jnp.sum(jnp.where(mask, mine["inner"], 0.0), axis=-1, keepdims=True)
        ds = (p.astype(F32) * (dp - inner)).astype(BF16)
        mine["gq"].append(mm(ds, qkv_ref[pair, :count, PAIR : 2 * PAIR]))
        mine["gkt"].append(mm(mine["qt"][hs], ds))
        if half == 1:
            joined = jnp.where(lane < HD, mine["gq"][0], mine["gq"][1])
            gp_ref[pair, :count, :PAIR] = (joined * (HD**-0.5)).astype(BF16)
            gp_ref[pair, :count, PAIR : 2 * PAIR] = jnp.concatenate(mine["gkt"], axis=0).astype(BF16).T
            gp_ref[pair, :count, 2 * PAIR :] = jnp.concatenate(mine["gvt"], axis=0).astype(BF16).T
            if count < rows:
                gp_ref[pair, count:, :] = jnp.zeros((rows - count, 3 * PAIR), BF16)
            gqkv_ref[pair] += mm(n1t_ref[:, :count], gp_ref[pair, :count, :])

    pending = None
    for pair in range(pairs):
        for half in range(2):
            fresh = begin(pair, half)
            if pending is not None:
                finish(*pending)
            pending = fresh
    finish(*pending)


def backward(side, lengths, n1t, qkv, probs, gatt, attended):
    seqs, rows, width = attended.shape
    pairs = width // PAIR
    sq = pl.squeezed
    rowspec = pl.BlockSpec((sq, rows, width), lambda s: (s, 0, 0))
    groupspec = pl.BlockSpec((sq, pairs, rows, 3 * PAIR), lambda s: (s, 0, 0, 0))
    shape = jax.ShapeDtypeStruct
    packed = (width, 10 * HD)
    return pl.pallas_call(
        backward_kernel,
        grid=(seqs,),
        in_specs=[
            IN_SMEM,
            IN_SMEM,
            pl.BlockSpec((sq, width, rows), lambda s: (s, 0, 0)),
            groupspec,
            pl.BlockSpec((sq, 2 * pairs, rows, rows), lambda s: (s, 0, 0, 0)),
            rowspec,
            rowspec,
        ],
        out_specs=[groupspec, IN_VMEM, IN_VMEM],
        out_shape=[shape(qkv.shape, BF16), shape(packed, BF16), shape(packed, BF16)],
        scratch_shapes=[pltpu.VMEM((pairs, width, 3 * PAIR), F32)],
        compiler_params=LIMIT_C,
        cost_estimate=cost(27),
        name="attention_backward",
    )(side, lengths, n1t, qkv, probs, gatt, attended)


def input_kernel(tok_ref, gp_ref, gmid_ref, w_ref, norms_ref, two_ref, gin_ref, terms_ref):
    rows, width = tok_ref.shape
    gone = mm(gp_ref[0], w_ref[0], NT)
    for pair in range(1, w_ref.shape[0]):
        gone = gone + mm(gp_ref[pair], w_ref[pair], NT)
    normal, rs = normalize(tok_ref[...].astype(F32))

    @pl.when(pl.program_id(0) == 0)
    def _():
        terms_ref[...] = jnp.zeros_like(terms_ref)
        terms_ref[2:3, :] = jnp.sum(two_ref[0:8, :], axis=0, keepdims=True)
        terms_ref[3:4, :] = jnp.sum(two_ref[8:16, :], axis=0, keepdims=True)

    terms_ref[0:1, :] += jnp.sum(gone * normal, axis=0, keepdims=True)
    terms_ref[1:2, :] += jnp.sum(gone, axis=0, keepdims=True)
    gin_ref[...] = gmid_ref[...] + norm_backward(normal, rs, gone * norms_ref[0:1, :])


def input_gradient(tokens, gp, gmid, wpairs, norms, gnorm_two):
    seqs, rows, width = tokens.shape
    pairs = width // PAIR
    sq = pl.squeezed
    full = pl.BlockSpec((sq, rows, width), lambda s: (s, 0, 0))
    whole = lambda *dims: pl.BlockSpec(dims, lambda s: (0,) * len(dims))
    shape = jax.ShapeDtypeStruct
    return pl.pallas_call(
        input_kernel,
        grid=(seqs,),
        in_specs=[
            full,
            pl.BlockSpec((sq, pairs, rows, 3 * PAIR), lambda s: (s, 0, 0, 0)),
            full,
            whole(pairs, width, 3 * PAIR),
            IN_VMEM,
            whole(16, width),
        ],
        out_specs=[full, IN_VMEM],
        out_shape=[shape((seqs, rows, width), F32), shape((8, width), F32)],
        compiler_params=LIMIT_D,
        cost_estimate=cost(12),
        name="input_gradient",
    )(tokens, gp, gmid, wpairs, norms, gnorm_two)


def pack_lead_kernel(qkv_ref, norm_ref, lead_ref):
    chips, rows, _ = lead_ref.shape
    part = norm_ref.shape[1]
    norm = norm_ref[...]
    high = norm.astype(BF16).astype(F32)
    row = lax.broadcasted_iota(jnp.int32, (rows, part), 0)
    extra = jnp.where(row == 0, high, jnp.where(row == 1, norm - high, 0.0))
    columns = [qkv_ref[c, :, :PAIR] for c in range(3)] + [qkv_ref[c, :, PAIR:] for c in range(3)]
    blank = jnp.zeros((rows, HD - part), F32)
    packed = jnp.concatenate(columns + [extra, blank], axis=1).astype(BF16)
    lead_ref[...] = jnp.broadcast_to(packed[None], lead_ref.shape)


def pack_rest_kernel(out_ref, up_ref, down_ref, rest_ref):
    blank = jnp.zeros((out_ref.shape[0], HD), F32)
    rest_ref[...] = jnp.concatenate([up_ref[...], down_ref[...], out_ref[...], blank], axis=1).astype(BF16)


def pair_kernel(half_ref, own_ref, far_ref, out_ref):
    own, far = own_ref[...], far_ref[...]
    first = half_ref[0] == 0
    for slot, value in enumerate((jnp.where(first, own, far), jnp.where(first, far, own))):
        for member in range(out_ref.shape[0]):
            out_ref[member, slot] = value


def add_kernel(left_ref, right_ref, out_ref):
    out_ref[...] = (left_ref[...].astype(F32) + right_ref[...].astype(F32)).astype(BF16)


def add_split_kernel(left_ref, right_ref, out_ref):
    total = (left_ref[...].astype(F32) + right_ref[...].astype(F32)).astype(BF16)
    members, halves, rows, _ = out_ref.shape
    for half in range(halves):
        for member in range(members):
            start = (half * members + member) * rows
            out_ref[member, half] = total[start : start + rows]


def sum_parts(parts_ref, out_ref):
    total = jnp.zeros((out_ref.shape[0], PAIR), F32)
    for start in range(0, out_ref.shape[1], PAIR):
        cols = slice(start, start + PAIR)
        piece = jnp.sum(parts_ref[:, :, cols].astype(F32), axis=0)
        out_ref[:, cols] = piece
        total = total + piece * piece
    return jnp.sum(total, axis=0, keepdims=True)


def sum_rest_kernel(half_ref, parts_ref, mine_ref, theirs_ref):
    first = half_ref[0] == 0
    for start in range(0, mine_ref.shape[1], PAIR):
        cols = slice(start, start + PAIR)
        low = jnp.sum(parts_ref[:, 0, :, cols].astype(F32), axis=0)
        high = jnp.sum(parts_ref[:, 1, :, cols].astype(F32), axis=0)
        mine_ref[:, cols] = jnp.where(first, low, high)
        theirs_ref[:, cols] = jnp.where(first, high, low).astype(BF16)


def sum_lead_kernel(parts_ref, mine_ref, far_ref, terms_ref, out_ref, rest_ref, message_ref):
    squares = sum_parts(parts_ref, out_ref)
    rest = mine_ref[...] + far_ref[...].astype(F32)
    rest_ref[...] = rest
    total = jnp.zeros((rest.shape[0], PAIR), F32)
    for start in range(0, rest.shape[1], PAIR):
        piece = rest[:, start : start + PAIR]
        total = total + piece * piece
    message_ref[...] = terms_ref[...]
    message_ref[4:5, :PAIR] = squares + jnp.sum(total, axis=0, keepdims=True)


def adamw(master, gradient, moments, rate, decay):
    moment = BETA_ONE * moments[0] + (1.0 - BETA_ONE) * gradient
    second = BETA_TWO * moments[1] + (1.0 - BETA_TWO) * gradient * gradient
    step_size = (
        moment / (1.0 - BETA_ONE**STEP) / (jnp.sqrt(second / (1.0 - BETA_TWO**STEP)) + ADAM_EPS)
    )
    return master - rate * (step_size + decay * master), moment, second


def update_kernel(
    index_ref, message_ref, lead_ref, rest_ref,
    qkv_ref, out_ref, up_ref, down_ref, norm_ref,
    qkv_m_ref, out_m_ref, up_m_ref, down_m_ref, norm_m_ref,
    gn_ref, qkv_n_ref, out_n_ref, up_n_ref, down_n_ref, norm_n_ref,
    qkv_s_ref, out_s_ref, up_s_ref, down_s_ref, norm_s_ref, grads_ref,
):
    units = up_ref.shape[1]
    terms = message_ref[0:4, :]
    squares = jnp.sum(terms * terms, axis=(0, 1), keepdims=True) + jnp.sum(
        message_ref[4:5, :], axis=(0, 1), keepdims=True
    )
    grad_norm = jnp.sqrt(squares)
    gn_ref[...] = grad_norm
    factor = jnp.minimum(1.0, CLIP_NORM / (grad_norm + 1e-06))
    for c in range(3):
        wide = lead_ref[:, c * PAIR : (c + 1) * PAIR]
        narrow = lead_ref[:, 3 * PAIR + c * HD : 3 * PAIR + (c + 1) * HD]
        for cols, grad in ((slice(0, PAIR), wide), (slice(PAIR, PAIR + HD), narrow)):
            new, moment, second = adamw(
                qkv_ref[c, :, cols], factor * grad, qkv_m_ref[:, c, :, cols], RATE_LIST[0], DECAY_LIST[0]
            )
            qkv_n_ref[c, :, cols] = new
            qkv_s_ref[0, c, :, cols] = moment
            qkv_s_ref[1, c, :, cols] = second
    part = norm_ref.shape[1]
    per_row = terms.shape[1] // part
    row = message_ref[pl.ds(index_ref[0] // per_row, 1), :]
    mine = pltpu.roll(row, lax.rem(per_row - lax.rem(index_ref[0], per_row), per_row) * part, 1)[:, :part]
    norm_grads = factor * mine
    grads_ref[...] = norm_grads
    plain = (
        (out_ref, rest_ref[:, 2 * units : 2 * units + 3 * HD], out_m_ref, out_n_ref, out_s_ref, 1),
        (up_ref, rest_ref[:, :units], up_m_ref, up_n_ref, up_s_ref, 2),
        (down_ref, rest_ref[:, units : 2 * units], down_m_ref, down_n_ref, down_s_ref, 3),
    )
    for master, grad, moments, next_ref, state_ref, i in plain:
        next_ref[...], state_ref[0], state_ref[1] = adamw(
            master[...], factor * grad, moments[...], RATE_LIST[i], DECAY_LIST[i]
        )
    norm_n_ref[...], norm_s_ref[0:1, :], norm_s_ref[1:2, :] = adamw(
        norm_ref[...], norm_grads, (norm_m_ref[0:1, :], norm_m_ref[1:2, :]), RATE_LIST[4], DECAY_LIST[4]
    )


def small_call(kernel, name, out_shape, *operands, in_spec=IN_VMEM, limit=LIMIT_S):
    return pl.pallas_call(
        kernel,
        in_specs=[IN_SMEM if a.dtype == jnp.int32 else in_spec for a in operands],
        out_specs=jax.tree.map(lambda a: IN_VMEM, out_shape),
        out_shape=out_shape,
        compiler_params=limit,
        cost_estimate=cost(2),
        name=name,
    )(*operands)


def swap(values):
    return lax.ppermute(values, "head", [(0, 1), (1, 0)])


def per_device(
    chips,
    tokens,
    cotangent,
    lengths,
    key_masks,
    qkv_master,
    out_master,
    up_master,
    down_master,
    norm_master,
    qkv_moments,
    out_moments,
    up_moments,
    down_moments,
    norm_moments,
):
    seqs, slot_rows, width = tokens.shape
    shard_rows = qkv_master.shape[0]
    norm_part = norm_master.shape[0]
    units = up_master.shape[1]
    side = lax.axis_index("head")

    qkv_rows = qkv_master.transpose(1, 0, 2)
    masters = (qkv_rows, out_master.T, up_master, down_master.T, norm_master[None])
    shape = jax.ShapeDtypeStruct
    lead = small_call(
        pack_lead_kernel,
        "pack_lead",
        shape((chips, shard_rows, 10 * HD), BF16),
        qkv_rows,
        norm_master[None],
        in_spec=pl.BlockSpec(),
        limit=LIMIT_P,
    )
    rest = small_call(
        pack_rest_kernel, "pack_rest", shape((shard_rows, 2 * units + 4 * HD), BF16), masters[1], *masters[2:4]
    )
    lead_own = lax.all_to_all(lead, "batch", 0, 0)
    place = side.astype(jnp.int32).reshape(1)
    normal, masked, masked_t = prepare(place, lengths, tokens, cotangent)
    members = chips // 2
    far_pairs = [(i, i ^ members) for i in range(chips)]
    teams = [list(range(members)), list(range(members, chips))]
    half = (lax.axis_index("batch") // members).astype(jnp.int32).reshape(1)
    team_shape = shape((members, 2) + rest.shape, BF16)
    rest_pair = small_call(pair_kernel, "pair_rest", team_shape, half, rest, lax.ppermute(rest, "batch", far_pairs))
    lead_own, rest_pair, normal, masked, masked_t = lax.optimization_barrier(
        (lead_own, rest_pair, normal, masked, masked_t)
    )
    rest_own = lax.all_to_all(rest_pair, "batch", 0, 0, axis_index_groups=teams)
    lead_other = swap(lead_own)
    flat = lambda a: a.reshape(chips * shard_rows, a.shape[-1])
    per_seq = lambda a: a.reshape(seqs, slot_rows, width)
    n1t, qkv, attended, linv, probs, wpairs, norms = forward(
        chips, norm_part, place, lengths, per_seq(normal), key_masks, flat(lead_own), flat(lead_other)
    )
    rest_own, attended = lax.optimization_barrier((rest_own, attended))
    rest_other = swap(rest_own)
    block_out, gmid, gatt, grest_own, grest_other, gnorm_two = middle(
        tokens, masked, masked_t, attended, linv, rest_own, rest_other, norms
    )
    rest_sum = small_call(add_split_kernel, "add_rest", team_shape, grest_own, swap(grest_other))
    rest_sum, gatt = lax.optimization_barrier((rest_sum, gatt))
    rest_parts = lax.all_to_all(rest_sum, "batch", 0, 0, axis_index_groups=teams)
    gp, glead_own, glead_other = backward(place, lengths, n1t, qkv, probs, per_seq(gatt), attended)
    lead_sum = small_call(add_kernel, "add_lead", shape(glead_own.shape, BF16), glead_own, swap(glead_other))
    lead_sum, rest_parts = lax.optimization_barrier((lead_sum, rest_parts))
    lead_parts = lax.all_to_all(lead_sum.reshape(chips, shard_rows, 10 * HD), "batch", 0, 0)
    input_grad, terms = input_gradient(tokens, gp, per_seq(gmid), wpairs, norms, gnorm_two)
    rest_mine, rest_theirs = small_call(
        sum_rest_kernel, "sum_rest", [shape(rest.shape, F32), shape(rest.shape, BF16)], half, rest_parts
    )
    rest_far = lax.ppermute(rest_theirs, "batch", far_pairs)
    lead_shard, rest_shard, message = small_call(
        sum_lead_kernel,
        "sum_lead",
        [shape(lead.shape[1:], F32), shape(rest.shape, F32), shape(terms.shape, F32)],
        lead_parts,
        rest_mine,
        rest_far,
        terms,
    )
    message = message + swap(message)
    stride = 1
    while stride < chips:
        message = message + lax.ppermute(message, "batch", [(i, i ^ stride) for i in range(chips)])
        stride *= 2
    like = lambda a: shape(a.shape, F32)
    moments = (
        qkv_moments.transpose(0, 2, 1, 3),
        out_moments.transpose(0, 2, 1),
        up_moments,
        down_moments.transpose(0, 2, 1),
        norm_moments,
    )
    results = small_call(
        update_kernel,
        "update_weights",
        [shape((1, 1), F32)] + [like(a) for a in masters + moments] + [shape((1, norm_part), F32)],
        (lax.axis_index("batch") * 2 + side).astype(jnp.int32).reshape(1),
        message,
        lead_shard,
        rest_shard,
        *masters,
        *moments,
    )
    grad_norm, qkv_next, out_next, up_next, down_next, norm_next = results[:6]
    qkv_states, out_states, up_states, down_states, norm_states, norm_grads = results[6:]
    return (
        per_seq(block_out),
        input_grad,
        grad_norm.reshape(()),
        qkv_next.transpose(1, 0, 2),
        out_next.T,
        up_next,
        down_next.T,
        norm_next[0],
        qkv_states.transpose(0, 2, 1, 3),
        out_states.transpose(0, 2, 1),
        up_states,
        down_states.transpose(0, 2, 1),
        norm_states,
        norm_grads[0],
    )


def solution(mesh):
    chips = mesh.shape["batch"]
    return jax.shard_map(
        functools.partial(per_device, chips),
        mesh=mesh,
        in_specs=(
            P(("batch", "head"), None, None),
            P(("batch", "head"), None, None),
            P("batch"),
            P("batch", None),
            P("batch", None, "head"),
            P("head", "batch"),
            P("batch", "head"),
            P("head", "batch"),
            P(("batch", "head")),
            P(None, "batch", None, "head"),
            P(None, "head", "batch"),
            P(None, "batch", "head"),
            P(None, "head", "batch"),
            P(None, ("batch", "head")),
        ),
        out_specs=(
            P(("batch", "head"), None, None),
            P(("batch", "head"), None, None),
            P(),
            P("batch", None, "head"),
            P("head", "batch"),
            P("batch", "head"),
            P("head", "batch"),
            P(("batch", "head")),
            P(None, "batch", None, "head"),
            P(None, "head", "batch"),
            P(None, "batch", "head"),
            P(None, "head", "batch"),
            P(None, ("batch", "head")),
            P(("batch", "head")),
        ),
        check_vma=False,
    )
```

```python
import functools

import jax
import jax.numpy as jnp
from jax import lax
from jax.experimental import pallas as pl
from jax.experimental.pallas import tpu as pltpu
from jax.sharding import PartitionSpec as P

HD = 64
STEP = 10
NORM_EPS = 1e-06
CLIP_NORM = 1000.0
BETA_ONE = 0.5
BETA_TWO = 0.5
ADAM_EPS = 1e-08
RATE_LIST = (0.06, 0.25, 0.06, 0.03, 0.5)
DECAY_LIST = (0.04, 0.04, 0.04, 0.04, 0.0)

F32 = jnp.float32
BF16 = jnp.bfloat16
NN = (((1,), (0,)), ((), ()))
NT = (((1,), (1,)), ((), ()))
TN = (((0,), (0,)), ((), ()))
QB = 320
DB = 640
FB = 512
FC = 256
PAIR = 2 * HD
LIMIT_A, LIMIT_B, LIMIT_C, LIMIT_D, LIMIT_S, LIMIT_P = (
    pltpu.CompilerParams(vmem_limit_bytes=m * 2**20) for m in (52, 46, 52, 52, 16, 62)
)
IN_VMEM = pl.BlockSpec(memory_space=pltpu.VMEM)
IN_SMEM = pl.BlockSpec(memory_space=pltpu.SMEM)


def cost(microseconds):
    return pl.CostEstimate(flops=microseconds * 1_000_000_000, bytes_accessed=1_000_000, transcendentals=0)


def mm(left, right, dims=NN):
    return lax.dot_general(left, right, dims, preferred_element_type=F32)


def normalize(values):
    centred = values - jnp.mean(values, axis=-1, keepdims=True)
    variance = jnp.mean(centred * centred, axis=-1, keepdims=True)
    rs = lax.rsqrt(variance + NORM_EPS)
    return centred * rs, rs


def norm_backward(normal, rs, gained):
    inner = jnp.mean(gained * normal, axis=-1, keepdims=True)
    return rs * (gained - jnp.mean(gained, axis=-1, keepdims=True) - normal * inner)


def gelu_both(h, gradient):
    cdf = 0.5 + 0.5 * lax.erf(h * 0.7071067811865476)
    density = jnp.exp(h * h * -0.5) * 0.3989422804014327
    return (h * cdf).astype(BF16), (gradient * (cdf + h * density)).astype(BF16)


def split_pairs(own, other, per_pair):
    wide, narrow = 2 * per_pair, per_pair
    singles = []
    for part in range(per_pair // HD):
        cols = slice(wide + part * HD, wide + (part + 1) * HD)
        singles += [own[:, cols], other[:, cols]]
    return own[:, :wide], jnp.concatenate(singles, axis=1), other[:, :wide]


def join_pairs(first, second, third, per_pair):
    parts = [
        [second[:, p * PAIR + side * HD : p * PAIR + (side + 1) * HD] for p in range(per_pair // HD)]
        for side in range(2)
    ]
    return [first] + parts[0], [third] + parts[1]


def in_order(out_ref, own_ref, other_ref):
    members, sides, part, _ = own_ref.shape
    for head, ref in enumerate((own_ref, other_ref)):
        for place in range(members * sides):
            out_ref[head, place * part : (place + 1) * part, :] = ref[place % members, place // members]


def gathered_norms(first, second, chips, part, width):
    shard_rows = first.shape[0] // chips
    cols = slice(9 * HD, 9 * HD + part)
    pieces = []
    for chip in range(chips):
        row = chip * shard_rows
        for values in (first, second):
            pieces.append(values[row : row + 1, cols] + values[row + 1 : row + 2, cols])
    per_row = width // part
    return [jnp.concatenate(pieces[i * per_row : (i + 1) * per_row], axis=1) for i in range(4)]


def prepare_kernel(seq_rows, side_ref, len_ref, tok_ref, cot_ref, normal_ref, masked_ref, masked_t_ref):
    step = pl.program_id(0)
    rows = tok_ref.shape[0]
    first = step * rows
    row = first + lax.broadcasted_iota(jnp.int32, (rows, 1), 0)
    live = row < 0
    seqs = rows * pl.num_programs(0) // seq_rows
    for near in range(-(-rows // seq_rows) + 1):
        s = first // seq_rows + near
        bound = jnp.where(s < seqs, len_ref[side_ref[0] * seqs + jnp.minimum(s, seqs - 1)], 0)
        live = live | ((row >= s * seq_rows) & (row < s * seq_rows + bound))

    normal_ref[...], _ = normalize(tok_ref[...].astype(F32))
    masked = jnp.where(live, cot_ref[...].astype(F32), 0.0).astype(BF16)
    masked_ref[...] = masked
    masked_t_ref[...] = masked.T


def prepare(side, lengths, tokens, cotangent):
    seqs, seq_rows, width = tokens.shape
    total = seqs * seq_rows
    flat = lambda a: a.reshape(total, width)
    rowspec = pl.BlockSpec((FB, width), lambda s: (s, 0))
    shape = jax.ShapeDtypeStruct
    return pl.pallas_call(
        functools.partial(prepare_kernel, seq_rows),
        grid=(total // FB,),
        in_specs=[IN_SMEM, IN_SMEM, rowspec, rowspec],
        out_specs=[rowspec, rowspec, pl.BlockSpec((width, FB), lambda s: (0, s))],
        out_shape=[shape((total, width), F32), shape((total, width), BF16), shape((width, total), BF16)],
        compiler_params=LIMIT_P,
        cost_estimate=cost(5),
        name="prepare",
    )(side, lengths, flat(tokens), flat(cotangent))


def key_limits(rows):
    return [*range(256, rows, 256), rows]


def forward_kernel(
    chips, part, side_ref, len_ref, normal_ref, mask_ref, own_ref, other_ref,
    n1t_ref, qkv_ref, att_ref, linv_ref, p_ref, w_ref, norms_ref, lead_ref,
):
    rows, width = normal_ref.shape
    pairs = width // PAIR
    side, seq = side_ref[0], pl.program_id(0)

    @pl.when(seq == 0)
    def _():
        in_order(lead_ref, own_ref, other_ref)
        own, other = lead_ref[0], lead_ref[1]
        for i, weights in enumerate(split_pairs(own[:, : 9 * HD], other[:, : 9 * HD], 3 * HD)):
            w_ref[:, i * 3 * PAIR : (i + 1) * 3 * PAIR] = weights
        tail = slice(8 * HD, 10 * HD)
        mine, theirs = own[:, tail].astype(F32), other[:, tail].astype(F32)
        pad = jnp.zeros((own.shape[0], 8 * HD), F32)
        first = jnp.concatenate([pad, jnp.where(side == 0, mine, theirs)], axis=1)
        second = jnp.concatenate([pad, jnp.where(side == 0, theirs, mine)], axis=1)
        for i, row in enumerate(gathered_norms(first, second, chips, part, width)):
            norms_ref[i : i + 1, :] = row

    member = side * pl.num_programs(0) + seq
    position = lax.broadcasted_iota(jnp.int32, (1, rows), 1)
    mask = mask_ref[pl.ds(member, 1), :]
    visible = (position < len_ref[member]) & ((mask == 1) | (position == 0))
    hidden = jnp.where(visible, 0.0, -1e30)
    hidden = jnp.broadcast_to(hidden, (PAIR, rows)).T.astype(BF16)

    low = 0
    for keys in key_limits(rows):
        pl.when((len_ref[member] > low) & (len_ref[member] <= keys))(
            functools.partial(
                attend, keys, hidden, normal_ref, norms_ref, w_ref, n1t_ref, qkv_ref, att_ref, linv_ref, p_ref
            )
        )
        low = keys


def attend(count, hidden, normal_ref, norms_ref, w_ref, n1t_ref, qkv_ref, att_ref, linv_ref, p_ref):
    rows, width = normal_ref.shape
    pairs = width // PAIR
    n1 = (normal_ref[...] * norms_ref[0:1, :] + norms_ref[1:2, :]).astype(BF16)
    n1t_ref[...] = n1.T
    lane = lax.broadcasted_iota(jnp.int32, (QB, PAIR), 1)
    key_lane = lax.broadcasted_iota(jnp.int32, (count, PAIR), 1)
    ones = jnp.ones((count, PAIR), BF16)
    hidden = hidden[:count]
    ready = {}
    projected = mm(n1, w_ref[...])

    def project(pair):
        out = projected[:, pair * 3 * PAIR : (pair + 1) * 3 * PAIR]
        queries = (out[:, :PAIR].astype(BF16).astype(F32) * (HD**-0.5)).astype(BF16)
        others = out[:, PAIR:].astype(BF16)
        qkv_ref[pair, :, :PAIR] = queries
        qkv_ref[pair, :, PAIR:] = others
        keys = [jnp.where(key_lane == HD * (1 - half), hidden, others[:count, :PAIR]) for half in range(2)]
        return queries, keys, jnp.concatenate([others[:count, PAIR:], ones], axis=1)

    def scores(pair, block, half):
        if pair not in ready:
            ready[pair] = project(pair)
        queries, keys, _ = ready[pair]
        spot = jnp.where(lane == HD * (1 - half), 1.0, 0.0).astype(BF16)
        part_queries = jnp.where((lane < HD) == (half == 0), queries[block * QB : (block + 1) * QB], spot)
        return mm(part_queries, keys[half], NT)

    outs = {}

    def finish(pair, block, half, s):
        sl = slice(block * QB, (block + 1) * QB)
        p = jnp.exp(s - jnp.max(s, axis=-1, keepdims=True)).astype(BF16)
        p_ref[pair * 2 + half, sl, :count] = p
        out = mm(p, ready[pair][2])
        inverse = 1.0 / out[:, PAIR:]
        outs[half] = (out[:, :PAIR] * inverse, inverse)
        if half == 1:
            cols = slice(pair * PAIR, (pair + 1) * PAIR)
            att_ref[sl, cols] = jnp.where(lane < HD, outs[0][0], outs[1][0]).astype(BF16)
            linv_ref[sl, cols] = jnp.where(lane < HD, outs[0][1], outs[1][1])

    pending = None
    for pair in range(pairs):
        for block in range(rows // QB):
            for half in range(2):
                fresh = (pair, block, half, scores(pair, block, half))
                if pending is not None:
                    finish(*pending)
                pending = fresh
    finish(*pending)


def forward(chips, part, side, lengths, normal, key_masks, own, other):
    seqs, rows, width = normal.shape
    heads, pairs = width // HD, width // PAIR
    sq = pl.squeezed
    shape = jax.ShapeDtypeStruct
    whole = lambda *dims: pl.BlockSpec(dims, lambda s: (0,) * len(dims))
    row_spec = pl.BlockSpec((sq, rows, width), lambda s: (s, 0, 0))
    return pl.pallas_call(
        functools.partial(forward_kernel, chips, part),
        grid=(seqs,),
        in_specs=[IN_SMEM, IN_SMEM, row_spec, IN_VMEM, IN_VMEM, IN_VMEM],
        out_specs=[
            pl.BlockSpec((sq, width, rows), lambda s: (s, 0, 0)),
            pl.BlockSpec((sq, pairs, rows, 3 * PAIR), lambda s: (s, 0, 0, 0)),
            row_spec,
            row_spec,
            pl.BlockSpec((sq, heads, rows, rows), lambda s: (s, 0, 0, 0)),
            IN_VMEM,
            IN_VMEM,
        ],
        out_shape=[
            shape((seqs, width, rows), BF16),
            shape((seqs, pairs, rows, 3 * PAIR), BF16),
            shape((seqs, rows, width), BF16),
            shape((seqs, rows, width), F32),
            shape((seqs, heads, rows, rows), BF16),
            shape((width, 3 * width), BF16),
            shape((4, width), F32),
        ],
        scratch_shapes=[pltpu.VMEM((2, width, own.shape[-1]), BF16)],
        compiler_params=LIMIT_A,
        cost_estimate=cost(24),
        name="attention_forward",
    )(side, lengths, normal, key_masks, own, other)


def middle_kernel(
    units, tok_ref, gb_ref, gbt_ref, att_ref, linv_ref, own_ref, other_ref, norms_ref,
    mid_ref, act_ref, gmid_ref, gatt_ref, gown_ref, gother_ref, gnorm_ref, halves,
    wo_ref, gout_ref, gup_ref, gdown_ref,
):
    step = pl.program_id(0)
    rows, width = tok_ref.shape

    @pl.when(step == 0)
    def _():
        gout_ref[...] = jnp.zeros_like(gout_ref)
        gup_ref[...] = jnp.zeros_like(gup_ref)
        gdown_ref[...] = jnp.zeros_like(gdown_ref)
        gnorm_ref[...] = jnp.zeros_like(gnorm_ref)
        in_order(halves, own_ref, other_ref)
        cols = slice(2 * units, 2 * units + 3 * HD)
        parts = split_pairs(halves[0, :, cols], halves[1, :, cols], HD)
        for i, part in enumerate(parts):
            wo_ref[:, i * PAIR : (i + 1) * PAIR] = part

    x = tok_ref[...].astype(F32)
    att = att_ref[...]
    mid = x + mm(att, wo_ref[...], NT)
    normal, rs = normalize(mid)
    gain, shift = norms_ref[2:3, :], norms_ref[3:4, :]
    n2 = (normal * gain + shift).astype(BF16)
    n2t = n2.T
    gb, gbt = gb_ref[...], gbt_ref[...]
    mid_ref[...] = mid
    sums = [jnp.zeros_like(mid)]

    def begin(half, c):
        wu = halves[half, :, c * FC : (c + 1) * FC]
        wd = halves[half, :, units + c * FC : units + (c + 1) * FC]
        return half, c, wu, wd, mm(n2, wu), mm(gb, wd)

    def finish(half, c, wu, wd, h, ga):
        cols = slice(c * FC, (c + 1) * FC)
        act, gh = gelu_both(h, ga)
        act_ref[half, :, cols] = act
        sums[0] = sums[0] + mm(gh, wu, NT)
        gup_ref[half, :, cols] += mm(n2t, gh)
        gdown_ref[half, :, cols] += mm(gbt, act)

    pending = None
    for half in range(2):
        for c in range(units // FC):
            fresh = begin(half, c)
            if pending is not None:
                finish(*pending)
            pending = fresh
    finish(*pending)
    gtwo = sums[0]
    gnorm_ref[0:8, :] += jnp.sum((gtwo * normal).reshape(rows // 8, 8, width), axis=0)
    gnorm_ref[8:16, :] += jnp.sum(gtwo.reshape(rows // 8, 8, width), axis=0)
    gmid = gb.astype(F32) + norm_backward(normal, rs, gtwo * gain)
    gmid_ref[...] = gmid
    gm = gmid.astype(BF16)
    gout_ref[...] += mm(gm, att, TN)
    gatt_ref[...] = (mm(gm, wo_ref[...]) * linv_ref[...]).astype(BF16)

    @pl.when(step == pl.num_programs(0) - 1)
    def _():
        total = gout_ref[...]
        sides = join_pairs(
            total[:, :PAIR], total[:, PAIR : 2 * PAIR], total[:, 2 * PAIR :], HD
        )
        for half, ref in enumerate((gown_ref, gother_ref)):
            ref[:, :units] = gup_ref[half].astype(BF16)
            ref[:, units : 2 * units] = gdown_ref[half].astype(BF16)
            blank = jnp.zeros((total.shape[0], HD), F32)
            ref[:, 2 * units :] = jnp.concatenate(sides[half] + [blank], axis=1).astype(BF16)


def middle(tokens, masked, masked_t, attended, linv, own, other, norms):
    seqs, seq_rows, width = tokens.shape
    total = seqs * seq_rows
    packed = own.shape[-1]
    units = (packed - 4 * HD) // 2
    flat = lambda a: a.reshape(total, width)
    rowspec = pl.BlockSpec((FB, width), lambda s: (s, 0))
    whole = lambda *dims: pl.BlockSpec(dims, lambda s: (0,) * len(dims))
    shape = jax.ShapeDtypeStruct
    return pl.pallas_call(
        functools.partial(middle_kernel, units),
        grid=(total // FB,),
        in_specs=[
            rowspec,
            rowspec,
            pl.BlockSpec((width, FB), lambda s: (0, s)),
            rowspec,
            rowspec,
            IN_VMEM,
            IN_VMEM,
            IN_VMEM,
        ],
        out_specs=[
            rowspec,
            pl.BlockSpec((2, FB, units), lambda s: (0, s, 0)),
            rowspec,
            rowspec,
            IN_VMEM,
            IN_VMEM,
            whole(16, width),
            IN_VMEM,
        ],
        out_shape=[
            shape((total, width), F32),
            shape((2, total, units), BF16),
            shape((total, width), F32),
            shape((total, width), BF16),
            shape((width, packed), BF16),
            shape((width, packed), BF16),
            shape((16, width), F32),
            shape((2, width, packed), BF16),
        ],
        scratch_shapes=[
            pltpu.VMEM((width, width), BF16),
            pltpu.VMEM((width, width), F32),
            pltpu.VMEM((2, width, units), F32),
            pltpu.VMEM((2, width, units), F32),
        ],
        compiler_params=LIMIT_B,
        cost_estimate=cost(36),
        name="feed_forward",
    )(flat(tokens), masked, masked_t, flat(attended), flat(linv), own, other, norms)


def backward_kernel(
    side_ref, len_ref, n1t_ref, qkv_ref, p_ref, gatt_ref, att_ref, gp_ref, gown_ref, gother_ref, gqkv_ref
):
    seq = pl.program_id(0)
    rows = qkv_ref.shape[1]

    @pl.when(seq == 0)
    def _():
        gqkv_ref[...] = jnp.zeros_like(gqkv_ref)

    length = len_ref[side_ref[0] * pl.num_programs(0) + seq]
    low = 0
    for count in key_limits(rows):
        pl.when((length > low) & (length <= count))(
            functools.partial(attend_backward, count, n1t_ref, qkv_ref, p_ref, gatt_ref, att_ref, gp_ref, gqkv_ref)
        )
        low = count

    @pl.when(seq == pl.num_programs(0) - 1)
    def _():
        group = 3 * PAIR
        thirds = [gqkv_ref[:, i * group : (i + 1) * group] for i in range(3)]
        sides = join_pairs(*thirds, 3 * HD)
        blank = jnp.zeros((gqkv_ref.shape[0], HD), F32)
        for columns, ref in zip(sides, (gown_ref, gother_ref)):
            ref[...] = jnp.concatenate(columns + [blank], axis=1).astype(BF16)


def attend_backward(count, n1t_ref, qkv_ref, p_ref, gatt_ref, att_ref, gp_ref, gqkv_ref):
    pairs, rows = qkv_ref.shape[:2]
    lane = lax.broadcasted_iota(jnp.int32, (count, PAIR), 1)
    zero = jnp.zeros((count, PAIR), BF16)
    state = {}

    def begin(pair, half):
        if half == 0:
            cols = slice(pair * PAIR, (pair + 1) * PAIR)
            ga = gatt_ref[:count, cols]
            state[pair] = dict(
                ga=ga,
                inner=ga.astype(F32) * att_ref[:count, cols].astype(F32),
                gat=ga.T,
                qt=qkv_ref[pair, :count, :PAIR].T,
                gq=[],
                gkt=[],
                gvt=[],
            )
        mask = (lane < HD) == (half == 0)
        values = qkv_ref[pair, :count, 2 * PAIR :]
        return pair, half, mask, mm(jnp.where(mask, state[pair]["ga"], zero), values, NT)

    def finish(pair, half, mask, dp):
        mine = state[pair]
        hs = slice(half * HD, half * HD + HD)
        p = p_ref[pair * 2 + half, :count, :count]
        mine["gvt"].append(mm(mine["gat"][hs], p))
        inner = jnp.sum(jnp.where(mask, mine["inner"], 0.0), axis=-1, keepdims=True)
        ds = (p.astype(F32) * (dp - inner)).astype(BF16)
        mine["gq"].append(mm(ds, qkv_ref[pair, :count, PAIR : 2 * PAIR]))
        mine["gkt"].append(mm(mine["qt"][hs], ds))
        if half == 1:
            joined = jnp.where(lane < HD, mine["gq"][0], mine["gq"][1])
            columns = (
                (joined * (HD**-0.5)).astype(BF16),
                jnp.concatenate(mine["gkt"], axis=0).astype(BF16).T,
                jnp.concatenate(mine["gvt"], axis=0).astype(BF16).T,
            )
            for i, values in enumerate(columns):
                start = (3 * pair + i) * PAIR
                gp_ref[:count, start : start + PAIR] = values

    pending = None
    for pair in range(pairs):
        for half in range(2):
            fresh = begin(pair, half)
            if pending is not None:
                finish(*pending)
            pending = fresh
    finish(*pending)
    gqkv_ref[...] += mm(n1t_ref[:, :count], gp_ref[:count, :])
    if count < rows:
        gp_ref[count:, :] = jnp.zeros((rows - count, gp_ref.shape[1]), BF16)


def backward(side, lengths, n1t, qkv, probs, gatt, attended):
    seqs, rows, width = attended.shape
    pairs = width // PAIR
    sq = pl.squeezed
    rowspec = pl.BlockSpec((sq, rows, width), lambda s: (s, 0, 0))
    groupspec = pl.BlockSpec((sq, pairs, rows, 3 * PAIR), lambda s: (s, 0, 0, 0))
    shape = jax.ShapeDtypeStruct
    packed = (width, 10 * HD)
    return pl.pallas_call(
        backward_kernel,
        grid=(seqs,),
        in_specs=[
            IN_SMEM,
            IN_SMEM,
            pl.BlockSpec((sq, width, rows), lambda s: (s, 0, 0)),
            groupspec,
            pl.BlockSpec((sq, 2 * pairs, rows, rows), lambda s: (s, 0, 0, 0)),
            rowspec,
            rowspec,
        ],
        out_specs=[pl.BlockSpec((sq, rows, 3 * width), lambda s: (s, 0, 0)), IN_VMEM, IN_VMEM],
        out_shape=[shape((seqs, rows, 3 * width), BF16), shape(packed, BF16), shape(packed, BF16)],
        scratch_shapes=[pltpu.VMEM((width, 3 * width), F32)],
        compiler_params=LIMIT_C,
        cost_estimate=cost(27),
        name="attention_backward",
    )(side, lengths, n1t, qkv, probs, gatt, attended)


def input_kernel(
    tok_ref, gp_ref, gmid_ref, w_ref, norms_ref, two_ref, mid_ref, act_ref, weights_ref,
    gin_ref, terms_ref, out_ref,
):
    rows, width = tok_ref.shape
    units = act_ref.shape[2]
    gone = mm(gp_ref[...], w_ref[...], NT)
    normal, rs = normalize(tok_ref[...].astype(F32))

    @pl.when((pl.program_id(0) == 0) & (pl.program_id(1) == 0))
    def _():
        terms_ref[...] = jnp.zeros_like(terms_ref)
        terms_ref[2:3, :] = jnp.sum(two_ref[0:8, :], axis=0, keepdims=True)
        terms_ref[3:4, :] = jnp.sum(two_ref[8:16, :], axis=0, keepdims=True)

    terms_ref[0:1, :] += jnp.sum(gone * normal, axis=0, keepdims=True)
    terms_ref[1:2, :] += jnp.sum(gone, axis=0, keepdims=True)
    gin_ref[...] = gmid_ref[...] + norm_backward(normal, rs, gone * norms_ref[0:1, :])
    out = mid_ref[...]
    for half in range(2):
        out = out + mm(act_ref[half], weights_ref[half, :, units : 2 * units], NT)
    out_ref[...] = out.astype(BF16)


def input_gradient(tokens, gp, gmid, wpairs, norms, gnorm_two, mid, act, weights):
    seqs, rows, width = tokens.shape
    units = act.shape[2]
    sq = pl.squeezed
    full = pl.BlockSpec((sq, DB, width), lambda s, r: (s, r, 0))
    shape = jax.ShapeDtypeStruct
    return pl.pallas_call(
        input_kernel,
        grid=(seqs, rows // DB),
        in_specs=[
            full,
            pl.BlockSpec((sq, DB, 3 * width), lambda s, r: (s, r, 0)),
            full,
            IN_VMEM,
            IN_VMEM,
            IN_VMEM,
            full,
            pl.BlockSpec((2, DB, units), lambda s, r: (0, s * (rows // DB) + r, 0)),
            IN_VMEM,
        ],
        out_specs=[full, IN_VMEM, full],
        out_shape=[
            shape((seqs, rows, width), F32),
            shape((8, width), F32),
            shape((seqs, rows, width), BF16),
        ],
        compiler_params=LIMIT_D,
        cost_estimate=cost(13),
        name="input_gradient",
    )(tokens, gp, gmid, wpairs, norms, gnorm_two, mid, act, weights)


def pack_kernel(qkv_ref, out_ref, up_ref, down_ref, norm_ref, lead_ref, rest_ref):
    rows = lead_ref.shape[0]
    part = norm_ref.shape[1]
    norm = norm_ref[...]
    high = norm.astype(BF16).astype(F32)
    row = lax.broadcasted_iota(jnp.int32, (rows, part), 0)
    extra = jnp.where(row == 0, high, jnp.where(row == 1, norm - high, 0.0))
    columns = [qkv_ref[c, :, :PAIR] for c in range(3)] + [qkv_ref[c, :, PAIR:] for c in range(3)]
    blank = jnp.zeros((rows, HD - part), F32)
    lead_ref[...] = jnp.concatenate(columns + [extra, blank], axis=1).astype(BF16)
    blank = jnp.zeros((rows, HD), F32)
    rest_ref[...] = jnp.concatenate([up_ref[...], down_ref[...], out_ref[...], blank], axis=1).astype(BF16)


def pair_kernel(half_ref, own_ref, far_ref, out_ref):
    own, far = own_ref[...], far_ref[...]
    first = half_ref[0] == 0
    for slot, value in enumerate((jnp.where(first, own, far), jnp.where(first, far, own))):
        for member in range(out_ref.shape[0]):
            out_ref[member, slot] = value


def add_kernel(left_ref, right_ref, out_ref):
    out_ref[...] = (left_ref[...].astype(F32) + right_ref[...].astype(F32)).astype(BF16)


def add_split_kernel(left_ref, right_ref, out_ref):
    total = (left_ref[...].astype(F32) + right_ref[...].astype(F32)).astype(BF16)
    members, halves, rows, _ = out_ref.shape
    for half in range(halves):
        for member in range(members):
            start = (half * members + member) * rows
            out_ref[member, half] = total[start : start + rows]


def sum_parts(parts_ref, out_ref):
    total = jnp.zeros((out_ref.shape[0], PAIR), F32)
    for start in range(0, out_ref.shape[1], PAIR):
        cols = slice(start, start + PAIR)
        piece = jnp.sum(parts_ref[:, :, cols].astype(F32), axis=0)
        out_ref[:, cols] = piece
        total = total + piece * piece
    return jnp.sum(total, axis=0, keepdims=True)


def sum_rest_kernel(half_ref, parts_ref, mine_ref, theirs_ref):
    first = half_ref[0] == 0
    for start in range(0, mine_ref.shape[1], PAIR):
        cols = slice(start, start + PAIR)
        low = jnp.sum(parts_ref[:, 0, :, cols].astype(F32), axis=0)
        high = jnp.sum(parts_ref[:, 1, :, cols].astype(F32), axis=0)
        mine_ref[:, cols] = jnp.where(first, low, high)
        theirs_ref[:, cols] = jnp.where(first, high, low).astype(BF16)


def sum_lead_kernel(parts_ref, mine_ref, far_ref, terms_ref, out_ref, rest_ref, message_ref):
    squares = sum_parts(parts_ref, out_ref)
    rest = mine_ref[...] + far_ref[...].astype(F32)
    rest_ref[...] = rest
    total = jnp.zeros((rest.shape[0], PAIR), F32)
    for start in range(0, rest.shape[1], PAIR):
        piece = rest[:, start : start + PAIR]
        total = total + piece * piece
    message_ref[...] = terms_ref[...]
    message_ref[4:5, :PAIR] = squares + jnp.sum(total, axis=0, keepdims=True)


def adamw(master, gradient, moments, rate, decay):
    moment = BETA_ONE * moments[0] + (1.0 - BETA_ONE) * gradient
    second = BETA_TWO * moments[1] + (1.0 - BETA_TWO) * gradient * gradient
    step_size = (
        moment / (1.0 - BETA_ONE**STEP) / (jnp.sqrt(second / (1.0 - BETA_TWO**STEP)) + ADAM_EPS)
    )
    return master - rate * (step_size + decay * master), moment, second


def update_kernel(
    index_ref, message_ref, lead_ref, rest_ref,
    qkv_ref, out_ref, up_ref, down_ref, norm_ref,
    qkv_m_ref, out_m_ref, up_m_ref, down_m_ref, norm_m_ref,
    gn_ref, qkv_n_ref, out_n_ref, up_n_ref, down_n_ref, norm_n_ref,
    qkv_s_ref, out_s_ref, up_s_ref, down_s_ref, norm_s_ref, grads_ref,
):
    units = up_ref.shape[1]
    terms = message_ref[0:4, :]
    squares = jnp.sum(terms * terms, axis=(0, 1), keepdims=True) + jnp.sum(
        message_ref[4:5, :], axis=(0, 1), keepdims=True
    )
    grad_norm = jnp.sqrt(squares)
    gn_ref[...] = grad_norm
    factor = jnp.minimum(1.0, CLIP_NORM / (grad_norm + 1e-06))
    for c in range(3):
        wide = lead_ref[:, c * PAIR : (c + 1) * PAIR]
        narrow = lead_ref[:, 3 * PAIR + c * HD : 3 * PAIR + (c + 1) * HD]
        for cols, grad in ((slice(0, PAIR), wide), (slice(PAIR, PAIR + HD), narrow)):
            new, moment, second = adamw(
                qkv_ref[c, :, cols], factor * grad, qkv_m_ref[:, c, :, cols], RATE_LIST[0], DECAY_LIST[0]
            )
            qkv_n_ref[c, :, cols] = new
            qkv_s_ref[0, c, :, cols] = moment
            qkv_s_ref[1, c, :, cols] = second
    part = norm_ref.shape[1]
    per_row = terms.shape[1] // part
    row = message_ref[pl.ds(index_ref[0] // per_row, 1), :]
    mine = pltpu.roll(row, lax.rem(per_row - lax.rem(index_ref[0], per_row), per_row) * part, 1)[:, :part]
    norm_grads = factor * mine
    grads_ref[...] = norm_grads
    plain = (
        (out_ref, rest_ref[:, 2 * units : 2 * units + 3 * HD], out_m_ref, out_n_ref, out_s_ref, 1),
        (up_ref, rest_ref[:, :units], up_m_ref, up_n_ref, up_s_ref, 2),
        (down_ref, rest_ref[:, units : 2 * units], down_m_ref, down_n_ref, down_s_ref, 3),
    )
    for master, grad, moments, next_ref, state_ref, i in plain:
        next_ref[...], state_ref[0], state_ref[1] = adamw(
            master[...], factor * grad, moments[...], RATE_LIST[i], DECAY_LIST[i]
        )
    norm_n_ref[...], norm_s_ref[0:1, :], norm_s_ref[1:2, :] = adamw(
        norm_ref[...], norm_grads, (norm_m_ref[0:1, :], norm_m_ref[1:2, :]), RATE_LIST[4], DECAY_LIST[4]
    )


def small_call(kernel, name, out_shape, *operands, in_spec=IN_VMEM, limit=LIMIT_S):
    return pl.pallas_call(
        kernel,
        in_specs=[IN_SMEM if a.dtype == jnp.int32 else in_spec for a in operands],
        out_specs=jax.tree.map(lambda a: IN_VMEM, out_shape),
        out_shape=out_shape,
        compiler_params=limit,
        cost_estimate=cost(2),
        name=name,
    )(*operands)


def swap(values):
    return lax.ppermute(values, "head", [(0, 1), (1, 0)])


def per_device(
    chips,
    tokens,
    cotangent,
    lengths,
    key_masks,
    qkv_master,
    out_master,
    up_master,
    down_master,
    norm_master,
    qkv_moments,
    out_moments,
    up_moments,
    down_moments,
    norm_moments,
):
    seqs, slot_rows, width = tokens.shape
    shard_rows = qkv_master.shape[0]
    norm_part = norm_master.shape[0]
    units = up_master.shape[1]
    side = lax.axis_index("head")

    qkv_rows = qkv_master.transpose(1, 0, 2)
    masters = (qkv_rows, out_master.T, up_master, down_master.T, norm_master[None])
    shape = jax.ShapeDtypeStruct
    lead, rest = small_call(
        pack_kernel,
        "pack_weights",
        [shape((shard_rows, 10 * HD), BF16), shape((shard_rows, 2 * units + 4 * HD), BF16)],
        *masters,
        in_spec=pl.BlockSpec(),
        limit=LIMIT_P,
    )
    members = chips // 2
    far_pairs = [(i, i ^ members) for i in range(chips)]
    teams = [list(range(members)), list(range(members, chips))]
    half = (lax.axis_index("batch") // members).astype(jnp.int32).reshape(1)
    lead_far = lax.ppermute(lead, "batch", far_pairs)
    rest_far = lax.ppermute(rest, "batch", far_pairs)
    team_of = lambda a: shape((members, 2) + a.shape, BF16)
    lead_pair = small_call(pair_kernel, "pair_lead", team_of(lead), half, lead, lead_far)
    lead_own = lax.all_to_all(lead_pair, "batch", 0, 0, axis_index_groups=teams)
    place = side.astype(jnp.int32).reshape(1)
    normal, masked, masked_t = prepare(place, lengths, tokens, cotangent)
    rest_pair = small_call(pair_kernel, "pair_rest", team_of(rest), half, rest, rest_far)
    lead_own, rest_pair, normal, masked, masked_t = lax.optimization_barrier(
        (lead_own, rest_pair, normal, masked, masked_t)
    )
    rest_own = lax.all_to_all(rest_pair, "batch", 0, 0, axis_index_groups=teams)
    lead_other = swap(lead_own)
    per_seq = lambda a: a.reshape(seqs, slot_rows, width)
    n1t, qkv, attended, linv, probs, wpairs, norms = forward(
        chips, norm_part, place, lengths, per_seq(normal), key_masks, lead_own, lead_other
    )
    rest_own, attended = lax.optimization_barrier((rest_own, attended))
    rest_other = swap(rest_own)
    mid, act, gmid, gatt, grest_own, grest_other, gnorm_two, weights = middle(
        tokens, masked, masked_t, attended, linv, rest_own, rest_other, norms
    )
    rest_sum = small_call(add_split_kernel, "add_rest", team_of(rest), grest_own, swap(grest_other))
    rest_sum, gatt = lax.optimization_barrier((rest_sum, gatt))
    rest_parts = lax.all_to_all(rest_sum, "batch", 0, 0, axis_index_groups=teams)
    gp, glead_own, glead_other = backward(place, lengths, n1t, qkv, probs, per_seq(gatt), attended)
    lead_sum = small_call(add_kernel, "add_lead", shape(glead_own.shape, BF16), glead_own, swap(glead_other))
    lead_sum, rest_parts = lax.optimization_barrier((lead_sum, rest_parts))
    lead_parts = lax.all_to_all(lead_sum.reshape(chips, shard_rows, 10 * HD), "batch", 0, 0)
    input_grad, terms, block_out = input_gradient(
        tokens, gp, per_seq(gmid), wpairs, norms, gnorm_two, per_seq(mid), act, weights
    )
    rest_mine, rest_theirs = small_call(
        sum_rest_kernel, "sum_rest", [shape(rest.shape, F32), shape(rest.shape, BF16)], half, rest_parts
    )
    rest_far = lax.ppermute(rest_theirs, "batch", far_pairs)
    lead_shard, rest_shard, message = small_call(
        sum_lead_kernel,
        "sum_lead",
        [shape(lead.shape, F32), shape(rest.shape, F32), shape(terms.shape, F32)],
        lead_parts,
        rest_mine,
        rest_far,
        terms,
    )
    message = message + swap(message)
    stride = 1
    while stride < chips:
        message = message + lax.ppermute(message, "batch", [(i, i ^ stride) for i in range(chips)])
        stride *= 2
    like = lambda a: shape(a.shape, F32)
    moments = (
        qkv_moments.transpose(0, 2, 1, 3),
        out_moments.transpose(0, 2, 1),
        up_moments,
        down_moments.transpose(0, 2, 1),
        norm_moments,
    )
    results = small_call(
        update_kernel,
        "update_weights",
        [shape((1, 1), F32)] + [like(a) for a in masters + moments] + [shape((1, norm_part), F32)],
        (lax.axis_index("batch") * 2 + side).astype(jnp.int32).reshape(1),
        message,
        lead_shard,
        rest_shard,
        *masters,
        *moments,
    )
    grad_norm, qkv_next, out_next, up_next, down_next, norm_next = results[:6]
    qkv_states, out_states, up_states, down_states, norm_states, norm_grads = results[6:]
    return (
        block_out,
        input_grad,
        grad_norm.reshape(()),
        qkv_next.transpose(1, 0, 2),
        out_next.T,
        up_next,
        down_next.T,
        norm_next[0],
        qkv_states.transpose(0, 2, 1, 3),
        out_states.transpose(0, 2, 1),
        up_states,
        down_states.transpose(0, 2, 1),
        norm_states,
        norm_grads[0],
    )


def solution(mesh):
    chips = mesh.shape["batch"]
    return jax.shard_map(
        functools.partial(per_device, chips),
        mesh=mesh,
        in_specs=(
            P(("batch", "head"), None, None),
            P(("batch", "head"), None, None),
            P("batch"),
            P("batch", None),
            P("batch", None, "head"),
            P("head", "batch"),
            P("batch", "head"),
            P("head", "batch"),
            P(("batch", "head")),
            P(None, "batch", None, "head"),
            P(None, "head", "batch"),
            P(None, "batch", "head"),
            P(None, "head", "batch"),
            P(None, ("batch", "head")),
        ),
        out_specs=(
            P(("batch", "head"), None, None),
            P(("batch", "head"), None, None),
            P(),
            P("batch", None, "head"),
            P("head", "batch"),
            P("batch", "head"),
            P("head", "batch"),
            P(("batch", "head")),
            P(None, "batch", None, "head"),
            P(None, "head", "batch"),
            P(None, "batch", "head"),
            P(None, "head", "batch"),
            P(None, ("batch", "head")),
            P(("batch", "head")),
        ),
        check_vma=False,
    )
```

```python
import functools

import jax
import jax.numpy as jnp
from jax import lax
from jax.experimental import pallas as pl
from jax.experimental.pallas import tpu as pltpu
from jax.sharding import PartitionSpec as P

HD = 64
STEP = 10
NORM_EPS = 1e-06
CLIP_NORM = 1000.0
BETA_ONE = 0.5
BETA_TWO = 0.5
ADAM_EPS = 1e-08
RATE_LIST = (0.06, 0.25, 0.06, 0.03, 0.5)
DECAY_LIST = (0.04, 0.04, 0.04, 0.04, 0.0)

F32 = jnp.float32
BF16 = jnp.bfloat16
NN = (((1,), (0,)), ((), ()))
NT = (((1,), (1,)), ((), ()))
TN = (((0,), (0,)), ((), ()))
QB = 320
DB = 640
FB = 512
FC = 256
PAIR = 2 * HD
LIMIT_A, LIMIT_B, LIMIT_C, LIMIT_D, LIMIT_S, LIMIT_P = (
    pltpu.CompilerParams(vmem_limit_bytes=m * 2**20) for m in (52, 46, 52, 52, 16, 62)
)
IN_VMEM = pl.BlockSpec(memory_space=pltpu.VMEM)
IN_SMEM = pl.BlockSpec(memory_space=pltpu.SMEM)


def cost(microseconds):
    return pl.CostEstimate(flops=microseconds * 1_000_000_000, bytes_accessed=1_000_000, transcendentals=0)


def mm(left, right, dims=NN):
    return lax.dot_general(left, right, dims, preferred_element_type=F32)


def normalize(values):
    centred = values - jnp.mean(values, axis=-1, keepdims=True)
    variance = jnp.mean(centred * centred, axis=-1, keepdims=True)
    rs = lax.rsqrt(variance + NORM_EPS)
    return centred * rs, rs


def norm_backward(normal, rs, gained):
    inner = jnp.mean(gained * normal, axis=-1, keepdims=True)
    return rs * (gained - jnp.mean(gained, axis=-1, keepdims=True) - normal * inner)


def gelu_both(h, gradient):
    cdf = 0.5 + 0.5 * lax.erf(h * 0.7071067811865476)
    density = jnp.exp(h * h * -0.5) * 0.3989422804014327
    return (h * cdf).astype(BF16), (gradient * (cdf + h * density)).astype(BF16)


def split_pairs(own, other, per_pair):
    wide, narrow = 2 * per_pair, per_pair
    singles = []
    for part in range(per_pair // HD):
        cols = slice(wide + part * HD, wide + (part + 1) * HD)
        singles += [own[:, cols], other[:, cols]]
    return own[:, :wide], jnp.concatenate(singles, axis=1), other[:, :wide]


def join_pairs(first, second, third, per_pair):
    parts = [
        [second[:, p * PAIR + side * HD : p * PAIR + (side + 1) * HD] for p in range(per_pair // HD)]
        for side in range(2)
    ]
    return [first] + parts[0], [third] + parts[1]


def in_order(out_ref, own_ref, other_ref):
    members, sides, part, _ = own_ref.shape
    for head, ref in enumerate((own_ref, other_ref)):
        for place in range(members * sides):
            out_ref[head, place * part : (place + 1) * part, :] = ref[place % members, place // members]


def gathered_norms(first, second, chips, part, width):
    shard_rows = first.shape[0] // chips
    cols = slice(9 * HD, 9 * HD + part)
    pieces = []
    for chip in range(chips):
        row = chip * shard_rows
        for values in (first, second):
            pieces.append(values[row : row + 1, cols] + values[row + 1 : row + 2, cols])
    per_row = width // part
    return [jnp.concatenate(pieces[i * per_row : (i + 1) * per_row], axis=1) for i in range(4)]


def prepare_kernel(seq_rows, side_ref, len_ref, tok_ref, cot_ref, normal_ref, masked_ref, masked_t_ref):
    step = pl.program_id(0)
    rows = tok_ref.shape[0]
    first = step * rows
    row = first + lax.broadcasted_iota(jnp.int32, (rows, 1), 0)
    live = row < 0
    seqs = rows * pl.num_programs(0) // seq_rows
    for near in range(-(-rows // seq_rows) + 1):
        s = first // seq_rows + near
        bound = jnp.where(s < seqs, len_ref[side_ref[0] * seqs + jnp.minimum(s, seqs - 1)], 0)
        live = live | ((row >= s * seq_rows) & (row < s * seq_rows + bound))

    normal_ref[...], _ = normalize(tok_ref[...].astype(F32))
    masked = jnp.where(live, cot_ref[...].astype(F32), 0.0).astype(BF16)
    masked_ref[...] = masked
    masked_t_ref[...] = masked.T


def prepare(side, lengths, tokens, cotangent):
    seqs, seq_rows, width = tokens.shape
    total = seqs * seq_rows
    flat = lambda a: a.reshape(total, width)
    rowspec = pl.BlockSpec((DB, width), lambda s: (s, 0))
    shape = jax.ShapeDtypeStruct
    return pl.pallas_call(
        functools.partial(prepare_kernel, seq_rows),
        grid=(total // DB,),
        in_specs=[IN_SMEM, IN_SMEM, rowspec, rowspec],
        out_specs=[rowspec, rowspec, pl.BlockSpec((width, DB), lambda s: (0, s))],
        out_shape=[shape((total, width), F32), shape((total, width), BF16), shape((width, total), BF16)],
        compiler_params=LIMIT_P,
        cost_estimate=cost(5),
        name="prepare",
    )(side, lengths, flat(tokens), flat(cotangent))


def key_limits(rows):
    return [*range(256, rows, 256), rows]


def forward_kernel(
    chips, part, side_ref, len_ref, normal_ref, mask_ref, own_ref, other_ref,
    n1t_ref, qkv_ref, att_ref, linv_ref, p_ref, w_ref, norms_ref, lead_ref,
):
    rows, width = normal_ref.shape
    pairs = width // PAIR
    side, seq = side_ref[0], pl.program_id(0)

    @pl.when(seq == 0)
    def _():
        in_order(lead_ref, own_ref, other_ref)
        own, other = lead_ref[0], lead_ref[1]
        for i, weights in enumerate(split_pairs(own[:, : 9 * HD], other[:, : 9 * HD], 3 * HD)):
            w_ref[:, i * 3 * PAIR : (i + 1) * 3 * PAIR] = weights
        tail = slice(8 * HD, 10 * HD)
        mine, theirs = own[:, tail].astype(F32), other[:, tail].astype(F32)
        pad = jnp.zeros((own.shape[0], 8 * HD), F32)
        first = jnp.concatenate([pad, jnp.where(side == 0, mine, theirs)], axis=1)
        second = jnp.concatenate([pad, jnp.where(side == 0, theirs, mine)], axis=1)
        for i, row in enumerate(gathered_norms(first, second, chips, part, width)):
            norms_ref[i : i + 1, :] = row

    member = side * pl.num_programs(0) + seq
    position = lax.broadcasted_iota(jnp.int32, (1, rows), 1)
    mask = mask_ref[pl.ds(member, 1), :]
    visible = (position < len_ref[member]) & ((mask == 1) | (position == 0))
    hidden = jnp.where(visible, 0.0, -1e30)
    hidden = jnp.broadcast_to(hidden, (PAIR, rows)).T.astype(BF16)

    low = 0
    for keys in key_limits(rows):
        pl.when((len_ref[member] > low) & (len_ref[member] <= keys))(
            functools.partial(
                attend, keys, hidden, normal_ref, norms_ref, w_ref, n1t_ref, qkv_ref, att_ref, linv_ref, p_ref
            )
        )
        low = keys


def attend(count, hidden, normal_ref, norms_ref, w_ref, n1t_ref, qkv_ref, att_ref, linv_ref, p_ref):
    rows, width = normal_ref.shape
    pairs = width // PAIR
    n1 = (normal_ref[...] * norms_ref[0:1, :] + norms_ref[1:2, :]).astype(BF16)
    n1t_ref[...] = n1.T
    lane = lax.broadcasted_iota(jnp.int32, (QB, PAIR), 1)
    key_lane = lax.broadcasted_iota(jnp.int32, (count, PAIR), 1)
    ones = jnp.ones((count, PAIR), BF16)
    hidden = hidden[:count]
    ready = {}
    projected = mm(n1, w_ref[...])

    def project(pair):
        out = projected[:, pair * 3 * PAIR : (pair + 1) * 3 * PAIR]
        queries = (out[:, :PAIR].astype(BF16).astype(F32) * (HD**-0.5)).astype(BF16)
        others = out[:, PAIR:].astype(BF16)
        qkv_ref[pair, :, :PAIR] = queries
        qkv_ref[pair, :, PAIR:] = others
        keys = [jnp.where(key_lane == HD * (1 - half), hidden, others[:count, :PAIR]) for half in range(2)]
        return queries, keys, jnp.concatenate([others[:count, PAIR:], ones], axis=1)

    def scores(pair, block, half):
        if pair not in ready:
            ready[pair] = project(pair)
        queries, keys, _ = ready[pair]
        spot = jnp.where(lane == HD * (1 - half), 1.0, 0.0).astype(BF16)
        part_queries = jnp.where((lane < HD) == (half == 0), queries[block * QB : (block + 1) * QB], spot)
        return mm(part_queries, keys[half], NT)

    outs = {}

    def finish(pair, block, half, s):
        sl = slice(block * QB, (block + 1) * QB)
        p = jnp.exp(s - jnp.max(s, axis=-1, keepdims=True)).astype(BF16)
        p_ref[pair * 2 + half, sl, :count] = p
        out = mm(p, ready[pair][2])
        inverse = 1.0 / out[:, PAIR:]
        outs[half] = (out[:, :PAIR] * inverse, inverse)
        if half == 1:
            cols = slice(pair * PAIR, (pair + 1) * PAIR)
            att_ref[sl, cols] = jnp.where(lane < HD, outs[0][0], outs[1][0]).astype(BF16)
            linv_ref[sl, cols] = jnp.where(lane < HD, outs[0][1], outs[1][1])

    pending = None
    for pair in range(pairs):
        for block in range(rows // QB):
            for half in range(2):
                fresh = (pair, block, half, scores(pair, block, half))
                if pending is not None:
                    finish(*pending)
                pending = fresh
    finish(*pending)


def forward(chips, part, side, lengths, normal, key_masks, own, other):
    seqs, rows, width = normal.shape
    heads, pairs = width // HD, width // PAIR
    sq = pl.squeezed
    shape = jax.ShapeDtypeStruct
    whole = lambda *dims: pl.BlockSpec(dims, lambda s: (0,) * len(dims))
    row_spec = pl.BlockSpec((sq, rows, width), lambda s: (s, 0, 0))
    return pl.pallas_call(
        functools.partial(forward_kernel, chips, part),
        grid=(seqs,),
        in_specs=[IN_SMEM, IN_SMEM, row_spec, IN_VMEM, IN_VMEM, IN_VMEM],
        out_specs=[
            pl.BlockSpec((sq, width, rows), lambda s: (s, 0, 0)),
            pl.BlockSpec((sq, pairs, rows, 3 * PAIR), lambda s: (s, 0, 0, 0)),
            row_spec,
            row_spec,
            pl.BlockSpec((sq, heads, rows, rows), lambda s: (s, 0, 0, 0)),
            IN_VMEM,
            IN_VMEM,
        ],
        out_shape=[
            shape((seqs, width, rows), BF16),
            shape((seqs, pairs, rows, 3 * PAIR), BF16),
            shape((seqs, rows, width), BF16),
            shape((seqs, rows, width), F32),
            shape((seqs, heads, rows, rows), BF16),
            shape((width, 3 * width), BF16),
            shape((4, width), F32),
        ],
        scratch_shapes=[pltpu.VMEM((2, width, own.shape[-1]), BF16)],
        compiler_params=LIMIT_A,
        cost_estimate=cost(24),
        name="attention_forward",
    )(side, lengths, normal, key_masks, own, other)


def middle_kernel(
    units, tok_ref, gb_ref, gbt_ref, att_ref, linv_ref, own_ref, other_ref, norms_ref,
    mid_ref, act_ref, gmid_ref, gatt_ref, gown_ref, gother_ref, gnorm_ref, halves,
    wo_ref, gout_ref, gup_ref, gdown_ref, gh_ref,
):
    step = pl.program_id(0)
    rows, width = tok_ref.shape

    @pl.when(step == 0)
    def _():
        gout_ref[...] = jnp.zeros_like(gout_ref)
        gup_ref[...] = jnp.zeros_like(gup_ref)
        gdown_ref[...] = jnp.zeros_like(gdown_ref)
        gnorm_ref[...] = jnp.zeros_like(gnorm_ref)
        in_order(halves, own_ref, other_ref)
        cols = slice(2 * units, 2 * units + 3 * HD)
        parts = split_pairs(halves[0, :, cols], halves[1, :, cols], HD)
        for i, part in enumerate(parts):
            wo_ref[:, i * PAIR : (i + 1) * PAIR] = part

    x = tok_ref[...].astype(F32)
    att = att_ref[...]
    mid = x + mm(att, wo_ref[...], NT)
    gb, gbt = gb_ref[...], gbt_ref[...]
    early = [mm(gb, halves[0, :, units + c * FC : units + (c + 1) * FC]) for c in range(2)]
    normal, rs = normalize(mid)
    gain, shift = norms_ref[2:3, :], norms_ref[3:4, :]
    n2 = (normal * gain + shift).astype(BF16)
    n2t = n2.T
    mid_ref[...] = mid
    sums = [jnp.zeros_like(mid)]

    def begin(half, c):
        wu = halves[half, :, c * FC : (c + 1) * FC]
        wd = halves[half, :, units + c * FC : units + (c + 1) * FC]
        ga = early[c] if half == 0 and c < len(early) else mm(gb, wd)
        return half, c, wu, wd, mm(n2, wu), ga

    def finish(half, c, wu, wd, h, ga):
        cols = slice(c * FC, (c + 1) * FC)
        act, gh = gelu_both(h, ga)
        act_ref[half, :, cols] = act
        sums[0] = sums[0] + mm(gh, wu, NT)
        gh_ref[half, :, cols] = gh

    def weigh(half):
        gup_ref[half] += mm(n2t, gh_ref[half])
        gdown_ref[half] += mm(gbt, act_ref[half])

    pending = None
    for half in range(2):
        for c in range(units // FC):
            fresh = begin(half, c)
            if pending is not None:
                finish(*pending)
            pending = fresh
        if half == 1:
            weigh(0)
    finish(*pending)
    gtwo = sums[0]
    gnorm_ref[0:8, :] += jnp.sum((gtwo * normal).reshape(rows // 8, 8, width), axis=0)
    gnorm_ref[8:16, :] += jnp.sum(gtwo.reshape(rows // 8, 8, width), axis=0)
    gmid = gb.astype(F32) + norm_backward(normal, rs, gtwo * gain)
    gmid_ref[...] = gmid
    weigh(1)
    gm = gmid.astype(BF16)
    gout_ref[...] += mm(gm, att, TN)
    gatt_ref[...] = (mm(gm, wo_ref[...]) * linv_ref[...]).astype(BF16)

    @pl.when(step == pl.num_programs(0) - 1)
    def _():
        total = gout_ref[...]
        sides = join_pairs(
            total[:, :PAIR], total[:, PAIR : 2 * PAIR], total[:, 2 * PAIR :], HD
        )
        for half, ref in enumerate((gown_ref, gother_ref)):
            ref[:, :units] = gup_ref[half].astype(BF16)
            ref[:, units : 2 * units] = gdown_ref[half].astype(BF16)
            blank = jnp.zeros((total.shape[0], HD), F32)
            ref[:, 2 * units :] = jnp.concatenate(sides[half] + [blank], axis=1).astype(BF16)


def middle(tokens, masked, masked_t, attended, linv, own, other, norms):
    seqs, seq_rows, width = tokens.shape
    total = seqs * seq_rows
    packed = own.shape[-1]
    units = (packed - 4 * HD) // 2
    flat = lambda a: a.reshape(total, width)
    rowspec = pl.BlockSpec((FB, width), lambda s: (s, 0))
    whole = lambda *dims: pl.BlockSpec(dims, lambda s: (0,) * len(dims))
    shape = jax.ShapeDtypeStruct
    return pl.pallas_call(
        functools.partial(middle_kernel, units),
        grid=(total // FB,),
        in_specs=[
            rowspec,
            rowspec,
            pl.BlockSpec((width, FB), lambda s: (0, s)),
            rowspec,
            rowspec,
            IN_VMEM,
            IN_VMEM,
            IN_VMEM,
        ],
        out_specs=[
            rowspec,
            pl.BlockSpec((2, FB, units), lambda s: (0, s, 0)),
            rowspec,
            rowspec,
            IN_VMEM,
            IN_VMEM,
            whole(16, width),
            IN_VMEM,
        ],
        out_shape=[
            shape((total, width), F32),
            shape((2, total, units), BF16),
            shape((total, width), F32),
            shape((total, width), BF16),
            shape((width, packed), BF16),
            shape((width, packed), BF16),
            shape((16, width), F32),
            shape((2, width, packed), BF16),
        ],
        scratch_shapes=[
            pltpu.VMEM((width, width), BF16),
            pltpu.VMEM((width, width), F32),
            pltpu.VMEM((2, width, units), F32),
            pltpu.VMEM((2, width, units), F32),
            pltpu.VMEM((2, FB, units), BF16),
        ],
        compiler_params=LIMIT_B,
        cost_estimate=cost(36),
        name="feed_forward",
    )(flat(tokens), masked, masked_t, flat(attended), flat(linv), own, other, norms)


def backward_kernel(
    side_ref, len_ref, n1t_ref, qkv_ref, p_ref, gatt_ref, att_ref, gp_ref, gown_ref, gother_ref, gqkv_ref
):
    seq = pl.program_id(0)
    rows = qkv_ref.shape[1]

    @pl.when(seq == 0)
    def _():
        gqkv_ref[...] = jnp.zeros_like(gqkv_ref)

    length = len_ref[side_ref[0] * pl.num_programs(0) + seq]
    low = 0
    for count in key_limits(rows):
        pl.when((length > low) & (length <= count))(
            functools.partial(attend_backward, count, n1t_ref, qkv_ref, p_ref, gatt_ref, att_ref, gp_ref, gqkv_ref)
        )
        low = count

    @pl.when(seq == pl.num_programs(0) - 1)
    def _():
        group = 3 * PAIR
        thirds = [gqkv_ref[:, i * group : (i + 1) * group] for i in range(3)]
        sides = join_pairs(*thirds, 3 * HD)
        blank = jnp.zeros((gqkv_ref.shape[0], HD), F32)
        for columns, ref in zip(sides, (gown_ref, gother_ref)):
            ref[...] = jnp.concatenate(columns + [blank], axis=1).astype(BF16)


def attend_backward(count, n1t_ref, qkv_ref, p_ref, gatt_ref, att_ref, gp_ref, gqkv_ref):
    pairs, rows = qkv_ref.shape[:2]
    lane = lax.broadcasted_iota(jnp.int32, (count, PAIR), 1)
    zero = jnp.zeros((count, PAIR), BF16)
    state = {}

    def begin(pair, half):
        if half == 0:
            cols = slice(pair * PAIR, (pair + 1) * PAIR)
            ga = gatt_ref[:count, cols]
            state[pair] = dict(
                ga=ga,
                inner=ga.astype(F32) * att_ref[:count, cols].astype(F32),
                gat=ga.T,
                qt=qkv_ref[pair, :count, :PAIR].T,
                gq=[],
                gkt=[],
                gvt=[],
            )
        mask = (lane < HD) == (half == 0)
        values = qkv_ref[pair, :count, 2 * PAIR :]
        return pair, half, mask, mm(jnp.where(mask, state[pair]["ga"], zero), values, NT)

    def finish(pair, half, mask, dp):
        mine = state[pair]
        hs = slice(half * HD, half * HD + HD)
        p = p_ref[pair * 2 + half, :count, :count]
        mine["gvt"].append(mm(mine["gat"][hs], p))
        inner = jnp.sum(jnp.where(mask, mine["inner"], 0.0), axis=-1, keepdims=True)
        ds = (p.astype(F32) * (dp - inner)).astype(BF16)
        mine["gq"].append(mm(ds, qkv_ref[pair, :count, PAIR : 2 * PAIR]))
        mine["gkt"].append(mm(mine["qt"][hs], ds))
        if half == 1:
            joined = jnp.where(lane < HD, mine["gq"][0], mine["gq"][1])
            columns = (
                (joined * (HD**-0.5)).astype(BF16),
                jnp.concatenate(mine["gkt"], axis=0).astype(BF16).T,
                jnp.concatenate(mine["gvt"], axis=0).astype(BF16).T,
            )
            for i, values in enumerate(columns):
                start = (3 * pair + i) * PAIR
                gp_ref[:count, start : start + PAIR] = values

    pending = None
    for pair in range(pairs):
        for half in range(2):
            fresh = begin(pair, half)
            if pending is not None:
                finish(*pending)
            pending = fresh
    finish(*pending)
    gqkv_ref[...] += mm(n1t_ref[:, :count], gp_ref[:count, :])
    if count < rows:
        gp_ref[count:, :] = jnp.zeros((rows - count, gp_ref.shape[1]), BF16)


def backward(side, lengths, n1t, qkv, probs, gatt, attended):
    seqs, rows, width = attended.shape
    pairs = width // PAIR
    sq = pl.squeezed
    rowspec = pl.BlockSpec((sq, rows, width), lambda s: (s, 0, 0))
    groupspec = pl.BlockSpec((sq, pairs, rows, 3 * PAIR), lambda s: (s, 0, 0, 0))
    shape = jax.ShapeDtypeStruct
    packed = (width, 10 * HD)
    return pl.pallas_call(
        backward_kernel,
        grid=(seqs,),
        in_specs=[
            IN_SMEM,
            IN_SMEM,
            pl.BlockSpec((sq, width, rows), lambda s: (s, 0, 0)),
            groupspec,
            pl.BlockSpec((sq, 2 * pairs, rows, rows), lambda s: (s, 0, 0, 0)),
            rowspec,
            rowspec,
        ],
        out_specs=[pl.BlockSpec((sq, rows, 3 * width), lambda s: (s, 0, 0)), IN_VMEM, IN_VMEM],
        out_shape=[shape((seqs, rows, 3 * width), BF16), shape(packed, BF16), shape(packed, BF16)],
        scratch_shapes=[pltpu.VMEM((width, 3 * width), F32)],
        compiler_params=LIMIT_C,
        cost_estimate=cost(27),
        name="attention_backward",
    )(side, lengths, n1t, qkv, probs, gatt, attended)


def input_kernel(
    tok_ref, gp_ref, gmid_ref, w_ref, norms_ref, two_ref, mid_ref, act_ref, weights_ref,
    gin_ref, terms_ref, out_ref,
):
    rows, width = tok_ref.shape
    units = act_ref.shape[2]
    gone = mm(gp_ref[...], w_ref[...], NT)
    normal, rs = normalize(tok_ref[...].astype(F32))

    @pl.when((pl.program_id(0) == 0) & (pl.program_id(1) == 0))
    def _():
        terms_ref[...] = jnp.zeros_like(terms_ref)
        terms_ref[2:3, :] = jnp.sum(two_ref[0:8, :], axis=0, keepdims=True)
        terms_ref[3:4, :] = jnp.sum(two_ref[8:16, :], axis=0, keepdims=True)

    terms_ref[0:1, :] += jnp.sum(gone * normal, axis=0, keepdims=True)
    terms_ref[1:2, :] += jnp.sum(gone, axis=0, keepdims=True)
    gin_ref[...] = gmid_ref[...] + norm_backward(normal, rs, gone * norms_ref[0:1, :])
    out = mid_ref[...]
    for half in range(2):
        out = out + mm(act_ref[half], weights_ref[half, :, units : 2 * units], NT)
    out_ref[...] = out.astype(BF16)


def input_gradient(tokens, gp, gmid, wpairs, norms, gnorm_two, mid, act, weights):
    seqs, rows, width = tokens.shape
    units = act.shape[2]
    sq = pl.squeezed
    full = pl.BlockSpec((sq, DB, width), lambda s, r: (s, r, 0))
    shape = jax.ShapeDtypeStruct
    return pl.pallas_call(
        input_kernel,
        grid=(seqs, rows // DB),
        in_specs=[
            full,
            pl.BlockSpec((sq, DB, 3 * width), lambda s, r: (s, r, 0)),
            full,
            IN_VMEM,
            IN_VMEM,
            IN_VMEM,
            full,
            pl.BlockSpec((2, DB, units), lambda s, r: (0, s * (rows // DB) + r, 0)),
            IN_VMEM,
        ],
        out_specs=[full, IN_VMEM, full],
        out_shape=[
            shape((seqs, rows, width), F32),
            shape((8, width), F32),
            shape((seqs, rows, width), BF16),
        ],
        compiler_params=LIMIT_D,
        cost_estimate=cost(13),
        name="input_gradient",
    )(tokens, gp, gmid, wpairs, norms, gnorm_two, mid, act, weights)


def pack_kernel(qkv_ref, out_ref, up_ref, down_ref, norm_ref, lead_ref, rest_ref):
    rows = lead_ref.shape[0]
    part = norm_ref.shape[1]
    norm = norm_ref[...]
    high = norm.astype(BF16).astype(F32)
    row = lax.broadcasted_iota(jnp.int32, (rows, part), 0)
    extra = jnp.where(row == 0, high, jnp.where(row == 1, norm - high, 0.0))
    columns = [qkv_ref[c, :, :PAIR] for c in range(3)] + [qkv_ref[c, :, PAIR:] for c in range(3)]
    blank = jnp.zeros((rows, HD - part), F32)
    lead_ref[...] = jnp.concatenate(columns + [extra, blank], axis=1).astype(BF16)
    blank = jnp.zeros((rows, HD), F32)
    rest_ref[...] = jnp.concatenate([up_ref[...], down_ref[...], out_ref[...], blank], axis=1).astype(BF16)


def pair_kernel(half_ref, own_ref, far_ref, out_ref):
    own, far = own_ref[...], far_ref[...]
    first = half_ref[0] == 0
    for slot, value in enumerate((jnp.where(first, own, far), jnp.where(first, far, own))):
        for member in range(out_ref.shape[0]):
            out_ref[member, slot] = value


def add_kernel(left_ref, right_ref, out_ref):
    out_ref[...] = (left_ref[...].astype(F32) + right_ref[...].astype(F32)).astype(BF16)


def add_split_kernel(left_ref, right_ref, out_ref):
    total = (left_ref[...].astype(F32) + right_ref[...].astype(F32)).astype(BF16)
    members, halves, rows, _ = out_ref.shape
    for half in range(halves):
        for member in range(members):
            start = (half * members + member) * rows
            out_ref[member, half] = total[start : start + rows]


def sum_parts(parts_ref, out_ref):
    total = jnp.zeros((out_ref.shape[0], PAIR), F32)
    for start in range(0, out_ref.shape[1], PAIR):
        cols = slice(start, start + PAIR)
        piece = jnp.sum(parts_ref[:, :, cols].astype(F32), axis=0)
        out_ref[:, cols] = piece
        total = total + piece * piece
    return jnp.sum(total, axis=0, keepdims=True)


def sum_rest_kernel(half_ref, parts_ref, mine_ref, theirs_ref):
    first = half_ref[0] == 0
    for start in range(0, mine_ref.shape[1], PAIR):
        cols = slice(start, start + PAIR)
        low = jnp.sum(parts_ref[:, 0, :, cols].astype(F32), axis=0)
        high = jnp.sum(parts_ref[:, 1, :, cols].astype(F32), axis=0)
        mine_ref[:, cols] = jnp.where(first, low, high)
        theirs_ref[:, cols] = jnp.where(first, high, low).astype(BF16)


def sum_lead_kernel(parts_ref, mine_ref, far_ref, terms_ref, out_ref, rest_ref, message_ref):
    squares = sum_parts(parts_ref, out_ref)
    rest = mine_ref[...] + far_ref[...].astype(F32)
    rest_ref[...] = rest
    total = jnp.zeros((rest.shape[0], PAIR), F32)
    for start in range(0, rest.shape[1], PAIR):
        piece = rest[:, start : start + PAIR]
        total = total + piece * piece
    message_ref[...] = terms_ref[...]
    message_ref[4:5, :PAIR] = squares + jnp.sum(total, axis=0, keepdims=True)


def adamw(master, gradient, moments, rate, decay):
    moment = BETA_ONE * moments[0] + (1.0 - BETA_ONE) * gradient
    second = BETA_TWO * moments[1] + (1.0 - BETA_TWO) * gradient * gradient
    step_size = (
        moment / (1.0 - BETA_ONE**STEP) / (jnp.sqrt(second / (1.0 - BETA_TWO**STEP)) + ADAM_EPS)
    )
    return master - rate * (step_size + decay * master), moment, second


def update_kernel(
    index_ref, message_ref, lead_ref, rest_ref,
    qkv_ref, out_ref, up_ref, down_ref, norm_ref,
    qkv_m_ref, out_m_ref, up_m_ref, down_m_ref, norm_m_ref,
    gn_ref, qkv_n_ref, out_n_ref, up_n_ref, down_n_ref, norm_n_ref,
    qkv_s_ref, out_s_ref, up_s_ref, down_s_ref, norm_s_ref, grads_ref,
):
    units = up_ref.shape[1]
    terms = message_ref[0:4, :]
    squares = jnp.sum(terms * terms, axis=(0, 1), keepdims=True) + jnp.sum(
        message_ref[4:5, :], axis=(0, 1), keepdims=True
    )
    grad_norm = jnp.sqrt(squares)
    gn_ref[...] = grad_norm
    factor = jnp.minimum(1.0, CLIP_NORM / (grad_norm + 1e-06))
    for c in range(3):
        wide = lead_ref[:, c * PAIR : (c + 1) * PAIR]
        narrow = lead_ref[:, 3 * PAIR + c * HD : 3 * PAIR + (c + 1) * HD]
        for cols, grad in ((slice(0, PAIR), wide), (slice(PAIR, PAIR + HD), narrow)):
            new, moment, second = adamw(
                qkv_ref[c, :, cols], factor * grad, qkv_m_ref[:, c, :, cols], RATE_LIST[0], DECAY_LIST[0]
            )
            qkv_n_ref[c, :, cols] = new
            qkv_s_ref[0, c, :, cols] = moment
            qkv_s_ref[1, c, :, cols] = second
    part = norm_ref.shape[1]
    per_row = terms.shape[1] // part
    row = message_ref[pl.ds(index_ref[0] // per_row, 1), :]
    mine = pltpu.roll(row, lax.rem(per_row - lax.rem(index_ref[0], per_row), per_row) * part, 1)[:, :part]
    norm_grads = factor * mine
    grads_ref[...] = norm_grads
    plain = (
        (out_ref, rest_ref[:, 2 * units : 2 * units + 3 * HD], out_m_ref, out_n_ref, out_s_ref, 1),
        (up_ref, rest_ref[:, :units], up_m_ref, up_n_ref, up_s_ref, 2),
        (down_ref, rest_ref[:, units : 2 * units], down_m_ref, down_n_ref, down_s_ref, 3),
    )
    for master, grad, moments, next_ref, state_ref, i in plain:
        next_ref[...], state_ref[0], state_ref[1] = adamw(
            master[...], factor * grad, moments[...], RATE_LIST[i], DECAY_LIST[i]
        )
    norm_n_ref[...], norm_s_ref[0:1, :], norm_s_ref[1:2, :] = adamw(
        norm_ref[...], norm_grads, (norm_m_ref[0:1, :], norm_m_ref[1:2, :]), RATE_LIST[4], DECAY_LIST[4]
    )


def small_call(kernel, name, out_shape, *operands, in_spec=IN_VMEM, limit=LIMIT_S):
    return pl.pallas_call(
        kernel,
        in_specs=[IN_SMEM if a.dtype == jnp.int32 else in_spec for a in operands],
        out_specs=jax.tree.map(lambda a: IN_VMEM, out_shape),
        out_shape=out_shape,
        compiler_params=limit,
        cost_estimate=cost(2),
        name=name,
    )(*operands)


def swap(values):
    return lax.ppermute(values, "head", [(0, 1), (1, 0)])


def per_device(
    chips,
    tokens,
    cotangent,
    lengths,
    key_masks,
    qkv_master,
    out_master,
    up_master,
    down_master,
    norm_master,
    qkv_moments,
    out_moments,
    up_moments,
    down_moments,
    norm_moments,
):
    seqs, slot_rows, width = tokens.shape
    shard_rows = qkv_master.shape[0]
    norm_part = norm_master.shape[0]
    units = up_master.shape[1]
    side = lax.axis_index("head")

    qkv_rows = qkv_master.transpose(1, 0, 2)
    masters = (qkv_rows, out_master.T, up_master, down_master.T, norm_master[None])
    shape = jax.ShapeDtypeStruct
    lead, rest = small_call(
        pack_kernel,
        "pack_weights",
        [shape((shard_rows, 10 * HD), BF16), shape((shard_rows, 2 * units + 4 * HD), BF16)],
        *masters,
        in_spec=pl.BlockSpec(),
        limit=LIMIT_P,
    )
    members = chips // 2
    far_pairs = [(i, i ^ members) for i in range(chips)]
    teams = [list(range(members)), list(range(members, chips))]
    half = (lax.axis_index("batch") // members).astype(jnp.int32).reshape(1)
    lead_far = lax.ppermute(lead, "batch", far_pairs)
    rest_far = lax.ppermute(rest, "batch", far_pairs)
    team_of = lambda a: shape((members, 2) + a.shape, BF16)
    lead_pair = small_call(pair_kernel, "pair_lead", team_of(lead), half, lead, lead_far)
    lead_own = lax.all_to_all(lead_pair, "batch", 0, 0, axis_index_groups=teams)
    place = side.astype(jnp.int32).reshape(1)
    normal, masked, masked_t = prepare(place, lengths, tokens, cotangent)
    rest_pair = small_call(pair_kernel, "pair_rest", team_of(rest), half, rest, rest_far)
    lead_own, rest_pair, normal, masked, masked_t = lax.optimization_barrier(
        (lead_own, rest_pair, normal, masked, masked_t)
    )
    rest_own = lax.all_to_all(rest_pair, "batch", 0, 0, axis_index_groups=teams)
    lead_other = swap(lead_own)
    per_seq = lambda a: a.reshape(seqs, slot_rows, width)
    n1t, qkv, attended, linv, probs, wpairs, norms = forward(
        chips, norm_part, place, lengths, per_seq(normal), key_masks, lead_own, lead_other
    )
    rest_own, attended = lax.optimization_barrier((rest_own, attended))
    rest_other = swap(rest_own)
    mid, act, gmid, gatt, grest_own, grest_other, gnorm_two, weights = middle(
        tokens, masked, masked_t, attended, linv, rest_own, rest_other, norms
    )
    rest_sum = small_call(add_split_kernel, "add_rest", team_of(rest), grest_own, swap(grest_other))
    rest_sum, gatt = lax.optimization_barrier((rest_sum, gatt))
    rest_parts = lax.all_to_all(rest_sum, "batch", 0, 0, axis_index_groups=teams)
    gp, glead_own, glead_other = backward(place, lengths, n1t, qkv, probs, per_seq(gatt), attended)
    lead_sum = small_call(add_kernel, "add_lead", shape(glead_own.shape, BF16), glead_own, swap(glead_other))
    lead_sum, rest_parts = lax.optimization_barrier((lead_sum, rest_parts))
    lead_parts = lax.all_to_all(lead_sum.reshape(chips, shard_rows, 10 * HD), "batch", 0, 0)
    input_grad, terms, block_out = input_gradient(
        tokens, gp, per_seq(gmid), wpairs, norms, gnorm_two, per_seq(mid), act, weights
    )
    rest_mine, rest_theirs = small_call(
        sum_rest_kernel, "sum_rest", [shape(rest.shape, F32), shape(rest.shape, BF16)], half, rest_parts
    )
    rest_far = lax.ppermute(rest_theirs, "batch", far_pairs)
    lead_shard, rest_shard, message = small_call(
        sum_lead_kernel,
        "sum_lead",
        [shape(lead.shape, F32), shape(rest.shape, F32), shape(terms.shape, F32)],
        lead_parts,
        rest_mine,
        rest_far,
        terms,
    )
    message = message + swap(message)
    stride = 1
    while stride < chips:
        message = message + lax.ppermute(message, "batch", [(i, i ^ stride) for i in range(chips)])
        stride *= 2
    like = lambda a: shape(a.shape, F32)
    moments = (
        qkv_moments.transpose(0, 2, 1, 3),
        out_moments.transpose(0, 2, 1),
        up_moments,
        down_moments.transpose(0, 2, 1),
        norm_moments,
    )
    results = small_call(
        update_kernel,
        "update_weights",
        [shape((1, 1), F32)] + [like(a) for a in masters + moments] + [shape((1, norm_part), F32)],
        (lax.axis_index("batch") * 2 + side).astype(jnp.int32).reshape(1),
        message,
        lead_shard,
        rest_shard,
        *masters,
        *moments,
    )
    grad_norm, qkv_next, out_next, up_next, down_next, norm_next = results[:6]
    qkv_states, out_states, up_states, down_states, norm_states, norm_grads = results[6:]
    return (
        block_out,
        input_grad,
        grad_norm.reshape(()),
        qkv_next.transpose(1, 0, 2),
        out_next.T,
        up_next,
        down_next.T,
        norm_next[0],
        qkv_states.transpose(0, 2, 1, 3),
        out_states.transpose(0, 2, 1),
        up_states,
        down_states.transpose(0, 2, 1),
        norm_states,
        norm_grads[0],
    )


def solution(mesh):
    chips = mesh.shape["batch"]
    return jax.shard_map(
        functools.partial(per_device, chips),
        mesh=mesh,
        in_specs=(
            P(("batch", "head"), None, None),
            P(("batch", "head"), None, None),
            P("batch"),
            P("batch", None),
            P("batch", None, "head"),
            P("head", "batch"),
            P("batch", "head"),
            P("head", "batch"),
            P(("batch", "head")),
            P(None, "batch", None, "head"),
            P(None, "head", "batch"),
            P(None, "batch", "head"),
            P(None, "head", "batch"),
            P(None, ("batch", "head")),
        ),
        out_specs=(
            P(("batch", "head"), None, None),
            P(("batch", "head"), None, None),
            P(),
            P("batch", None, "head"),
            P("head", "batch"),
            P("batch", "head"),
            P("head", "batch"),
            P(("batch", "head")),
            P(None, "batch", None, "head"),
            P(None, "head", "batch"),
            P(None, "batch", "head"),
            P(None, "head", "batch"),
            P(None, ("batch", "head")),
            P(("batch", "head")),
        ),
        check_vma=False,
    )
```

```python
import functools

import jax
import jax.numpy as jnp
from jax import lax
from jax.experimental import pallas as pl
from jax.experimental.pallas import tpu as pltpu
from jax.sharding import PartitionSpec as P

HD = 64
STEP = 10
NORM_EPS = 1e-06
CLIP_NORM = 1000.0
BETA_ONE = 0.5
BETA_TWO = 0.5
ADAM_EPS = 1e-08
RATE_LIST = (0.06, 0.25, 0.06, 0.03, 0.5)
DECAY_LIST = (0.04, 0.04, 0.04, 0.04, 0.0)

F32 = jnp.float32
BF16 = jnp.bfloat16
NN = (((1,), (0,)), ((), ()))
NT = (((1,), (1,)), ((), ()))
TN = (((0,), (0,)), ((), ()))
QB = 320
DB = 640
FB = 512
FC = 256
PAIR = 2 * HD
LIMIT_A, LIMIT_B, LIMIT_C, LIMIT_D, LIMIT_S, LIMIT_P = (
    pltpu.CompilerParams(vmem_limit_bytes=m * 2**20) for m in (52, 46, 52, 52, 16, 62)
)
IN_VMEM = pl.BlockSpec(memory_space=pltpu.VMEM)
IN_SMEM = pl.BlockSpec(memory_space=pltpu.SMEM)


def cost(microseconds):
    return pl.CostEstimate(flops=microseconds * 1_000_000_000, bytes_accessed=1_000_000, transcendentals=0)


def mm(left, right, dims=NN):
    return lax.dot_general(left, right, dims, preferred_element_type=F32)


def normalize(values):
    centred = values - jnp.mean(values, axis=-1, keepdims=True)
    variance = jnp.mean(centred * centred, axis=-1, keepdims=True)
    rs = lax.rsqrt(variance + NORM_EPS)
    return centred * rs, rs


def norm_backward(normal, rs, gained):
    inner = jnp.mean(gained * normal, axis=-1, keepdims=True)
    return rs * (gained - jnp.mean(gained, axis=-1, keepdims=True) - normal * inner)


def gelu_both(h, gradient):
    cdf = 0.5 + 0.5 * lax.erf(h * 0.7071067811865476)
    density = jnp.exp(h * h * -0.5) * 0.3989422804014327
    return (h * cdf).astype(BF16), (gradient * (cdf + h * density)).astype(BF16)


def split_pairs(own, other, per_pair):
    wide, narrow = 2 * per_pair, per_pair
    singles = []
    for part in range(per_pair // HD):
        cols = slice(wide + part * HD, wide + (part + 1) * HD)
        singles += [own[:, cols], other[:, cols]]
    return own[:, :wide], jnp.concatenate(singles, axis=1), other[:, :wide]


def join_pairs(first, second, third, per_pair):
    parts = [
        [second[:, p * PAIR + side * HD : p * PAIR + (side + 1) * HD] for p in range(per_pair // HD)]
        for side in range(2)
    ]
    return [first] + parts[0], [third] + parts[1]


def in_order(out_ref, own_ref, other_ref):
    members, sides, part, _ = own_ref.shape
    for head, ref in enumerate((own_ref, other_ref)):
        for place in range(members * sides):
            out_ref[head, place * part : (place + 1) * part, :] = ref[place % members, place // members]


def gathered_norms(first, second, chips, part, width):
    shard_rows = first.shape[0] // chips
    cols = slice(9 * HD, 9 * HD + part)
    pieces = []
    for chip in range(chips):
        row = chip * shard_rows
        for values in (first, second):
            pieces.append(values[row : row + 1, cols] + values[row + 1 : row + 2, cols])
    per_row = width // part
    return [jnp.concatenate(pieces[i * per_row : (i + 1) * per_row], axis=1) for i in range(4)]


def prepare_kernel(seq_rows, side_ref, len_ref, tok_ref, cot_ref, normal_ref, masked_ref, masked_t_ref):
    step = pl.program_id(0)
    rows = tok_ref.shape[0]
    first = step * rows
    row = first + lax.broadcasted_iota(jnp.int32, (rows, 1), 0)
    live = row < 0
    seqs = rows * pl.num_programs(0) // seq_rows
    for near in range(-(-rows // seq_rows) + 1):
        s = first // seq_rows + near
        bound = jnp.where(s < seqs, len_ref[side_ref[0] * seqs + jnp.minimum(s, seqs - 1)], 0)
        live = live | ((row >= s * seq_rows) & (row < s * seq_rows + bound))

    normal_ref[...], _ = normalize(tok_ref[...].astype(F32))
    masked = jnp.where(live, cot_ref[...].astype(F32), 0.0).astype(BF16)
    masked_ref[...] = masked
    masked_t_ref[...] = masked.T


def prepare(side, lengths, tokens, cotangent):
    seqs, seq_rows, width = tokens.shape
    total = seqs * seq_rows
    flat = lambda a: a.reshape(total, width)
    rowspec = pl.BlockSpec((DB, width), lambda s: (s, 0))
    shape = jax.ShapeDtypeStruct
    return pl.pallas_call(
        functools.partial(prepare_kernel, seq_rows),
        grid=(total // DB,),
        in_specs=[IN_SMEM, IN_SMEM, rowspec, rowspec],
        out_specs=[rowspec, rowspec, pl.BlockSpec((width, DB), lambda s: (0, s))],
        out_shape=[shape((total, width), F32), shape((total, width), BF16), shape((width, total), BF16)],
        compiler_params=LIMIT_P,
        cost_estimate=cost(5),
        name="prepare",
    )(side, lengths, flat(tokens), flat(cotangent))


def key_limits(rows):
    return [*range(256, rows, 256), rows]


def forward_kernel(
    chips, part, side_ref, len_ref, normal_ref, mask_ref, own_ref, other_ref,
    n1t_ref, qkv_ref, att_ref, linv_ref, p_ref, w_ref, norms_ref, lead_ref,
):
    rows, width = normal_ref.shape
    pairs = width // PAIR
    side, seq = side_ref[0], pl.program_id(0)

    @pl.when(seq == 0)
    def _():
        in_order(lead_ref, own_ref, other_ref)
        own, other = lead_ref[0], lead_ref[1]
        for i, weights in enumerate(split_pairs(own[:, : 9 * HD], other[:, : 9 * HD], 3 * HD)):
            w_ref[:, i * 3 * PAIR : (i + 1) * 3 * PAIR] = weights
        tail = slice(8 * HD, 10 * HD)
        mine, theirs = own[:, tail].astype(F32), other[:, tail].astype(F32)
        pad = jnp.zeros((own.shape[0], 8 * HD), F32)
        first = jnp.concatenate([pad, jnp.where(side == 0, mine, theirs)], axis=1)
        second = jnp.concatenate([pad, jnp.where(side == 0, theirs, mine)], axis=1)
        for i, row in enumerate(gathered_norms(first, second, chips, part, width)):
            norms_ref[i : i + 1, :] = row

    member = side * pl.num_programs(0) + seq
    position = lax.broadcasted_iota(jnp.int32, (1, rows), 1)
    mask = mask_ref[pl.ds(member, 1), :]
    visible = (position < len_ref[member]) & ((mask == 1) | (position == 0))
    hidden = jnp.where(visible, 0.0, -1e30)
    hidden = jnp.broadcast_to(hidden, (PAIR, rows)).T.astype(BF16)

    low = 0
    for keys in key_limits(rows):
        pl.when((len_ref[member] > low) & (len_ref[member] <= keys))(
            functools.partial(
                attend, keys, hidden, normal_ref, norms_ref, w_ref, n1t_ref, qkv_ref, att_ref, linv_ref, p_ref
            )
        )
        low = keys


def attend(count, hidden, normal_ref, norms_ref, w_ref, n1t_ref, qkv_ref, att_ref, linv_ref, p_ref):
    rows, width = normal_ref.shape
    pairs = width // PAIR
    n1 = (normal_ref[...] * norms_ref[0:1, :] + norms_ref[1:2, :]).astype(BF16)
    n1t_ref[...] = n1.T
    lane = lax.broadcasted_iota(jnp.int32, (QB, PAIR), 1)
    key_lane = lax.broadcasted_iota(jnp.int32, (count, PAIR), 1)
    ones = jnp.ones((count, PAIR), BF16)
    hidden = hidden[:count]
    ready = {}
    projected = mm(n1, w_ref[...])

    def project(pair):
        out = projected[:, pair * 3 * PAIR : (pair + 1) * 3 * PAIR]
        queries = (out[:, :PAIR].astype(BF16).astype(F32) * (HD**-0.5)).astype(BF16)
        others = out[:, PAIR:].astype(BF16)
        qkv_ref[pair, :, :PAIR] = queries
        qkv_ref[pair, :, PAIR:] = others
        keys = [jnp.where(key_lane == HD * (1 - half), hidden, others[:count, :PAIR]) for half in range(2)]
        return queries, keys, jnp.concatenate([others[:count, PAIR:], ones], axis=1)

    def scores(pair, block, half):
        if pair not in ready:
            ready[pair] = project(pair)
        queries, keys, _ = ready[pair]
        spot = jnp.where(lane == HD * (1 - half), 1.0, 0.0).astype(BF16)
        part_queries = jnp.where((lane < HD) == (half == 0), queries[block * QB : (block + 1) * QB], spot)
        return mm(part_queries, keys[half], NT)

    outs = {}

    def finish(pair, block, half, s):
        sl = slice(block * QB, (block + 1) * QB)
        p = jnp.exp(s - jnp.max(s, axis=-1, keepdims=True)).astype(BF16)
        p_ref[pair * 2 + half, sl, :count] = p
        out = mm(p, ready[pair][2])
        inverse = 1.0 / out[:, PAIR:]
        outs[half] = (out[:, :PAIR] * inverse, inverse)
        if half == 1:
            cols = slice(pair * PAIR, (pair + 1) * PAIR)
            att_ref[sl, cols] = jnp.where(lane < HD, outs[0][0], outs[1][0]).astype(BF16)
            linv_ref[sl, cols] = jnp.where(lane < HD, outs[0][1], outs[1][1])

    pending = None
    for pair in range(pairs):
        for block in range(rows // QB):
            for half in range(2):
                fresh = (pair, block, half, scores(pair, block, half))
                if pending is not None:
                    finish(*pending)
                pending = fresh
    finish(*pending)


def forward(chips, part, side, lengths, normal, key_masks, own, other):
    seqs, rows, width = normal.shape
    heads, pairs = width // HD, width // PAIR
    sq = pl.squeezed
    shape = jax.ShapeDtypeStruct
    whole = lambda *dims: pl.BlockSpec(dims, lambda s: (0,) * len(dims))
    row_spec = pl.BlockSpec((sq, rows, width), lambda s: (s, 0, 0))
    return pl.pallas_call(
        functools.partial(forward_kernel, chips, part),
        grid=(seqs,),
        in_specs=[IN_SMEM, IN_SMEM, row_spec, IN_VMEM, IN_VMEM, IN_VMEM],
        out_specs=[
            pl.BlockSpec((sq, width, rows), lambda s: (s, 0, 0)),
            pl.BlockSpec((sq, pairs, rows, 3 * PAIR), lambda s: (s, 0, 0, 0)),
            row_spec,
            row_spec,
            pl.BlockSpec((sq, heads, rows, rows), lambda s: (s, 0, 0, 0)),
            IN_VMEM,
            IN_VMEM,
        ],
        out_shape=[
            shape((seqs, width, rows), BF16),
            shape((seqs, pairs, rows, 3 * PAIR), BF16),
            shape((seqs, rows, width), BF16),
            shape((seqs, rows, width), F32),
            shape((seqs, heads, rows, rows), BF16),
            shape((width, 3 * width), BF16),
            shape((4, width), F32),
        ],
        scratch_shapes=[pltpu.VMEM((2, width, own.shape[-1]), BF16)],
        compiler_params=LIMIT_A,
        cost_estimate=cost(24),
        name="attention_forward",
    )(side, lengths, normal, key_masks, own, other)


def middle_kernel(
    units, tok_ref, gb_ref, gbt_ref, att_ref, linv_ref, own_ref, other_ref, norms_ref,
    mid_ref, act_ref, gmid_ref, gatt_ref, gown_ref, gother_ref, gnorm_ref, halves,
    wo_ref, gout_ref, gup_ref, gdown_ref, gh_ref,
):
    step = pl.program_id(0)
    rows, width = tok_ref.shape

    @pl.when(step == 0)
    def _():
        gout_ref[...] = jnp.zeros_like(gout_ref)
        gup_ref[...] = jnp.zeros_like(gup_ref)
        gdown_ref[...] = jnp.zeros_like(gdown_ref)
        gnorm_ref[...] = jnp.zeros_like(gnorm_ref)
        in_order(halves, own_ref, other_ref)
        cols = slice(2 * units, 2 * units + 3 * HD)
        parts = split_pairs(halves[0, :, cols], halves[1, :, cols], HD)
        for i, part in enumerate(parts):
            wo_ref[:, i * PAIR : (i + 1) * PAIR] = part

    x = tok_ref[...].astype(F32)
    att = att_ref[...]
    mid = x + mm(att, wo_ref[...], NT)
    gb, gbt = gb_ref[...], gbt_ref[...]
    early = [mm(gb, halves[0, :, units + c * FC : units + (c + 1) * FC]) for c in range(2)]
    normal, rs = normalize(mid)
    gain, shift = norms_ref[2:3, :], norms_ref[3:4, :]
    n2 = (normal * gain + shift).astype(BF16)
    n2t = n2.T
    mid_ref[...] = mid
    sums = [jnp.zeros_like(mid)]

    def begin(half, c):
        wu = halves[half, :, c * FC : (c + 1) * FC]
        wd = halves[half, :, units + c * FC : units + (c + 1) * FC]
        ga = early[c] if half == 0 and c < len(early) else mm(gb, wd)
        return half, c, wu, wd, mm(n2, wu), ga

    def finish(half, c, wu, wd, h, ga):
        cols = slice(c * FC, (c + 1) * FC)
        act, gh = gelu_both(h, ga)
        act_ref[half, :, cols] = act
        sums[0] = sums[0] + mm(gh, wu, NT)
        gh_ref[half, :, cols] = gh

    def weigh(half):
        gup_ref[half] += mm(n2t, gh_ref[half])
        gdown_ref[half] += mm(gbt, act_ref[half])

    pending = None
    for half in range(2):
        for c in range(units // FC):
            fresh = begin(half, c)
            if pending is not None:
                finish(*pending)
            pending = fresh
        if half == 1:
            weigh(0)
    finish(*pending)
    gtwo = sums[0]
    gnorm_ref[0:8, :] += jnp.sum((gtwo * normal).reshape(rows // 8, 8, width), axis=0)
    gnorm_ref[8:16, :] += jnp.sum(gtwo.reshape(rows // 8, 8, width), axis=0)
    gmid = gb.astype(F32) + norm_backward(normal, rs, gtwo * gain)
    gmid_ref[...] = gmid
    weigh(1)
    gm = gmid.astype(BF16)
    gout_ref[...] += mm(gm, att, TN)
    gatt_ref[...] = (mm(gm, wo_ref[...]) * linv_ref[...]).astype(BF16)

    @pl.when(step == pl.num_programs(0) - 1)
    def _():
        total = gout_ref[...]
        sides = join_pairs(
            total[:, :PAIR], total[:, PAIR : 2 * PAIR], total[:, 2 * PAIR :], HD
        )
        for half, ref in enumerate((gown_ref, gother_ref)):
            ref[:, :units] = gup_ref[half].astype(BF16)
            ref[:, units : 2 * units] = gdown_ref[half].astype(BF16)
            blank = jnp.zeros((total.shape[0], HD), F32)
            ref[:, 2 * units :] = jnp.concatenate(sides[half] + [blank], axis=1).astype(BF16)


def middle(tokens, masked, masked_t, attended, linv, own, other, norms):
    seqs, seq_rows, width = tokens.shape
    total = seqs * seq_rows
    packed = own.shape[-1]
    units = (packed - 4 * HD) // 2
    flat = lambda a: a.reshape(total, width)
    rowspec = pl.BlockSpec((FB, width), lambda s: (s, 0))
    whole = lambda *dims: pl.BlockSpec(dims, lambda s: (0,) * len(dims))
    shape = jax.ShapeDtypeStruct
    return pl.pallas_call(
        functools.partial(middle_kernel, units),
        grid=(total // FB,),
        in_specs=[
            rowspec,
            rowspec,
            pl.BlockSpec((width, FB), lambda s: (0, s)),
            rowspec,
            rowspec,
            IN_VMEM,
            IN_VMEM,
            IN_VMEM,
        ],
        out_specs=[
            rowspec,
            pl.BlockSpec((2, FB, units), lambda s: (0, s, 0)),
            rowspec,
            rowspec,
            IN_VMEM,
            IN_VMEM,
            whole(16, width),
            IN_VMEM,
        ],
        out_shape=[
            shape((total, width), F32),
            shape((2, total, units), BF16),
            shape((total, width), F32),
            shape((total, width), BF16),
            shape((width, packed), BF16),
            shape((width, packed), BF16),
            shape((16, width), F32),
            shape((2, width, packed), BF16),
        ],
        scratch_shapes=[
            pltpu.VMEM((width, width), BF16),
            pltpu.VMEM((width, width), F32),
            pltpu.VMEM((2, width, units), F32),
            pltpu.VMEM((2, width, units), F32),
            pltpu.VMEM((2, FB, units), BF16),
        ],
        compiler_params=LIMIT_B,
        cost_estimate=cost(36),
        name="feed_forward",
    )(flat(tokens), masked, masked_t, flat(attended), flat(linv), own, other, norms)


def backward_kernel(
    side_ref, len_ref, n1t_ref, qkv_ref, p_ref, gatt_ref, att_ref, gp_ref, gown_ref, gother_ref, gqkv_ref
):
    seq = pl.program_id(0)
    rows = qkv_ref.shape[1]

    @pl.when(seq == 0)
    def _():
        gqkv_ref[...] = jnp.zeros_like(gqkv_ref)

    length = len_ref[side_ref[0] * pl.num_programs(0) + seq]
    low = 0
    for count in key_limits(rows):
        pl.when((length > low) & (length <= count))(
            functools.partial(attend_backward, count, n1t_ref, qkv_ref, p_ref, gatt_ref, att_ref, gp_ref, gqkv_ref)
        )
        low = count

    @pl.when(seq == pl.num_programs(0) - 1)
    def _():
        group = 3 * PAIR
        thirds = [gqkv_ref[:, i * group : (i + 1) * group] for i in range(3)]
        sides = join_pairs(*thirds, 3 * HD)
        blank = jnp.zeros((gqkv_ref.shape[0], HD), F32)
        for columns, ref in zip(sides, (gown_ref, gother_ref)):
            ref[...] = jnp.concatenate(columns + [blank], axis=1).astype(BF16)


def attend_backward(count, n1t_ref, qkv_ref, p_ref, gatt_ref, att_ref, gp_ref, gqkv_ref):
    pairs, rows = qkv_ref.shape[:2]
    lane = lax.broadcasted_iota(jnp.int32, (count, PAIR), 1)
    zero = jnp.zeros((count, PAIR), BF16)
    state = {}

    def begin(pair, half):
        if half == 0:
            cols = slice(pair * PAIR, (pair + 1) * PAIR)
            ga = gatt_ref[:count, cols]
            state[pair] = dict(
                ga=ga,
                inner=ga.astype(F32) * att_ref[:count, cols].astype(F32),
                gat=ga.T,
                qt=qkv_ref[pair, :count, :PAIR].T,
                gq=[],
                gkt=[],
                gvt=[],
            )
        mask = (lane < HD) == (half == 0)
        values = qkv_ref[pair, :count, 2 * PAIR :]
        return pair, half, mask, mm(jnp.where(mask, state[pair]["ga"], zero), values, NT)

    def finish(pair, half, mask, dp):
        mine = state[pair]
        hs = slice(half * HD, half * HD + HD)
        p = p_ref[pair * 2 + half, :count, :count]
        mine["gvt"].append(mm(mine["gat"][hs], p))
        inner = jnp.sum(jnp.where(mask, mine["inner"], 0.0), axis=-1, keepdims=True)
        ds = (p.astype(F32) * (dp - inner)).astype(BF16)
        mine["gq"].append(mm(ds, qkv_ref[pair, :count, PAIR : 2 * PAIR]))
        mine["gkt"].append(mm(mine["qt"][hs], ds))
        if half == 1:
            joined = jnp.where(lane < HD, mine["gq"][0], mine["gq"][1])
            columns = (
                (joined * (HD**-0.5)).astype(BF16),
                jnp.concatenate(mine["gkt"], axis=0).astype(BF16).T,
                jnp.concatenate(mine["gvt"], axis=0).astype(BF16).T,
            )
            for i, values in enumerate(columns):
                start = (3 * pair + i) * PAIR
                gp_ref[:count, start : start + PAIR] = values

    pending = None
    for pair in range(pairs):
        for half in range(2):
            fresh = begin(pair, half)
            if pending is not None:
                finish(*pending)
            pending = fresh
    finish(*pending)
    gqkv_ref[...] += mm(n1t_ref[:, :count], gp_ref[:count, :])
    if count < rows:
        gp_ref[count:, :] = jnp.zeros((rows - count, gp_ref.shape[1]), BF16)


def backward(side, lengths, n1t, qkv, probs, gatt, attended):
    seqs, rows, width = attended.shape
    pairs = width // PAIR
    sq = pl.squeezed
    rowspec = pl.BlockSpec((sq, rows, width), lambda s: (s, 0, 0))
    groupspec = pl.BlockSpec((sq, pairs, rows, 3 * PAIR), lambda s: (s, 0, 0, 0))
    shape = jax.ShapeDtypeStruct
    packed = (width, 10 * HD)
    return pl.pallas_call(
        backward_kernel,
        grid=(seqs,),
        in_specs=[
            IN_SMEM,
            IN_SMEM,
            pl.BlockSpec((sq, width, rows), lambda s: (s, 0, 0)),
            groupspec,
            pl.BlockSpec((sq, 2 * pairs, rows, rows), lambda s: (s, 0, 0, 0)),
            rowspec,
            rowspec,
        ],
        out_specs=[pl.BlockSpec((sq, rows, 3 * width), lambda s: (s, 0, 0)), IN_VMEM, IN_VMEM],
        out_shape=[shape((seqs, rows, 3 * width), BF16), shape(packed, BF16), shape(packed, BF16)],
        scratch_shapes=[pltpu.VMEM((width, 3 * width), F32)],
        compiler_params=LIMIT_C,
        cost_estimate=cost(27),
        name="attention_backward",
    )(side, lengths, n1t, qkv, probs, gatt, attended)


def input_kernel(
    tok_ref, gp_ref, gmid_ref, w_ref, norms_ref, two_ref, mid_ref, act_ref, weights_ref,
    gin_ref, terms_ref, out_ref,
):
    rows, width = tok_ref.shape
    units = act_ref.shape[2]
    gone = mm(gp_ref[...], w_ref[...], NT)
    normal, rs = normalize(tok_ref[...].astype(F32))

    @pl.when((pl.program_id(0) == 0) & (pl.program_id(1) == 0))
    def _():
        terms_ref[...] = jnp.zeros_like(terms_ref)
        terms_ref[2:3, :] = jnp.sum(two_ref[0:8, :], axis=0, keepdims=True)
        terms_ref[3:4, :] = jnp.sum(two_ref[8:16, :], axis=0, keepdims=True)

    terms_ref[0:1, :] += jnp.sum(gone * normal, axis=0, keepdims=True)
    terms_ref[1:2, :] += jnp.sum(gone, axis=0, keepdims=True)
    gin_ref[...] = gmid_ref[...] + norm_backward(normal, rs, gone * norms_ref[0:1, :])
    out = mid_ref[...]
    for half in range(2):
        out = out + mm(act_ref[half], weights_ref[half, :, units : 2 * units], NT)
    out_ref[...] = out.astype(BF16)


def input_gradient(tokens, gp, gmid, wpairs, norms, gnorm_two, mid, act, weights):
    seqs, rows, width = tokens.shape
    units = act.shape[2]
    sq = pl.squeezed
    full = pl.BlockSpec((sq, DB, width), lambda s, r: (s, r, 0))
    shape = jax.ShapeDtypeStruct
    return pl.pallas_call(
        input_kernel,
        grid=(seqs, rows // DB),
        in_specs=[
            full,
            pl.BlockSpec((sq, DB, 3 * width), lambda s, r: (s, r, 0)),
            full,
            IN_VMEM,
            IN_VMEM,
            IN_VMEM,
            full,
            pl.BlockSpec((2, DB, units), lambda s, r: (0, s * (rows // DB) + r, 0)),
            IN_VMEM,
        ],
        out_specs=[full, IN_VMEM, full],
        out_shape=[
            shape((seqs, rows, width), F32),
            shape((8, width), F32),
            shape((seqs, rows, width), BF16),
        ],
        compiler_params=LIMIT_D,
        cost_estimate=cost(13),
        name="input_gradient",
    )(tokens, gp, gmid, wpairs, norms, gnorm_two, mid, act, weights)


def pack_kernel(qkv_ref, out_ref, up_ref, down_ref, norm_ref, lead_ref, rest_ref):
    rows = lead_ref.shape[0]
    part = norm_ref.shape[1]
    norm = norm_ref[...]
    high = norm.astype(BF16).astype(F32)
    row = lax.broadcasted_iota(jnp.int32, (rows, part), 0)
    extra = jnp.where(row == 0, high, jnp.where(row == 1, norm - high, 0.0))
    columns = [qkv_ref[c, :, :PAIR] for c in range(3)] + [qkv_ref[c, :, PAIR:] for c in range(3)]
    blank = jnp.zeros((rows, HD - part), F32)
    lead_ref[...] = jnp.concatenate(columns + [extra, blank], axis=1).astype(BF16)
    blank = jnp.zeros((rows, HD), F32)
    rest_ref[...] = jnp.concatenate([up_ref[...], down_ref[...], out_ref[...], blank], axis=1).astype(BF16)


def pair_kernel(half_ref, own_ref, far_ref, out_ref):
    own, far = own_ref[...], far_ref[...]
    first = half_ref[0] == 0
    for slot, value in enumerate((jnp.where(first, own, far), jnp.where(first, far, own))):
        for member in range(out_ref.shape[0]):
            out_ref[member, slot] = value


def add_kernel(left_ref, right_ref, out_ref):
    out_ref[...] = (left_ref[...].astype(F32) + right_ref[...].astype(F32)).astype(BF16)


def add_split_kernel(left_ref, right_ref, out_ref):
    total = (left_ref[...].astype(F32) + right_ref[...].astype(F32)).astype(BF16)
    members, halves, rows, _ = out_ref.shape
    for half in range(halves):
        for member in range(members):
            start = (half * members + member) * rows
            out_ref[member, half] = total[start : start + rows]


def sum_parts(parts_ref, out_ref):
    total = jnp.zeros((out_ref.shape[0], PAIR), F32)
    for start in range(0, out_ref.shape[1], PAIR):
        cols = slice(start, start + PAIR)
        piece = jnp.sum(parts_ref[:, :, cols].astype(F32), axis=0)
        out_ref[:, cols] = piece
        total = total + piece * piece
    return jnp.sum(total, axis=0, keepdims=True)


def sum_rest_kernel(half_ref, parts_ref, mine_ref, theirs_ref):
    first = half_ref[0] == 0
    for start in range(0, mine_ref.shape[1], PAIR):
        cols = slice(start, start + PAIR)
        low = jnp.sum(parts_ref[:, 0, :, cols].astype(F32), axis=0)
        high = jnp.sum(parts_ref[:, 1, :, cols].astype(F32), axis=0)
        mine_ref[:, cols] = jnp.where(first, low, high)
        theirs_ref[:, cols] = jnp.where(first, high, low).astype(BF16)


def sum_lead_kernel(parts_ref, mine_ref, far_ref, terms_ref, out_ref, rest_ref, message_ref):
    squares = sum_parts(parts_ref, out_ref)
    rest = mine_ref[...] + far_ref[...].astype(F32)
    rest_ref[...] = rest
    total = jnp.zeros((rest.shape[0], PAIR), F32)
    for start in range(0, rest.shape[1], PAIR):
        piece = rest[:, start : start + PAIR]
        total = total + piece * piece
    message_ref[...] = terms_ref[...]
    message_ref[4:5, :PAIR] = squares + jnp.sum(total, axis=0, keepdims=True)


def adamw(master, gradient, moments, rate, decay):
    moment = BETA_ONE * moments[0] + (1.0 - BETA_ONE) * gradient
    second = BETA_TWO * moments[1] + (1.0 - BETA_TWO) * gradient * gradient
    step_size = (
        moment / (1.0 - BETA_ONE**STEP) / (jnp.sqrt(second / (1.0 - BETA_TWO**STEP)) + ADAM_EPS)
    )
    return master - rate * (step_size + decay * master), moment, second


def update_kernel(
    index_ref, message_ref, lead_ref, rest_ref,
    qkv_ref, out_ref, up_ref, down_ref, norm_ref,
    qkv_m_ref, out_m_ref, up_m_ref, down_m_ref, norm_m_ref,
    gn_ref, qkv_n_ref, out_n_ref, up_n_ref, down_n_ref, norm_n_ref,
    qkv_s_ref, out_s_ref, up_s_ref, down_s_ref, norm_s_ref, grads_ref,
):
    units = up_ref.shape[1]
    terms = message_ref[0:4, :]
    squares = jnp.sum(terms * terms, axis=(0, 1), keepdims=True) + jnp.sum(
        message_ref[4:5, :], axis=(0, 1), keepdims=True
    )
    grad_norm = jnp.sqrt(squares)
    gn_ref[...] = grad_norm
    factor = jnp.minimum(1.0, CLIP_NORM / (grad_norm + 1e-06))
    for c in range(3):
        wide = lead_ref[:, c * PAIR : (c + 1) * PAIR]
        narrow = lead_ref[:, 3 * PAIR + c * HD : 3 * PAIR + (c + 1) * HD]
        for cols, grad in ((slice(0, PAIR), wide), (slice(PAIR, PAIR + HD), narrow)):
            new, moment, second = adamw(
                qkv_ref[c, :, cols], factor * grad, qkv_m_ref[:, c, :, cols], RATE_LIST[0], DECAY_LIST[0]
            )
            qkv_n_ref[c, :, cols] = new
            qkv_s_ref[0, c, :, cols] = moment
            qkv_s_ref[1, c, :, cols] = second
    part = norm_ref.shape[1]
    per_row = terms.shape[1] // part
    row = message_ref[pl.ds(index_ref[0] // per_row, 1), :]
    mine = pltpu.roll(row, lax.rem(per_row - lax.rem(index_ref[0], per_row), per_row) * part, 1)[:, :part]
    norm_grads = factor * mine
    grads_ref[...] = norm_grads
    plain = (
        (out_ref, rest_ref[:, 2 * units : 2 * units + 3 * HD], out_m_ref, out_n_ref, out_s_ref, 1),
        (up_ref, rest_ref[:, :units], up_m_ref, up_n_ref, up_s_ref, 2),
        (down_ref, rest_ref[:, units : 2 * units], down_m_ref, down_n_ref, down_s_ref, 3),
    )
    for master, grad, moments, next_ref, state_ref, i in plain:
        next_ref[...], state_ref[0], state_ref[1] = adamw(
            master[...], factor * grad, moments[...], RATE_LIST[i], DECAY_LIST[i]
        )
    norm_n_ref[...], norm_s_ref[0:1, :], norm_s_ref[1:2, :] = adamw(
        norm_ref[...], norm_grads, (norm_m_ref[0:1, :], norm_m_ref[1:2, :]), RATE_LIST[4], DECAY_LIST[4]
    )


def small_call(kernel, name, out_shape, *operands, in_spec=IN_VMEM, limit=LIMIT_S):
    return pl.pallas_call(
        kernel,
        in_specs=[IN_SMEM if a.dtype == jnp.int32 else in_spec for a in operands],
        out_specs=jax.tree.map(lambda a: IN_VMEM, out_shape),
        out_shape=out_shape,
        compiler_params=limit,
        cost_estimate=cost(2),
        name=name,
    )(*operands)


def swap(values):
    return lax.ppermute(values, "head", [(0, 1), (1, 0)])


def per_device(
    chips,
    tokens,
    cotangent,
    lengths,
    key_masks,
    qkv_master,
    out_master,
    up_master,
    down_master,
    norm_master,
    qkv_moments,
    out_moments,
    up_moments,
    down_moments,
    norm_moments,
):
    seqs, slot_rows, width = tokens.shape
    shard_rows = qkv_master.shape[0]
    norm_part = norm_master.shape[0]
    units = up_master.shape[1]
    side = lax.axis_index("head")

    qkv_rows = qkv_master.transpose(1, 0, 2)
    masters = (qkv_rows, out_master.T, up_master, down_master.T, norm_master[None])
    shape = jax.ShapeDtypeStruct
    lead, rest = small_call(
        pack_kernel,
        "pack_weights",
        [shape((shard_rows, 10 * HD), BF16), shape((shard_rows, 2 * units + 4 * HD), BF16)],
        *masters,
        in_spec=pl.BlockSpec(),
        limit=LIMIT_P,
    )
    members = chips // 2
    far_pairs = [(i, i ^ members) for i in range(chips)]
    teams = [list(range(members)), list(range(members, chips))]
    half = (lax.axis_index("batch") // members).astype(jnp.int32).reshape(1)
    lead_far = lax.ppermute(lead, "batch", far_pairs)
    rest_far = lax.ppermute(rest, "batch", far_pairs)
    team_of = lambda a: shape((members, 2) + a.shape, BF16)
    lead_pair = small_call(pair_kernel, "pair_lead", team_of(lead), half, lead, lead_far)
    lead_own = lax.all_to_all(lead_pair, "batch", 0, 0, axis_index_groups=teams)
    place = side.astype(jnp.int32).reshape(1)
    normal, masked, masked_t = prepare(place, lengths, tokens, cotangent)
    rest_pair = small_call(pair_kernel, "pair_rest", team_of(rest), half, rest, rest_far)
    lead_own, rest_pair, normal, masked, masked_t = lax.optimization_barrier(
        (lead_own, rest_pair, normal, masked, masked_t)
    )
    rest_own = lax.all_to_all(rest_pair, "batch", 0, 0, axis_index_groups=teams)
    lead_other = swap(lead_own)
    per_seq = lambda a: a.reshape(seqs, slot_rows, width)
    n1t, qkv, attended, linv, probs, wpairs, norms = forward(
        chips, norm_part, place, lengths, per_seq(normal), key_masks, lead_own, lead_other
    )
    rest_own, attended = lax.optimization_barrier((rest_own, attended))
    rest_other = swap(rest_own)
    mid, act, gmid, gatt, grest_own, grest_other, gnorm_two, weights = middle(
        tokens, masked, masked_t, attended, linv, rest_own, rest_other, norms
    )
    rest_sum = small_call(add_split_kernel, "add_rest", team_of(rest), grest_own, swap(grest_other))
    rest_sum, gatt = lax.optimization_barrier((rest_sum, gatt))
    rest_parts = lax.all_to_all(rest_sum, "batch", 0, 0, axis_index_groups=teams)
    gp, glead_own, glead_other = backward(place, lengths, n1t, qkv, probs, per_seq(gatt), attended)
    lead_sum = small_call(add_kernel, "add_lead", shape(glead_own.shape, BF16), glead_own, swap(glead_other))
    lead_sum, rest_parts = lax.optimization_barrier((lead_sum, rest_parts))
    lead_parts = lax.all_to_all(lead_sum.reshape(chips, shard_rows, 10 * HD), "batch", 0, 0)
    input_grad, terms, block_out = input_gradient(
        tokens, gp, per_seq(gmid), wpairs, norms, gnorm_two, per_seq(mid), act, weights
    )
    rest_mine, rest_theirs = small_call(
        sum_rest_kernel, "sum_rest", [shape(rest.shape, F32), shape(rest.shape, BF16)], half, rest_parts
    )
    rest_far = lax.ppermute(rest_theirs, "batch", far_pairs)
    lead_shard, rest_shard, message = small_call(
        sum_lead_kernel,
        "sum_lead",
        [shape(lead.shape, F32), shape(rest.shape, F32), shape(terms.shape, F32)],
        lead_parts,
        rest_mine,
        rest_far,
        terms,
    )
    message = message + swap(message)
    stride = 1
    while stride < chips:
        across = [(2 * i + core, 2 * (i ^ stride) + 1 - core) for i in range(chips) for core in range(2)]
        message = message + lax.ppermute(message, ("batch", "head"), across)
        stride *= 2
    like = lambda a: shape(a.shape, F32)
    moments = (
        qkv_moments.transpose(0, 2, 1, 3),
        out_moments.transpose(0, 2, 1),
        up_moments,
        down_moments.transpose(0, 2, 1),
        norm_moments,
    )
    results = small_call(
        update_kernel,
        "update_weights",
        [shape((1, 1), F32)] + [like(a) for a in masters + moments] + [shape((1, norm_part), F32)],
        (lax.axis_index("batch") * 2 + side).astype(jnp.int32).reshape(1),
        message,
        lead_shard,
        rest_shard,
        *masters,
        *moments,
    )
    grad_norm, qkv_next, out_next, up_next, down_next, norm_next = results[:6]
    qkv_states, out_states, up_states, down_states, norm_states, norm_grads = results[6:]
    return (
        block_out,
        input_grad,
        grad_norm.reshape(()),
        qkv_next.transpose(1, 0, 2),
        out_next.T,
        up_next,
        down_next.T,
        norm_next[0],
        qkv_states.transpose(0, 2, 1, 3),
        out_states.transpose(0, 2, 1),
        up_states,
        down_states.transpose(0, 2, 1),
        norm_states,
        norm_grads[0],
    )


def solution(mesh):
    chips = mesh.shape["batch"]
    return jax.shard_map(
        functools.partial(per_device, chips),
        mesh=mesh,
        in_specs=(
            P(("batch", "head"), None, None),
            P(("batch", "head"), None, None),
            P("batch"),
            P("batch", None),
            P("batch", None, "head"),
            P("head", "batch"),
            P("batch", "head"),
            P("head", "batch"),
            P(("batch", "head")),
            P(None, "batch", None, "head"),
            P(None, "head", "batch"),
            P(None, "batch", "head"),
            P(None, "head", "batch"),
            P(None, ("batch", "head")),
        ),
        out_specs=(
            P(("batch", "head"), None, None),
            P(("batch", "head"), None, None),
            P(),
            P("batch", None, "head"),
            P("head", "batch"),
            P("batch", "head"),
            P("head", "batch"),
            P(("batch", "head")),
            P(None, "batch", None, "head"),
            P(None, "head", "batch"),
            P(None, "batch", "head"),
            P(None, "head", "batch"),
            P(None, ("batch", "head")),
            P(("batch", "head")),
        ),
        check_vma=False,
    )
```

```python
import functools

import jax
import jax.numpy as jnp
from jax import lax
from jax.experimental import pallas as pl
from jax.experimental.pallas import tpu as pltpu
from jax.sharding import PartitionSpec as P

HD = 64
STEP = 10
NORM_EPS = 1e-06
CLIP_NORM = 1000.0
BETA_ONE = 0.5
BETA_TWO = 0.5
ADAM_EPS = 1e-08
RATE_LIST = (0.06, 0.25, 0.06, 0.03, 0.5)
DECAY_LIST = (0.04, 0.04, 0.04, 0.04, 0.0)

F32 = jnp.float32
BF16 = jnp.bfloat16
NN = (((1,), (0,)), ((), ()))
NT = (((1,), (1,)), ((), ()))
TN = (((0,), (0,)), ((), ()))
QB = 320
DB = 640
FB = 512
FC = 256
PAIR = 2 * HD
LIMIT_A, LIMIT_B, LIMIT_C, LIMIT_D, LIMIT_S, LIMIT_P = (
    pltpu.CompilerParams(vmem_limit_bytes=m * 2**20) for m in (52, 46, 52, 54, 16, 62)
)
IN_VMEM = pl.BlockSpec(memory_space=pltpu.VMEM)
IN_SMEM = pl.BlockSpec(memory_space=pltpu.SMEM)


def cost(microseconds):
    return pl.CostEstimate(flops=microseconds * 1_000_000_000, bytes_accessed=1_000_000, transcendentals=0)


def mm(left, right, dims=NN):
    return lax.dot_general(left, right, dims, preferred_element_type=F32)


def normalize(values):
    centred = values - jnp.mean(values, axis=-1, keepdims=True)
    variance = jnp.mean(centred * centred, axis=-1, keepdims=True)
    rs = lax.rsqrt(variance + NORM_EPS)
    return centred * rs, rs


def norm_backward(normal, rs, gained):
    inner = jnp.mean(gained * normal, axis=-1, keepdims=True)
    return rs * (gained - jnp.mean(gained, axis=-1, keepdims=True) - normal * inner)


def gelu_both(h, gradient):
    cdf = 0.5 + 0.5 * lax.erf(h * 0.7071067811865476)
    density = jnp.exp(h * h * -0.5) * 0.3989422804014327
    return (h * cdf).astype(BF16), (gradient * (cdf + h * density)).astype(BF16)


def split_pairs(own, other, per_pair):
    wide, narrow = 2 * per_pair, per_pair
    singles = []
    for part in range(per_pair // HD):
        cols = slice(wide + part * HD, wide + (part + 1) * HD)
        singles += [own[:, cols], other[:, cols]]
    return own[:, :wide], jnp.concatenate(singles, axis=1), other[:, :wide]


def join_pairs(first, second, third, per_pair):
    parts = [
        [second[:, p * PAIR + side * HD : p * PAIR + (side + 1) * HD] for p in range(per_pair // HD)]
        for side in range(2)
    ]
    return [first] + parts[0], [third] + parts[1]


def in_order(out_ref, own_ref, other_ref):
    members, sides, part, _ = own_ref.shape
    for head, ref in enumerate((own_ref, other_ref)):
        for place in range(members * sides):
            out_ref[head, place * part : (place + 1) * part, :] = ref[place % members, place // members]


def gathered_norms(first, second, chips, part, width):
    shard_rows = first.shape[0] // chips
    cols = slice(9 * HD, 9 * HD + part)
    pieces = []
    for chip in range(chips):
        row = chip * shard_rows
        for values in (first, second):
            pieces.append(values[row : row + 1, cols] + values[row + 1 : row + 2, cols])
    per_row = width // part
    return [jnp.concatenate(pieces[i * per_row : (i + 1) * per_row], axis=1) for i in range(4)]


def prepare_kernel(seq_rows, side_ref, len_ref, tok_ref, cot_ref, normal_ref, masked_ref, masked_t_ref):
    step = pl.program_id(0)
    rows = tok_ref.shape[0]
    first = step * rows
    row = first + lax.broadcasted_iota(jnp.int32, (rows, 1), 0)
    live = row < 0
    seqs = rows * pl.num_programs(0) // seq_rows
    for near in range(-(-rows // seq_rows) + 1):
        s = first // seq_rows + near
        bound = jnp.where(s < seqs, len_ref[side_ref[0] * seqs + jnp.minimum(s, seqs - 1)], 0)
        live = live | ((row >= s * seq_rows) & (row < s * seq_rows + bound))

    normal_ref[...], _ = normalize(tok_ref[...].astype(F32))
    masked = jnp.where(live, cot_ref[...].astype(F32), 0.0).astype(BF16)
    masked_ref[...] = masked
    masked_t_ref[...] = masked.T


def prepare(side, lengths, tokens, cotangent):
    seqs, seq_rows, width = tokens.shape
    total = seqs * seq_rows
    flat = lambda a: a.reshape(total, width)
    rowspec = pl.BlockSpec((DB, width), lambda s: (s, 0))
    shape = jax.ShapeDtypeStruct
    return pl.pallas_call(
        functools.partial(prepare_kernel, seq_rows),
        grid=(total // DB,),
        in_specs=[IN_SMEM, IN_SMEM, rowspec, rowspec],
        out_specs=[rowspec, rowspec, pl.BlockSpec((width, DB), lambda s: (0, s))],
        out_shape=[shape((total, width), F32), shape((total, width), BF16), shape((width, total), BF16)],
        compiler_params=LIMIT_P,
        cost_estimate=cost(5),
        name="prepare",
    )(side, lengths, flat(tokens), flat(cotangent))


def key_limits(rows):
    return [*range(256, rows, 256), rows]


def forward_kernel(
    chips, part, side_ref, len_ref, normal_ref, mask_ref, own_ref, other_ref,
    n1t_ref, qkv_ref, att_ref, linv_ref, p_ref, w_ref, norms_ref, lead_ref,
):
    rows, width = normal_ref.shape
    pairs = width // PAIR
    side, seq = side_ref[0], pl.program_id(0)

    @pl.when(seq == 0)
    def _():
        in_order(lead_ref, own_ref, other_ref)
        own, other = lead_ref[0], lead_ref[1]
        for i, weights in enumerate(split_pairs(own[:, : 9 * HD], other[:, : 9 * HD], 3 * HD)):
            w_ref[:, i * 3 * PAIR : (i + 1) * 3 * PAIR] = weights
        tail = slice(8 * HD, 10 * HD)
        mine, theirs = own[:, tail].astype(F32), other[:, tail].astype(F32)
        pad = jnp.zeros((own.shape[0], 8 * HD), F32)
        first = jnp.concatenate([pad, jnp.where(side == 0, mine, theirs)], axis=1)
        second = jnp.concatenate([pad, jnp.where(side == 0, theirs, mine)], axis=1)
        for i, row in enumerate(gathered_norms(first, second, chips, part, width)):
            norms_ref[i : i + 1, :] = row

    member = side * pl.num_programs(0) + seq
    position = lax.broadcasted_iota(jnp.int32, (1, rows), 1)
    mask = mask_ref[pl.ds(member, 1), :]
    visible = (position < len_ref[member]) & ((mask == 1) | (position == 0))
    hidden = jnp.where(visible, 0.0, -1e30)
    hidden = jnp.broadcast_to(hidden, (PAIR, rows)).T.astype(BF16)

    low = 0
    for keys in key_limits(rows):
        pl.when((len_ref[member] > low) & (len_ref[member] <= keys))(
            functools.partial(
                attend, keys, hidden, normal_ref, norms_ref, w_ref, n1t_ref, qkv_ref, att_ref, linv_ref, p_ref
            )
        )
        low = keys


def attend(count, hidden, normal_ref, norms_ref, w_ref, n1t_ref, qkv_ref, att_ref, linv_ref, p_ref):
    rows, width = normal_ref.shape
    pairs = width // PAIR
    n1 = (normal_ref[...] * norms_ref[0:1, :] + norms_ref[1:2, :]).astype(BF16)
    n1t_ref[...] = n1.T
    lane = lax.broadcasted_iota(jnp.int32, (QB, PAIR), 1)
    key_lane = lax.broadcasted_iota(jnp.int32, (count, PAIR), 1)
    ones = jnp.ones((count, PAIR), BF16)
    hidden = hidden[:count]
    ready = {}
    projected = mm(n1, w_ref[...])

    def project(pair):
        out = projected[:, pair * 3 * PAIR : (pair + 1) * 3 * PAIR]
        queries = (out[:, :PAIR].astype(BF16).astype(F32) * (HD**-0.5)).astype(BF16)
        others = out[:, PAIR:].astype(BF16)
        qkv_ref[pair, :, :PAIR] = queries
        qkv_ref[pair, :, PAIR:] = others
        keys = [jnp.where(key_lane == HD * (1 - half), hidden, others[:count, :PAIR]) for half in range(2)]
        return queries, keys, jnp.concatenate([others[:count, PAIR:], ones], axis=1)

    def scores(pair, block, half):
        if pair not in ready:
            ready[pair] = project(pair)
        queries, keys, _ = ready[pair]
        spot = jnp.where(lane == HD * (1 - half), 1.0, 0.0).astype(BF16)
        part_queries = jnp.where((lane < HD) == (half == 0), queries[block * QB : (block + 1) * QB], spot)
        return mm(part_queries, keys[half], NT)

    outs = {}

    def finish(pair, block, half, s):
        sl = slice(block * QB, (block + 1) * QB)
        p = jnp.exp(s - jnp.max(s, axis=-1, keepdims=True)).astype(BF16)
        p_ref[pair * 2 + half, sl, :count] = p
        out = mm(p, ready[pair][2])
        inverse = 1.0 / out[:, PAIR:]
        outs[half] = (out[:, :PAIR] * inverse, inverse)
        if half == 1:
            cols = slice(pair * PAIR, (pair + 1) * PAIR)
            att_ref[sl, cols] = jnp.where(lane < HD, outs[0][0], outs[1][0]).astype(BF16)
            linv_ref[sl, cols] = jnp.where(lane < HD, outs[0][1], outs[1][1])

    pending = None
    for pair in range(pairs):
        for block in range(rows // QB):
            for half in range(2):
                fresh = (pair, block, half, scores(pair, block, half))
                if pending is not None:
                    finish(*pending)
                pending = fresh
    finish(*pending)


def forward(chips, part, side, lengths, normal, key_masks, own, other):
    seqs, rows, width = normal.shape
    heads, pairs = width // HD, width // PAIR
    sq = pl.squeezed
    shape = jax.ShapeDtypeStruct
    whole = lambda *dims: pl.BlockSpec(dims, lambda s: (0,) * len(dims))
    row_spec = pl.BlockSpec((sq, rows, width), lambda s: (s, 0, 0))
    return pl.pallas_call(
        functools.partial(forward_kernel, chips, part),
        grid=(seqs,),
        in_specs=[IN_SMEM, IN_SMEM, row_spec, IN_VMEM, IN_VMEM, IN_VMEM],
        out_specs=[
            pl.BlockSpec((sq, width, rows), lambda s: (s, 0, 0)),
            pl.BlockSpec((sq, pairs, rows, 3 * PAIR), lambda s: (s, 0, 0, 0)),
            row_spec,
            row_spec,
            pl.BlockSpec((sq, heads, rows, rows), lambda s: (s, 0, 0, 0)),
            IN_VMEM,
            IN_VMEM,
        ],
        out_shape=[
            shape((seqs, width, rows), BF16),
            shape((seqs, pairs, rows, 3 * PAIR), BF16),
            shape((seqs, rows, width), BF16),
            shape((seqs, rows, width), F32),
            shape((seqs, heads, rows, rows), BF16),
            shape((width, 3 * width), BF16),
            shape((4, width), F32),
        ],
        scratch_shapes=[pltpu.VMEM((2, width, own.shape[-1]), BF16)],
        compiler_params=LIMIT_A,
        cost_estimate=cost(24),
        name="attention_forward",
    )(side, lengths, normal, key_masks, own, other)


def middle_kernel(
    units, tok_ref, gb_ref, gbt_ref, att_ref, linv_ref, own_ref, other_ref, norms_ref,
    mid_ref, act_ref, gmid_ref, gatt_ref, gown_ref, gother_ref, gnorm_ref, halves,
    wo_ref, gout_ref, gup_ref, gdown_ref, gh_ref,
):
    step = pl.program_id(0)
    rows, width = tok_ref.shape

    @pl.when(step == 0)
    def _():
        gout_ref[...] = jnp.zeros_like(gout_ref)
        gup_ref[...] = jnp.zeros_like(gup_ref)
        gdown_ref[...] = jnp.zeros_like(gdown_ref)
        gnorm_ref[...] = jnp.zeros_like(gnorm_ref)
        in_order(halves, own_ref, other_ref)
        cols = slice(2 * units, 2 * units + 3 * HD)
        parts = split_pairs(halves[0, :, cols], halves[1, :, cols], HD)
        for i, part in enumerate(parts):
            wo_ref[:, i * PAIR : (i + 1) * PAIR] = part

    x = tok_ref[...].astype(F32)
    att = att_ref[...]
    mid = x + mm(att, wo_ref[...], NT)
    gb, gbt = gb_ref[...], gbt_ref[...]
    early = [mm(gb, halves[0, :, units + c * FC : units + (c + 1) * FC]) for c in range(2)]
    normal, rs = normalize(mid)
    gain, shift = norms_ref[2:3, :], norms_ref[3:4, :]
    n2 = (normal * gain + shift).astype(BF16)
    n2t = n2.T
    mid_ref[...] = mid
    sums = [jnp.zeros_like(mid)]

    def begin(half, c):
        wu = halves[half, :, c * FC : (c + 1) * FC]
        wd = halves[half, :, units + c * FC : units + (c + 1) * FC]
        ga = early[c] if half == 0 and c < len(early) else mm(gb, wd)
        return half, c, wu, wd, mm(n2, wu), ga

    def finish(half, c, wu, wd, h, ga):
        cols = slice(c * FC, (c + 1) * FC)
        act, gh = gelu_both(h, ga)
        act_ref[half, :, cols] = act
        sums[0] = sums[0] + mm(gh, wu, NT)
        gh_ref[half, :, cols] = gh

    def weigh(half):
        gup_ref[half] += mm(n2t, gh_ref[half])
        gdown_ref[half] += mm(gbt, act_ref[half])

    pending = None
    for half in range(2):
        for c in range(units // FC):
            fresh = begin(half, c)
            if pending is not None:
                finish(*pending)
            pending = fresh
        if half == 1:
            weigh(0)
    finish(*pending)
    gtwo = sums[0]
    gnorm_ref[0:8, :] += jnp.sum((gtwo * normal).reshape(rows // 8, 8, width), axis=0)
    gnorm_ref[8:16, :] += jnp.sum(gtwo.reshape(rows // 8, 8, width), axis=0)
    gmid = gb.astype(F32) + norm_backward(normal, rs, gtwo * gain)
    gmid_ref[...] = gmid
    weigh(1)
    gm = gmid.astype(BF16)
    gout_ref[...] += mm(gm, att, TN)
    gatt_ref[...] = (mm(gm, wo_ref[...]) * linv_ref[...]).astype(BF16)

    @pl.when(step == pl.num_programs(0) - 1)
    def _():
        total = gout_ref[...]
        sides = join_pairs(
            total[:, :PAIR], total[:, PAIR : 2 * PAIR], total[:, 2 * PAIR :], HD
        )
        for half, ref in enumerate((gown_ref, gother_ref)):
            ref[:, :units] = gup_ref[half].astype(BF16)
            ref[:, units : 2 * units] = gdown_ref[half].astype(BF16)
            blank = jnp.zeros((total.shape[0], HD), F32)
            ref[:, 2 * units :] = jnp.concatenate(sides[half] + [blank], axis=1).astype(BF16)


def middle(tokens, masked, masked_t, attended, linv, own, other, norms):
    seqs, seq_rows, width = tokens.shape
    total = seqs * seq_rows
    packed = own.shape[-1]
    units = (packed - 4 * HD) // 2
    flat = lambda a: a.reshape(total, width)
    rowspec = pl.BlockSpec((FB, width), lambda s: (s, 0))
    whole = lambda *dims: pl.BlockSpec(dims, lambda s: (0,) * len(dims))
    shape = jax.ShapeDtypeStruct
    return pl.pallas_call(
        functools.partial(middle_kernel, units),
        grid=(total // FB,),
        in_specs=[
            rowspec,
            rowspec,
            pl.BlockSpec((width, FB), lambda s: (0, s)),
            rowspec,
            rowspec,
            IN_VMEM,
            IN_VMEM,
            IN_VMEM,
        ],
        out_specs=[
            rowspec,
            pl.BlockSpec((2, FB, units), lambda s: (0, s, 0)),
            rowspec,
            rowspec,
            IN_VMEM,
            IN_VMEM,
            whole(16, width),
            IN_VMEM,
        ],
        out_shape=[
            shape((total, width), F32),
            shape((2, total, units), BF16),
            shape((total, width), F32),
            shape((total, width), BF16),
            shape((width, packed), BF16),
            shape((width, packed), BF16),
            shape((16, width), F32),
            shape((2, width, packed), BF16),
        ],
        scratch_shapes=[
            pltpu.VMEM((width, width), BF16),
            pltpu.VMEM((width, width), F32),
            pltpu.VMEM((2, width, units), F32),
            pltpu.VMEM((2, width, units), F32),
            pltpu.VMEM((2, FB, units), BF16),
        ],
        compiler_params=LIMIT_B,
        cost_estimate=cost(36),
        name="feed_forward",
    )(flat(tokens), masked, masked_t, flat(attended), flat(linv), own, other, norms)


def backward_kernel(
    side_ref, len_ref, n1t_ref, qkv_ref, p_ref, gatt_ref, att_ref, gp_ref, gown_ref, gother_ref, gqkv_ref
):
    seq = pl.program_id(0)
    rows = qkv_ref.shape[1]

    @pl.when(seq == 0)
    def _():
        gqkv_ref[...] = jnp.zeros_like(gqkv_ref)

    length = len_ref[side_ref[0] * pl.num_programs(0) + seq]
    low = 0
    for count in key_limits(rows):
        pl.when((length > low) & (length <= count))(
            functools.partial(attend_backward, count, n1t_ref, qkv_ref, p_ref, gatt_ref, att_ref, gp_ref, gqkv_ref)
        )
        low = count

    @pl.when(seq == pl.num_programs(0) - 1)
    def _():
        group = 3 * PAIR
        thirds = [gqkv_ref[:, i * group : (i + 1) * group] for i in range(3)]
        sides = join_pairs(*thirds, 3 * HD)
        blank = jnp.zeros((gqkv_ref.shape[0], HD), F32)
        for columns, ref in zip(sides, (gown_ref, gother_ref)):
            ref[...] = jnp.concatenate(columns + [blank], axis=1).astype(BF16)


def attend_backward(count, n1t_ref, qkv_ref, p_ref, gatt_ref, att_ref, gp_ref, gqkv_ref):
    pairs, rows = qkv_ref.shape[:2]
    lane = lax.broadcasted_iota(jnp.int32, (count, PAIR), 1)
    zero = jnp.zeros((count, PAIR), BF16)
    state = {}

    def begin(pair, half):
        if half == 0:
            cols = slice(pair * PAIR, (pair + 1) * PAIR)
            ga = gatt_ref[:count, cols]
            state[pair] = dict(
                ga=ga,
                inner=ga.astype(F32) * att_ref[:count, cols].astype(F32),
                gat=ga.T,
                qt=qkv_ref[pair, :count, :PAIR].T,
                gq=[],
                gkt=[],
                gvt=[],
            )
        mask = (lane < HD) == (half == 0)
        values = qkv_ref[pair, :count, 2 * PAIR :]
        return pair, half, mask, mm(jnp.where(mask, state[pair]["ga"], zero), values, NT)

    def finish(pair, half, mask, dp):
        mine = state[pair]
        hs = slice(half * HD, half * HD + HD)
        p = p_ref[pair * 2 + half, :count, :count]
        mine["gvt"].append(mm(mine["gat"][hs], p))
        inner = jnp.sum(jnp.where(mask, mine["inner"], 0.0), axis=-1, keepdims=True)
        ds = (p.astype(F32) * (dp - inner)).astype(BF16)
        mine["gq"].append(mm(ds, qkv_ref[pair, :count, PAIR : 2 * PAIR]))
        mine["gkt"].append(mm(mine["qt"][hs], ds))
        if half == 1:
            joined = jnp.where(lane < HD, mine["gq"][0], mine["gq"][1])
            columns = (
                (joined * (HD**-0.5)).astype(BF16),
                jnp.concatenate(mine["gkt"], axis=0).astype(BF16).T,
                jnp.concatenate(mine["gvt"], axis=0).astype(BF16).T,
            )
            for i, values in enumerate(columns):
                start = (3 * pair + i) * PAIR
                gp_ref[:count, start : start + PAIR] = values

    pending = None
    for pair in range(pairs):
        for half in range(2):
            fresh = begin(pair, half)
            if pending is not None:
                finish(*pending)
            pending = fresh
    finish(*pending)
    gqkv_ref[...] += mm(n1t_ref[:, :count], gp_ref[:count, :])
    if count < rows:
        gp_ref[count:, :] = jnp.zeros((rows - count, gp_ref.shape[1]), BF16)


def backward(side, lengths, n1t, qkv, probs, gatt, attended):
    seqs, rows, width = attended.shape
    pairs = width // PAIR
    sq = pl.squeezed
    rowspec = pl.BlockSpec((sq, rows, width), lambda s: (s, 0, 0))
    groupspec = pl.BlockSpec((sq, pairs, rows, 3 * PAIR), lambda s: (s, 0, 0, 0))
    shape = jax.ShapeDtypeStruct
    packed = (width, 10 * HD)
    return pl.pallas_call(
        backward_kernel,
        grid=(seqs,),
        in_specs=[
            IN_SMEM,
            IN_SMEM,
            pl.BlockSpec((sq, width, rows), lambda s: (s, 0, 0)),
            groupspec,
            pl.BlockSpec((sq, 2 * pairs, rows, rows), lambda s: (s, 0, 0, 0)),
            rowspec,
            rowspec,
        ],
        out_specs=[pl.BlockSpec((sq, rows, 3 * width), lambda s: (s, 0, 0)), IN_VMEM, IN_VMEM],
        out_shape=[shape((seqs, rows, 3 * width), BF16), shape(packed, BF16), shape(packed, BF16)],
        scratch_shapes=[pltpu.VMEM((width, 3 * width), F32)],
        compiler_params=LIMIT_C,
        cost_estimate=cost(27),
        name="attention_backward",
    )(side, lengths, n1t, qkv, probs, gatt, attended)


def input_kernel(
    tok_ref, gp_ref, gmid_ref, w_ref, norms_ref, two_ref, mid_ref, act_ref, weights_ref,
    gin_ref, terms_ref, out_ref,
):
    rows, width = tok_ref.shape
    units = act_ref.shape[2]
    gone = mm(gp_ref[...], w_ref[...], NT)
    normal, rs = normalize(tok_ref[...].astype(F32))

    @pl.when((pl.program_id(0) == 0) & (pl.program_id(1) == 0))
    def _():
        terms_ref[...] = jnp.zeros_like(terms_ref)
        terms_ref[2:3, :] = jnp.sum(two_ref[0:8, :], axis=0, keepdims=True)
        terms_ref[3:4, :] = jnp.sum(two_ref[8:16, :], axis=0, keepdims=True)

    terms_ref[0:1, :] += jnp.sum(gone * normal, axis=0, keepdims=True)
    terms_ref[1:2, :] += jnp.sum(gone, axis=0, keepdims=True)
    gin_ref[...] = gmid_ref[...] + norm_backward(normal, rs, gone * norms_ref[0:1, :])
    out = mid_ref[...]
    for half in range(2):
        out = out + mm(act_ref[half], weights_ref[half, :, units : 2 * units], NT)
    out_ref[...] = out.astype(BF16)


def input_gradient(tokens, gp, gmid, wpairs, norms, gnorm_two, mid, act, weights):
    seqs, rows, width = tokens.shape
    units = act.shape[2]
    sq = pl.squeezed
    full = pl.BlockSpec((sq, DB, width), lambda s, r: (s, r, 0))
    shape = jax.ShapeDtypeStruct
    return pl.pallas_call(
        input_kernel,
        grid=(seqs, rows // DB),
        in_specs=[
            full,
            pl.BlockSpec((sq, DB, 3 * width), lambda s, r: (s, r, 0)),
            full,
            IN_VMEM,
            IN_VMEM,
            IN_VMEM,
            full,
            pl.BlockSpec((2, DB, units), lambda s, r: (0, s * (rows // DB) + r, 0)),
            IN_VMEM,
        ],
        out_specs=[full, IN_VMEM, full],
        out_shape=[
            shape((seqs, rows, width), F32),
            shape((8, width), F32),
            shape((seqs, rows, width), BF16),
        ],
        compiler_params=LIMIT_D,
        cost_estimate=cost(13),
        name="input_gradient",
    )(tokens, gp, gmid, wpairs, norms, gnorm_two, mid, act, weights)


def pack_kernel(qkv_ref, out_ref, up_ref, down_ref, norm_ref, lead_ref, rest_ref):
    rows = lead_ref.shape[0]
    part = norm_ref.shape[1]
    norm = norm_ref[...]
    high = norm.astype(BF16).astype(F32)
    row = lax.broadcasted_iota(jnp.int32, (rows, part), 0)
    extra = jnp.where(row == 0, high, jnp.where(row == 1, norm - high, 0.0))
    columns = [qkv_ref[c, :, :PAIR] for c in range(3)] + [qkv_ref[c, :, PAIR:] for c in range(3)]
    blank = jnp.zeros((rows, HD - part), F32)
    lead_ref[...] = jnp.concatenate(columns + [extra, blank], axis=1).astype(BF16)
    blank = jnp.zeros((rows, HD), F32)
    rest_ref[...] = jnp.concatenate([up_ref[...], down_ref[...], out_ref[...], blank], axis=1).astype(BF16)


def pair_kernel(half_ref, own_ref, far_ref, out_ref):
    own, far = own_ref[...], far_ref[...]
    first = half_ref[0] == 0
    for slot, value in enumerate((jnp.where(first, own, far), jnp.where(first, far, own))):
        for member in range(out_ref.shape[0]):
            out_ref[member, slot] = value


def add_kernel(left_ref, right_ref, out_ref):
    out_ref[...] = (left_ref[...].astype(F32) + right_ref[...].astype(F32)).astype(BF16)


def add_split_kernel(left_ref, right_ref, out_ref):
    total = (left_ref[...].astype(F32) + right_ref[...].astype(F32)).astype(BF16)
    members, halves, rows, _ = out_ref.shape
    for half in range(halves):
        for member in range(members):
            start = (half * members + member) * rows
            out_ref[member, half] = total[start : start + rows]


def sum_parts(parts_ref, out_ref):
    total = jnp.zeros((out_ref.shape[0], PAIR), F32)
    for start in range(0, out_ref.shape[1], PAIR):
        cols = slice(start, start + PAIR)
        piece = jnp.sum(parts_ref[:, :, cols].astype(F32), axis=0)
        out_ref[:, cols] = piece
        total = total + piece * piece
    return jnp.sum(total, axis=0, keepdims=True)


def sum_rest_kernel(half_ref, parts_ref, mine_ref, theirs_ref):
    first = half_ref[0] == 0
    for start in range(0, mine_ref.shape[1], PAIR):
        cols = slice(start, start + PAIR)
        low = jnp.sum(parts_ref[:, 0, :, cols].astype(F32), axis=0)
        high = jnp.sum(parts_ref[:, 1, :, cols].astype(F32), axis=0)
        mine_ref[:, cols] = jnp.where(first, low, high)
        theirs_ref[:, cols] = jnp.where(first, high, low).astype(BF16)


def sum_lead_kernel(parts_ref, mine_ref, far_ref, terms_ref, out_ref, rest_ref, message_ref):
    squares = sum_parts(parts_ref, out_ref)
    rest = mine_ref[...] + far_ref[...].astype(F32)
    rest_ref[...] = rest
    total = jnp.zeros((rest.shape[0], PAIR), F32)
    for start in range(0, rest.shape[1], PAIR):
        piece = rest[:, start : start + PAIR]
        total = total + piece * piece
    message_ref[...] = terms_ref[...]
    message_ref[4:5, :PAIR] = squares + jnp.sum(total, axis=0, keepdims=True)


def adamw(master, gradient, moments, rate, decay):
    moment = BETA_ONE * moments[0] + (1.0 - BETA_ONE) * gradient
    second = BETA_TWO * moments[1] + (1.0 - BETA_TWO) * gradient * gradient
    step_size = (
        moment / (1.0 - BETA_ONE**STEP) / (jnp.sqrt(second / (1.0 - BETA_TWO**STEP)) + ADAM_EPS)
    )
    return master - rate * (step_size + decay * master), moment, second


def update_kernel(
    index_ref, message_ref, lead_ref, rest_ref,
    qkv_ref, out_ref, up_ref, down_ref, norm_ref,
    qkv_m_ref, out_m_ref, up_m_ref, down_m_ref, norm_m_ref,
    gn_ref, qkv_n_ref, out_n_ref, up_n_ref, down_n_ref, norm_n_ref,
    qkv_s_ref, out_s_ref, up_s_ref, down_s_ref, norm_s_ref, grads_ref,
):
    units = up_ref.shape[1]
    terms = message_ref[0:4, :]
    squares = jnp.sum(terms * terms, axis=(0, 1), keepdims=True) + jnp.sum(
        message_ref[4:5, :], axis=(0, 1), keepdims=True
    )
    grad_norm = jnp.sqrt(squares)
    gn_ref[...] = grad_norm
    factor = jnp.minimum(1.0, CLIP_NORM / (grad_norm + 1e-06))
    for c in range(3):
        wide = lead_ref[:, c * PAIR : (c + 1) * PAIR]
        narrow = lead_ref[:, 3 * PAIR + c * HD : 3 * PAIR + (c + 1) * HD]
        for cols, grad in ((slice(0, PAIR), wide), (slice(PAIR, PAIR + HD), narrow)):
            new, moment, second = adamw(
                qkv_ref[c, :, cols], factor * grad, qkv_m_ref[:, c, :, cols], RATE_LIST[0], DECAY_LIST[0]
            )
            qkv_n_ref[c, :, cols] = new
            qkv_s_ref[0, c, :, cols] = moment
            qkv_s_ref[1, c, :, cols] = second
    part = norm_ref.shape[1]
    per_row = terms.shape[1] // part
    row = message_ref[pl.ds(index_ref[0] // per_row, 1), :]
    mine = pltpu.roll(row, lax.rem(per_row - lax.rem(index_ref[0], per_row), per_row) * part, 1)[:, :part]
    norm_grads = factor * mine
    grads_ref[...] = norm_grads
    plain = (
        (out_ref, rest_ref[:, 2 * units : 2 * units + 3 * HD], out_m_ref, out_n_ref, out_s_ref, 1),
        (up_ref, rest_ref[:, :units], up_m_ref, up_n_ref, up_s_ref, 2),
        (down_ref, rest_ref[:, units : 2 * units], down_m_ref, down_n_ref, down_s_ref, 3),
    )
    for master, grad, moments, next_ref, state_ref, i in plain:
        next_ref[...], state_ref[0], state_ref[1] = adamw(
            master[...], factor * grad, moments[...], RATE_LIST[i], DECAY_LIST[i]
        )
    norm_n_ref[...], norm_s_ref[0:1, :], norm_s_ref[1:2, :] = adamw(
        norm_ref[...], norm_grads, (norm_m_ref[0:1, :], norm_m_ref[1:2, :]), RATE_LIST[4], DECAY_LIST[4]
    )


def small_call(kernel, name, out_shape, *operands, in_spec=IN_VMEM, limit=LIMIT_S):
    return pl.pallas_call(
        kernel,
        in_specs=[IN_SMEM if a.dtype == jnp.int32 else in_spec for a in operands],
        out_specs=jax.tree.map(lambda a: IN_VMEM, out_shape),
        out_shape=out_shape,
        compiler_params=limit,
        cost_estimate=cost(2),
        name=name,
    )(*operands)


def swap(values):
    return lax.ppermute(values, "head", [(0, 1), (1, 0)])


def per_device(
    chips,
    tokens,
    cotangent,
    lengths,
    key_masks,
    qkv_master,
    out_master,
    up_master,
    down_master,
    norm_master,
    qkv_moments,
    out_moments,
    up_moments,
    down_moments,
    norm_moments,
):
    seqs, slot_rows, width = tokens.shape
    shard_rows = qkv_master.shape[0]
    norm_part = norm_master.shape[0]
    units = up_master.shape[1]
    side = lax.axis_index("head")

    qkv_rows = qkv_master.transpose(1, 0, 2)
    masters = (qkv_rows, out_master.T, up_master, down_master.T, norm_master[None])
    shape = jax.ShapeDtypeStruct
    lead, rest = small_call(
        pack_kernel,
        "pack_weights",
        [shape((shard_rows, 10 * HD), BF16), shape((shard_rows, 2 * units + 4 * HD), BF16)],
        *masters,
        in_spec=pl.BlockSpec(),
        limit=LIMIT_P,
    )
    members = chips // 2
    far_pairs = [(i, i ^ members) for i in range(chips)]
    teams = [list(range(members)), list(range(members, chips))]
    half = (lax.axis_index("batch") // members).astype(jnp.int32).reshape(1)
    lead_far = lax.ppermute(lead, "batch", far_pairs)
    rest_far = lax.ppermute(rest, "batch", far_pairs)
    team_of = lambda a: shape((members, 2) + a.shape, BF16)
    lead_pair = small_call(pair_kernel, "pair_lead", team_of(lead), half, lead, lead_far)
    lead_own = lax.all_to_all(lead_pair, "batch", 0, 0, axis_index_groups=teams)
    place = side.astype(jnp.int32).reshape(1)
    normal, masked, masked_t = prepare(place, lengths, tokens, cotangent)
    rest_pair = small_call(pair_kernel, "pair_rest", team_of(rest), half, rest, rest_far)
    lead_own, rest_pair, normal, masked, masked_t = lax.optimization_barrier(
        (lead_own, rest_pair, normal, masked, masked_t)
    )
    rest_own = lax.all_to_all(rest_pair, "batch", 0, 0, axis_index_groups=teams)
    lead_other = swap(lead_own)
    per_seq = lambda a: a.reshape(seqs, slot_rows, width)
    n1t, qkv, attended, linv, probs, wpairs, norms = forward(
        chips, norm_part, place, lengths, per_seq(normal), key_masks, lead_own, lead_other
    )
    rest_own, attended = lax.optimization_barrier((rest_own, attended))
    rest_other = swap(rest_own)
    mid, act, gmid, gatt, grest_own, grest_other, gnorm_two, weights = middle(
        tokens, masked, masked_t, attended, linv, rest_own, rest_other, norms
    )
    rest_sum = small_call(add_split_kernel, "add_rest", team_of(rest), grest_own, swap(grest_other))
    rest_sum, gatt = lax.optimization_barrier((rest_sum, gatt))
    rest_parts = lax.all_to_all(rest_sum, "batch", 0, 0, axis_index_groups=teams)
    gp, glead_own, glead_other = backward(place, lengths, n1t, qkv, probs, per_seq(gatt), attended)
    rest_mine, rest_theirs = small_call(
        sum_rest_kernel, "sum_rest", [shape(rest.shape, F32), shape(rest.shape, BF16)], half, rest_parts
    )
    rest_theirs, glead_own = lax.optimization_barrier((rest_theirs, glead_own))
    lead_sum = small_call(add_kernel, "add_lead", shape(glead_own.shape, BF16), glead_own, swap(glead_other))
    lead_sum, rest_parts = lax.optimization_barrier((lead_sum, rest_parts))
    lead_parts = lax.all_to_all(lead_sum.reshape(chips, shard_rows, 10 * HD), "batch", 0, 0)
    input_grad, terms, block_out = input_gradient(
        tokens, gp, per_seq(gmid), wpairs, norms, gnorm_two, per_seq(mid), act, weights
    )
    rest_far = lax.ppermute(rest_theirs, "batch", far_pairs)
    lead_shard, rest_shard, message = small_call(
        sum_lead_kernel,
        "sum_lead",
        [shape(lead.shape, F32), shape(rest.shape, F32), shape(terms.shape, F32)],
        lead_parts,
        rest_mine,
        rest_far,
        terms,
    )
    message = message + swap(message)
    stride = 1
    while stride < chips:
        across = [(2 * i + core, 2 * (i ^ stride) + 1 - core) for i in range(chips) for core in range(2)]
        message = message + lax.ppermute(message, ("batch", "head"), across)
        stride *= 2
    like = lambda a: shape(a.shape, F32)
    moments = (
        qkv_moments.transpose(0, 2, 1, 3),
        out_moments.transpose(0, 2, 1),
        up_moments,
        down_moments.transpose(0, 2, 1),
        norm_moments,
    )
    results = small_call(
        update_kernel,
        "update_weights",
        [shape((1, 1), F32)] + [like(a) for a in masters + moments] + [shape((1, norm_part), F32)],
        (lax.axis_index("batch") * 2 + side).astype(jnp.int32).reshape(1),
        message,
        lead_shard,
        rest_shard,
        *masters,
        *moments,
    )
    grad_norm, qkv_next, out_next, up_next, down_next, norm_next = results[:6]
    qkv_states, out_states, up_states, down_states, norm_states, norm_grads = results[6:]
    return (
        block_out,
        input_grad,
        grad_norm.reshape(()),
        qkv_next.transpose(1, 0, 2),
        out_next.T,
        up_next,
        down_next.T,
        norm_next[0],
        qkv_states.transpose(0, 2, 1, 3),
        out_states.transpose(0, 2, 1),
        up_states,
        down_states.transpose(0, 2, 1),
        norm_states,
        norm_grads[0],
    )


def solution(mesh):
    chips = mesh.shape["batch"]
    return jax.shard_map(
        functools.partial(per_device, chips),
        mesh=mesh,
        in_specs=(
            P(("batch", "head"), None, None),
            P(("batch", "head"), None, None),
            P("batch"),
            P("batch", None),
            P("batch", None, "head"),
            P("head", "batch"),
            P("batch", "head"),
            P("head", "batch"),
            P(("batch", "head")),
            P(None, "batch", None, "head"),
            P(None, "head", "batch"),
            P(None, "batch", "head"),
            P(None, "head", "batch"),
            P(None, ("batch", "head")),
        ),
        out_specs=(
            P(("batch", "head"), None, None),
            P(("batch", "head"), None, None),
            P(),
            P("batch", None, "head"),
            P("head", "batch"),
            P("batch", "head"),
            P("head", "batch"),
            P(("batch", "head")),
            P(None, "batch", None, "head"),
            P(None, "head", "batch"),
            P(None, "batch", "head"),
            P(None, "head", "batch"),
            P(None, ("batch", "head")),
            P(("batch", "head")),
        ),
        check_vma=False,
    )
```

```python
import functools

import jax
import jax.numpy as jnp
from jax import lax
from jax.experimental import pallas as pl
from jax.experimental.pallas import tpu as pltpu
from jax.sharding import PartitionSpec as P

HD = 64
STEP = 10
NORM_EPS = 1e-06
CLIP_NORM = 1000.0
BETA_ONE = 0.5
BETA_TWO = 0.5
ADAM_EPS = 1e-08
RATE_LIST = (0.06, 0.25, 0.06, 0.03, 0.5)
DECAY_LIST = (0.04, 0.04, 0.04, 0.04, 0.0)

F32 = jnp.float32
BF16 = jnp.bfloat16
NN = (((1,), (0,)), ((), ()))
NT = (((1,), (1,)), ((), ()))
TN = (((0,), (0,)), ((), ()))
QB = 320
DB = 640
FB = 512
FC = 256
PAIR = 2 * HD
LIMIT_A, LIMIT_B, LIMIT_C, LIMIT_D, LIMIT_S, LIMIT_P = (
    pltpu.CompilerParams(vmem_limit_bytes=m * 2**20) for m in (52, 46, 52, 54, 16, 62)
)
IN_VMEM = pl.BlockSpec(memory_space=pltpu.VMEM)
IN_SMEM = pl.BlockSpec(memory_space=pltpu.SMEM)


def cost(microseconds):
    return pl.CostEstimate(flops=microseconds * 1_000_000_000, bytes_accessed=1_000_000, transcendentals=0)


def mm(left, right, dims=NN):
    return lax.dot_general(left, right, dims, preferred_element_type=F32)


def normalize(values):
    centred = values - jnp.mean(values, axis=-1, keepdims=True)
    variance = jnp.mean(centred * centred, axis=-1, keepdims=True)
    rs = lax.rsqrt(variance + NORM_EPS)
    return centred * rs, rs


def norm_backward(normal, rs, gained):
    inner = jnp.mean(gained * normal, axis=-1, keepdims=True)
    return rs * (gained - jnp.mean(gained, axis=-1, keepdims=True) - normal * inner)


def gelu_both(h, gradient):
    cdf = 0.5 + 0.5 * lax.erf(h * 0.7071067811865476)
    density = jnp.exp(h * h * -0.5) * 0.3989422804014327
    return (h * cdf).astype(BF16), (gradient * (cdf + h * density)).astype(BF16)


def split_pairs(own, other, per_pair):
    wide, narrow = 2 * per_pair, per_pair
    singles = []
    for part in range(per_pair // HD):
        cols = slice(wide + part * HD, wide + (part + 1) * HD)
        singles += [own[:, cols], other[:, cols]]
    return own[:, :wide], jnp.concatenate(singles, axis=1), other[:, :wide]


def join_pairs(first, second, third, per_pair):
    parts = [
        [second[:, p * PAIR + side * HD : p * PAIR + (side + 1) * HD] for p in range(per_pair // HD)]
        for side in range(2)
    ]
    return [first] + parts[0], [third] + parts[1]


def in_order(out_ref, own_ref, other_ref):
    members, sides, part, _ = own_ref.shape
    for head, ref in enumerate((own_ref, other_ref)):
        for place in range(members * sides):
            out_ref[head, place * part : (place + 1) * part, :] = ref[place % members, place // members]


def gathered_norms(first, second, chips, part, width):
    shard_rows = first.shape[0] // chips
    cols = slice(9 * HD, 9 * HD + part)
    pieces = []
    for chip in range(chips):
        row = chip * shard_rows
        for values in (first, second):
            pieces.append(values[row : row + 1, cols] + values[row + 1 : row + 2, cols])
    per_row = width // part
    return [jnp.concatenate(pieces[i * per_row : (i + 1) * per_row], axis=1) for i in range(4)]


def prepare_kernel(seq_rows, side_ref, len_ref, tok_ref, cot_ref, normal_ref, masked_ref, masked_t_ref):
    step = pl.program_id(0)
    rows = tok_ref.shape[0]
    first = step * rows
    row = first + lax.broadcasted_iota(jnp.int32, (rows, 1), 0)
    live = row < 0
    seqs = rows * pl.num_programs(0) // seq_rows
    for near in range(-(-rows // seq_rows) + 1):
        s = first // seq_rows + near
        bound = jnp.where(s < seqs, len_ref[side_ref[0] * seqs + jnp.minimum(s, seqs - 1)], 0)
        live = live | ((row >= s * seq_rows) & (row < s * seq_rows + bound))

    normal_ref[...], _ = normalize(tok_ref[...].astype(F32))
    masked = jnp.where(live, cot_ref[...].astype(F32), 0.0).astype(BF16)
    masked_ref[...] = masked
    masked_t_ref[...] = masked.T


def prepare(side, lengths, tokens, cotangent):
    seqs, seq_rows, width = tokens.shape
    total = seqs * seq_rows
    flat = lambda a: a.reshape(total, width)
    rowspec = pl.BlockSpec((DB, width), lambda s: (s, 0))
    shape = jax.ShapeDtypeStruct
    return pl.pallas_call(
        functools.partial(prepare_kernel, seq_rows),
        grid=(total // DB,),
        in_specs=[IN_SMEM, IN_SMEM, rowspec, rowspec],
        out_specs=[rowspec, rowspec, pl.BlockSpec((width, DB), lambda s: (0, s))],
        out_shape=[shape((total, width), F32), shape((total, width), BF16), shape((width, total), BF16)],
        compiler_params=LIMIT_P,
        cost_estimate=cost(5),
        name="prepare",
    )(side, lengths, flat(tokens), flat(cotangent))


def key_limits(rows):
    return [*range(256, rows, 256), rows]


def forward_kernel(
    chips, part, side_ref, len_ref, normal_ref, mask_ref, own_ref, other_ref,
    n1t_ref, qkv_ref, att_ref, linv_ref, p_ref, w_ref, norms_ref, lead_ref,
):
    rows, width = normal_ref.shape
    pairs = width // PAIR
    side, seq = side_ref[0], pl.program_id(0)

    @pl.when(seq == 0)
    def _():
        in_order(lead_ref, own_ref, other_ref)
        own, other = lead_ref[0], lead_ref[1]
        for i, weights in enumerate(split_pairs(own[:, : 9 * HD], other[:, : 9 * HD], 3 * HD)):
            w_ref[:, i * 3 * PAIR : (i + 1) * 3 * PAIR] = weights
        tail = slice(8 * HD, 10 * HD)
        mine, theirs = own[:, tail].astype(F32), other[:, tail].astype(F32)
        pad = jnp.zeros((own.shape[0], 8 * HD), F32)
        first = jnp.concatenate([pad, jnp.where(side == 0, mine, theirs)], axis=1)
        second = jnp.concatenate([pad, jnp.where(side == 0, theirs, mine)], axis=1)
        for i, row in enumerate(gathered_norms(first, second, chips, part, width)):
            norms_ref[i : i + 1, :] = row

    member = side * pl.num_programs(0) + seq
    position = lax.broadcasted_iota(jnp.int32, (1, rows), 1)
    mask = mask_ref[pl.ds(member, 1), :]
    visible = (position < len_ref[member]) & ((mask == 1) | (position == 0))
    hidden = jnp.where(visible, 0.0, -1e30)
    hidden = jnp.broadcast_to(hidden, (PAIR, rows)).T.astype(BF16)

    low = 0
    for keys in key_limits(rows):
        pl.when((len_ref[member] > low) & (len_ref[member] <= keys))(
            functools.partial(
                attend, keys, hidden, normal_ref, norms_ref, w_ref, n1t_ref, qkv_ref, att_ref, linv_ref, p_ref
            )
        )
        low = keys


def attend(count, hidden, normal_ref, norms_ref, w_ref, n1t_ref, qkv_ref, att_ref, linv_ref, p_ref):
    rows, width = normal_ref.shape
    pairs = width // PAIR
    n1 = (normal_ref[...] * norms_ref[0:1, :] + norms_ref[1:2, :]).astype(BF16)
    n1t_ref[...] = n1.T
    lane = lax.broadcasted_iota(jnp.int32, (QB, PAIR), 1)
    key_lane = lax.broadcasted_iota(jnp.int32, (count, PAIR), 1)
    ones = jnp.ones((count, PAIR), BF16)
    hidden = hidden[:count]
    ready = {}
    projected = mm(n1, w_ref[...])

    def project(pair):
        out = projected[:, pair * 3 * PAIR : (pair + 1) * 3 * PAIR]
        queries = (out[:, :PAIR].astype(BF16).astype(F32) * (HD**-0.5)).astype(BF16)
        others = out[:, PAIR:].astype(BF16)
        qkv_ref[pair, :, :PAIR] = queries
        qkv_ref[pair, :, PAIR:] = others
        keys = [jnp.where(key_lane == HD * (1 - half), hidden, others[:count, :PAIR]) for half in range(2)]
        return queries, keys, jnp.concatenate([others[:count, PAIR:], ones], axis=1)

    def scores(pair, block, half):
        if pair not in ready:
            ready[pair] = project(pair)
        queries, keys, _ = ready[pair]
        spot = jnp.where(lane == HD * (1 - half), 1.0, 0.0).astype(BF16)
        part_queries = jnp.where((lane < HD) == (half == 0), queries[block * QB : (block + 1) * QB], spot)
        return mm(part_queries, keys[half], NT)

    outs = {}

    def finish(pair, block, half, s):
        sl = slice(block * QB, (block + 1) * QB)
        p = jnp.exp(s - jnp.max(s, axis=-1, keepdims=True)).astype(BF16)
        p_ref[pair * 2 + half, sl, :count] = p
        out = mm(p, ready[pair][2])
        inverse = 1.0 / out[:, PAIR:]
        outs[half] = (out[:, :PAIR] * inverse, inverse)
        if half == 1:
            cols = slice(pair * PAIR, (pair + 1) * PAIR)
            att_ref[sl, cols] = jnp.where(lane < HD, outs[0][0], outs[1][0]).astype(BF16)
            linv_ref[sl, cols] = jnp.where(lane < HD, outs[0][1], outs[1][1]).astype(BF16)

    pending = None
    for pair in range(pairs):
        for block in range(rows // QB):
            for half in range(2):
                fresh = (pair, block, half, scores(pair, block, half))
                if pending is not None:
                    finish(*pending)
                pending = fresh
    finish(*pending)


def forward(chips, part, side, lengths, normal, key_masks, own, other):
    seqs, rows, width = normal.shape
    heads, pairs = width // HD, width // PAIR
    sq = pl.squeezed
    shape = jax.ShapeDtypeStruct
    whole = lambda *dims: pl.BlockSpec(dims, lambda s: (0,) * len(dims))
    row_spec = pl.BlockSpec((sq, rows, width), lambda s: (s, 0, 0))
    return pl.pallas_call(
        functools.partial(forward_kernel, chips, part),
        grid=(seqs,),
        in_specs=[IN_SMEM, IN_SMEM, row_spec, IN_VMEM, IN_VMEM, IN_VMEM],
        out_specs=[
            pl.BlockSpec((sq, width, rows), lambda s: (s, 0, 0)),
            pl.BlockSpec((sq, pairs, rows, 3 * PAIR), lambda s: (s, 0, 0, 0)),
            row_spec,
            row_spec,
            pl.BlockSpec((sq, heads, rows, rows), lambda s: (s, 0, 0, 0)),
            IN_VMEM,
            IN_VMEM,
        ],
        out_shape=[
            shape((seqs, width, rows), BF16),
            shape((seqs, pairs, rows, 3 * PAIR), BF16),
            shape((seqs, rows, width), BF16),
            shape((seqs, rows, width), BF16),
            shape((seqs, heads, rows, rows), BF16),
            shape((width, 3 * width), BF16),
            shape((4, width), F32),
        ],
        scratch_shapes=[pltpu.VMEM((2, width, own.shape[-1]), BF16)],
        compiler_params=LIMIT_A,
        cost_estimate=cost(24),
        name="attention_forward",
    )(side, lengths, normal, key_masks, own, other)


def middle_kernel(
    units, tok_ref, gb_ref, gbt_ref, att_ref, linv_ref, own_ref, other_ref, norms_ref,
    mid_ref, act_ref, gmid_ref, gatt_ref, gown_ref, gother_ref, gnorm_ref, halves,
    wo_ref, gout_ref, gup_ref, gdown_ref, gh_ref,
):
    step = pl.program_id(0)
    rows, width = tok_ref.shape

    @pl.when(step == 0)
    def _():
        gout_ref[...] = jnp.zeros_like(gout_ref)
        gup_ref[...] = jnp.zeros_like(gup_ref)
        gdown_ref[...] = jnp.zeros_like(gdown_ref)
        gnorm_ref[...] = jnp.zeros_like(gnorm_ref)
        in_order(halves, own_ref, other_ref)
        cols = slice(2 * units, 2 * units + 3 * HD)
        parts = split_pairs(halves[0, :, cols], halves[1, :, cols], HD)
        for i, part in enumerate(parts):
            wo_ref[:, i * PAIR : (i + 1) * PAIR] = part

    x = tok_ref[...].astype(F32)
    att = att_ref[...]
    mid = x + mm(att, wo_ref[...], NT)
    gb, gbt = gb_ref[...], gbt_ref[...]
    early = [mm(gb, halves[0, :, units + c * FC : units + (c + 1) * FC]) for c in range(2)]
    normal, rs = normalize(mid)
    gain, shift = norms_ref[2:3, :], norms_ref[3:4, :]
    n2 = (normal * gain + shift).astype(BF16)
    n2t = n2.T
    mid_ref[...] = mid
    sums = [jnp.zeros_like(mid)]

    def begin(half, c):
        wu = halves[half, :, c * FC : (c + 1) * FC]
        wd = halves[half, :, units + c * FC : units + (c + 1) * FC]
        ga = early[c] if half == 0 and c < len(early) else mm(gb, wd)
        return half, c, wu, wd, mm(n2, wu), ga

    def finish(half, c, wu, wd, h, ga):
        cols = slice(c * FC, (c + 1) * FC)
        act, gh = gelu_both(h, ga)
        act_ref[half, :, cols] = act
        sums[0] = sums[0] + mm(gh, wu, NT)
        gh_ref[half, :, cols] = gh

    def weigh(half):
        gup_ref[half] += mm(n2t, gh_ref[half])
        gdown_ref[half] += mm(gbt, act_ref[half])

    pending = None
    for half in range(2):
        for c in range(units // FC):
            fresh = begin(half, c)
            if pending is not None:
                finish(*pending)
            pending = fresh
        if half == 1:
            weigh(0)
    finish(*pending)
    gtwo = sums[0]
    gnorm_ref[0:8, :] += jnp.sum((gtwo * normal).reshape(rows // 8, 8, width), axis=0)
    gnorm_ref[8:16, :] += jnp.sum(gtwo.reshape(rows // 8, 8, width), axis=0)
    gmid = gb.astype(F32) + norm_backward(normal, rs, gtwo * gain)
    gmid_ref[...] = gmid
    weigh(1)
    gm = gmid.astype(BF16)
    gout_ref[...] += mm(gm, att, TN)
    gatt_ref[...] = (mm(gm, wo_ref[...]) * linv_ref[...].astype(F32)).astype(BF16)

    @pl.when(step == pl.num_programs(0) - 1)
    def _():
        total = gout_ref[...]
        sides = join_pairs(
            total[:, :PAIR], total[:, PAIR : 2 * PAIR], total[:, 2 * PAIR :], HD
        )
        for half, ref in enumerate((gown_ref, gother_ref)):
            ref[:, :units] = gup_ref[half].astype(BF16)
            ref[:, units : 2 * units] = gdown_ref[half].astype(BF16)
            blank = jnp.zeros((total.shape[0], HD), F32)
            ref[:, 2 * units :] = jnp.concatenate(sides[half] + [blank], axis=1).astype(BF16)


def middle(tokens, masked, masked_t, attended, linv, own, other, norms):
    seqs, seq_rows, width = tokens.shape
    total = seqs * seq_rows
    packed = own.shape[-1]
    units = (packed - 4 * HD) // 2
    flat = lambda a: a.reshape(total, width)
    rowspec = pl.BlockSpec((FB, width), lambda s: (s, 0))
    whole = lambda *dims: pl.BlockSpec(dims, lambda s: (0,) * len(dims))
    shape = jax.ShapeDtypeStruct
    return pl.pallas_call(
        functools.partial(middle_kernel, units),
        grid=(total // FB,),
        in_specs=[
            rowspec,
            rowspec,
            pl.BlockSpec((width, FB), lambda s: (0, s)),
            rowspec,
            rowspec,
            IN_VMEM,
            IN_VMEM,
            IN_VMEM,
        ],
        out_specs=[
            rowspec,
            pl.BlockSpec((2, FB, units), lambda s: (0, s, 0)),
            rowspec,
            rowspec,
            IN_VMEM,
            IN_VMEM,
            whole(16, width),
            IN_VMEM,
        ],
        out_shape=[
            shape((total, width), F32),
            shape((2, total, units), BF16),
            shape((total, width), F32),
            shape((total, width), BF16),
            shape((width, packed), BF16),
            shape((width, packed), BF16),
            shape((16, width), F32),
            shape((2, width, packed), BF16),
        ],
        scratch_shapes=[
            pltpu.VMEM((width, width), BF16),
            pltpu.VMEM((width, width), F32),
            pltpu.VMEM((2, width, units), F32),
            pltpu.VMEM((2, width, units), F32),
            pltpu.VMEM((2, FB, units), BF16),
        ],
        compiler_params=LIMIT_B,
        cost_estimate=cost(36),
        name="feed_forward",
    )(flat(tokens), masked, masked_t, flat(attended), flat(linv), own, other, norms)


def backward_kernel(
    side_ref, len_ref, n1t_ref, qkv_ref, p_ref, gatt_ref, att_ref, gp_ref, gown_ref, gother_ref, gqkv_ref
):
    seq = pl.program_id(0)
    rows = qkv_ref.shape[1]

    @pl.when(seq == 0)
    def _():
        gqkv_ref[...] = jnp.zeros_like(gqkv_ref)

    length = len_ref[side_ref[0] * pl.num_programs(0) + seq]
    low = 0
    for count in key_limits(rows):
        pl.when((length > low) & (length <= count))(
            functools.partial(attend_backward, count, n1t_ref, qkv_ref, p_ref, gatt_ref, att_ref, gp_ref, gqkv_ref)
        )
        low = count

    @pl.when(seq == pl.num_programs(0) - 1)
    def _():
        group = 3 * PAIR
        thirds = [gqkv_ref[:, i * group : (i + 1) * group] for i in range(3)]
        sides = join_pairs(*thirds, 3 * HD)
        blank = jnp.zeros((gqkv_ref.shape[0], HD), F32)
        for columns, ref in zip(sides, (gown_ref, gother_ref)):
            ref[...] = jnp.concatenate(columns + [blank], axis=1).astype(BF16)


def attend_backward(count, n1t_ref, qkv_ref, p_ref, gatt_ref, att_ref, gp_ref, gqkv_ref):
    pairs, rows = qkv_ref.shape[:2]
    lane = lax.broadcasted_iota(jnp.int32, (count, PAIR), 1)
    zero = jnp.zeros((count, PAIR), BF16)
    state = {}

    def begin(pair, half):
        if half == 0:
            cols = slice(pair * PAIR, (pair + 1) * PAIR)
            ga = gatt_ref[:count, cols]
            state[pair] = dict(
                ga=ga,
                inner=ga.astype(F32) * att_ref[:count, cols].astype(F32),
                gat=ga.T,
                qt=qkv_ref[pair, :count, :PAIR].T,
                gq=[],
                gkt=[],
                gvt=[],
            )
        mask = (lane < HD) == (half == 0)
        values = qkv_ref[pair, :count, 2 * PAIR :]
        return pair, half, mask, mm(jnp.where(mask, state[pair]["ga"], zero), values, NT)

    def finish(pair, half, mask, dp):
        mine = state[pair]
        hs = slice(half * HD, half * HD + HD)
        p = p_ref[pair * 2 + half, :count, :count]
        mine["gvt"].append(mm(mine["gat"][hs], p))
        inner = jnp.sum(jnp.where(mask, mine["inner"], 0.0), axis=-1, keepdims=True)
        ds = (p.astype(F32) * (dp - inner)).astype(BF16)
        mine["gq"].append(mm(ds, qkv_ref[pair, :count, PAIR : 2 * PAIR]))
        mine["gkt"].append(mm(mine["qt"][hs], ds))
        if half == 1:
            joined = jnp.where(lane < HD, mine["gq"][0], mine["gq"][1])
            columns = (
                (joined * (HD**-0.5)).astype(BF16),
                jnp.concatenate(mine["gkt"], axis=0).astype(BF16).T,
                jnp.concatenate(mine["gvt"], axis=0).astype(BF16).T,
            )
            for i, values in enumerate(columns):
                start = (3 * pair + i) * PAIR
                gp_ref[:count, start : start + PAIR] = values

    pending = None
    for pair in range(pairs):
        for half in range(2):
            fresh = begin(pair, half)
            if pending is not None:
                finish(*pending)
            pending = fresh
    finish(*pending)
    gqkv_ref[...] += mm(n1t_ref[:, :count], gp_ref[:count, :])
    if count < rows:
        gp_ref[count:, :] = jnp.zeros((rows - count, gp_ref.shape[1]), BF16)


def backward(side, lengths, n1t, qkv, probs, gatt, attended):
    seqs, rows, width = attended.shape
    pairs = width // PAIR
    sq = pl.squeezed
    rowspec = pl.BlockSpec((sq, rows, width), lambda s: (s, 0, 0))
    groupspec = pl.BlockSpec((sq, pairs, rows, 3 * PAIR), lambda s: (s, 0, 0, 0))
    shape = jax.ShapeDtypeStruct
    packed = (width, 10 * HD)
    return pl.pallas_call(
        backward_kernel,
        grid=(seqs,),
        in_specs=[
            IN_SMEM,
            IN_SMEM,
            pl.BlockSpec((sq, width, rows), lambda s: (s, 0, 0)),
            groupspec,
            pl.BlockSpec((sq, 2 * pairs, rows, rows), lambda s: (s, 0, 0, 0)),
            rowspec,
            rowspec,
        ],
        out_specs=[pl.BlockSpec((sq, rows, 3 * width), lambda s: (s, 0, 0)), IN_VMEM, IN_VMEM],
        out_shape=[shape((seqs, rows, 3 * width), BF16), shape(packed, BF16), shape(packed, BF16)],
        scratch_shapes=[pltpu.VMEM((width, 3 * width), F32)],
        compiler_params=LIMIT_C,
        cost_estimate=cost(27),
        name="attention_backward",
    )(side, lengths, n1t, qkv, probs, gatt, attended)


def input_kernel(
    tok_ref, gp_ref, gmid_ref, w_ref, norms_ref, two_ref, mid_ref, act_ref, weights_ref,
    gin_ref, terms_ref, out_ref,
):
    rows, width = tok_ref.shape
    units = act_ref.shape[2]
    gone = mm(gp_ref[...], w_ref[...], NT)
    normal, rs = normalize(tok_ref[...].astype(F32))

    @pl.when((pl.program_id(0) == 0) & (pl.program_id(1) == 0))
    def _():
        terms_ref[...] = jnp.zeros_like(terms_ref)
        terms_ref[2:3, :] = jnp.sum(two_ref[0:8, :], axis=0, keepdims=True)
        terms_ref[3:4, :] = jnp.sum(two_ref[8:16, :], axis=0, keepdims=True)

    terms_ref[0:1, :] += jnp.sum(gone * normal, axis=0, keepdims=True)
    terms_ref[1:2, :] += jnp.sum(gone, axis=0, keepdims=True)
    gin_ref[...] = gmid_ref[...] + norm_backward(normal, rs, gone * norms_ref[0:1, :])
    out = mid_ref[...]
    for half in range(2):
        out = out + mm(act_ref[half], weights_ref[half, :, units : 2 * units], NT)
    out_ref[...] = out.astype(BF16)


def input_gradient(tokens, gp, gmid, wpairs, norms, gnorm_two, mid, act, weights):
    seqs, rows, width = tokens.shape
    units = act.shape[2]
    sq = pl.squeezed
    full = pl.BlockSpec((sq, DB, width), lambda s, r: (s, r, 0))
    shape = jax.ShapeDtypeStruct
    return pl.pallas_call(
        input_kernel,
        grid=(seqs, rows // DB),
        in_specs=[
            full,
            pl.BlockSpec((sq, DB, 3 * width), lambda s, r: (s, r, 0)),
            full,
            IN_VMEM,
            IN_VMEM,
            IN_VMEM,
            full,
            pl.BlockSpec((2, DB, units), lambda s, r: (0, s * (rows // DB) + r, 0)),
            IN_VMEM,
        ],
        out_specs=[full, IN_VMEM, full],
        out_shape=[
            shape((seqs, rows, width), F32),
            shape((8, width), F32),
            shape((seqs, rows, width), BF16),
        ],
        compiler_params=LIMIT_D,
        cost_estimate=cost(13),
        name="input_gradient",
    )(tokens, gp, gmid, wpairs, norms, gnorm_two, mid, act, weights)


def pack_kernel(qkv_ref, out_ref, up_ref, down_ref, norm_ref, lead_ref, rest_ref):
    rows = lead_ref.shape[0]
    part = norm_ref.shape[1]
    norm = norm_ref[...]
    high = norm.astype(BF16).astype(F32)
    row = lax.broadcasted_iota(jnp.int32, (rows, part), 0)
    extra = jnp.where(row == 0, high, jnp.where(row == 1, norm - high, 0.0))
    columns = [qkv_ref[c, :, :PAIR] for c in range(3)] + [qkv_ref[c, :, PAIR:] for c in range(3)]
    blank = jnp.zeros((rows, HD - part), F32)
    lead_ref[...] = jnp.concatenate(columns + [extra, blank], axis=1).astype(BF16)
    blank = jnp.zeros((rows, HD), F32)
    rest_ref[...] = jnp.concatenate([up_ref[...], down_ref[...], out_ref[...], blank], axis=1).astype(BF16)


def pair_kernel(half_ref, own_ref, far_ref, out_ref):
    own, far = own_ref[...], far_ref[...]
    first = half_ref[0] == 0
    for slot, value in enumerate((jnp.where(first, own, far), jnp.where(first, far, own))):
        for member in range(out_ref.shape[0]):
            out_ref[member, slot] = value


def add_kernel(left_ref, right_ref, out_ref):
    out_ref[...] = (left_ref[...].astype(F32) + right_ref[...].astype(F32)).astype(BF16)


def add_split_kernel(left_ref, right_ref, out_ref):
    total = (left_ref[...].astype(F32) + right_ref[...].astype(F32)).astype(BF16)
    members, halves, rows, _ = out_ref.shape
    for half in range(halves):
        for member in range(members):
            start = (half * members + member) * rows
            out_ref[member, half] = total[start : start + rows]


def sum_parts(parts_ref, out_ref):
    total = jnp.zeros((out_ref.shape[0], PAIR), F32)
    for start in range(0, out_ref.shape[1], PAIR):
        cols = slice(start, start + PAIR)
        piece = jnp.sum(parts_ref[:, :, cols].astype(F32), axis=0)
        out_ref[:, cols] = piece
        total = total + piece * piece
    return jnp.sum(total, axis=0, keepdims=True)


def sum_rest_kernel(half_ref, parts_ref, mine_ref, theirs_ref):
    first = half_ref[0] == 0
    for start in range(0, mine_ref.shape[1], PAIR):
        cols = slice(start, start + PAIR)
        low = jnp.sum(parts_ref[:, 0, :, cols].astype(F32), axis=0)
        high = jnp.sum(parts_ref[:, 1, :, cols].astype(F32), axis=0)
        mine_ref[:, cols] = jnp.where(first, low, high)
        theirs_ref[:, cols] = jnp.where(first, high, low).astype(BF16)


def sum_lead_kernel(parts_ref, mine_ref, far_ref, terms_ref, out_ref, rest_ref, message_ref):
    squares = sum_parts(parts_ref, out_ref)
    rest = mine_ref[...] + far_ref[...].astype(F32)
    rest_ref[...] = rest
    total = jnp.zeros((rest.shape[0], PAIR), F32)
    for start in range(0, rest.shape[1], PAIR):
        piece = rest[:, start : start + PAIR]
        total = total + piece * piece
    message_ref[...] = terms_ref[...]
    message_ref[4:5, :PAIR] = squares + jnp.sum(total, axis=0, keepdims=True)


def adamw(master, gradient, moments, rate, decay):
    moment = BETA_ONE * moments[0] + (1.0 - BETA_ONE) * gradient
    second = BETA_TWO * moments[1] + (1.0 - BETA_TWO) * gradient * gradient
    step_size = (
        moment / (1.0 - BETA_ONE**STEP) / (jnp.sqrt(second / (1.0 - BETA_TWO**STEP)) + ADAM_EPS)
    )
    return master - rate * (step_size + decay * master), moment, second


def update_kernel(
    index_ref, message_ref, lead_ref, rest_ref,
    qkv_ref, out_ref, up_ref, down_ref, norm_ref,
    qkv_m_ref, out_m_ref, up_m_ref, down_m_ref, norm_m_ref,
    gn_ref, qkv_n_ref, out_n_ref, up_n_ref, down_n_ref, norm_n_ref,
    qkv_s_ref, out_s_ref, up_s_ref, down_s_ref, norm_s_ref, grads_ref,
):
    units = up_ref.shape[1]
    terms = message_ref[0:4, :]
    squares = jnp.sum(terms * terms, axis=(0, 1), keepdims=True) + jnp.sum(
        message_ref[4:5, :], axis=(0, 1), keepdims=True
    )
    grad_norm = jnp.sqrt(squares)
    gn_ref[...] = grad_norm
    factor = jnp.minimum(1.0, CLIP_NORM / (grad_norm + 1e-06))
    for c in range(3):
        wide = lead_ref[:, c * PAIR : (c + 1) * PAIR]
        narrow = lead_ref[:, 3 * PAIR + c * HD : 3 * PAIR + (c + 1) * HD]
        for cols, grad in ((slice(0, PAIR), wide), (slice(PAIR, PAIR + HD), narrow)):
            new, moment, second = adamw(
                qkv_ref[c, :, cols], factor * grad, qkv_m_ref[:, c, :, cols], RATE_LIST[0], DECAY_LIST[0]
            )
            qkv_n_ref[c, :, cols] = new
            qkv_s_ref[0, c, :, cols] = moment
            qkv_s_ref[1, c, :, cols] = second
    part = norm_ref.shape[1]
    per_row = terms.shape[1] // part
    row = message_ref[pl.ds(index_ref[0] // per_row, 1), :]
    mine = pltpu.roll(row, lax.rem(per_row - lax.rem(index_ref[0], per_row), per_row) * part, 1)[:, :part]
    norm_grads = factor * mine
    grads_ref[...] = norm_grads
    plain = (
        (out_ref, rest_ref[:, 2 * units : 2 * units + 3 * HD], out_m_ref, out_n_ref, out_s_ref, 1),
        (up_ref, rest_ref[:, :units], up_m_ref, up_n_ref, up_s_ref, 2),
        (down_ref, rest_ref[:, units : 2 * units], down_m_ref, down_n_ref, down_s_ref, 3),
    )
    for master, grad, moments, next_ref, state_ref, i in plain:
        next_ref[...], state_ref[0], state_ref[1] = adamw(
            master[...], factor * grad, moments[...], RATE_LIST[i], DECAY_LIST[i]
        )
    norm_n_ref[...], norm_s_ref[0:1, :], norm_s_ref[1:2, :] = adamw(
        norm_ref[...], norm_grads, (norm_m_ref[0:1, :], norm_m_ref[1:2, :]), RATE_LIST[4], DECAY_LIST[4]
    )


def small_call(kernel, name, out_shape, *operands, in_spec=IN_VMEM, limit=LIMIT_S):
    return pl.pallas_call(
        kernel,
        in_specs=[IN_SMEM if a.dtype == jnp.int32 else in_spec for a in operands],
        out_specs=jax.tree.map(lambda a: IN_VMEM, out_shape),
        out_shape=out_shape,
        compiler_params=limit,
        cost_estimate=cost(2),
        name=name,
    )(*operands)


def swap(values):
    return lax.ppermute(values, "head", [(0, 1), (1, 0)])


def per_device(
    chips,
    tokens,
    cotangent,
    lengths,
    key_masks,
    qkv_master,
    out_master,
    up_master,
    down_master,
    norm_master,
    qkv_moments,
    out_moments,
    up_moments,
    down_moments,
    norm_moments,
):
    seqs, slot_rows, width = tokens.shape
    shard_rows = qkv_master.shape[0]
    norm_part = norm_master.shape[0]
    units = up_master.shape[1]
    side = lax.axis_index("head")

    qkv_rows = qkv_master.transpose(1, 0, 2)
    masters = (qkv_rows, out_master.T, up_master, down_master.T, norm_master[None])
    shape = jax.ShapeDtypeStruct
    lead, rest = small_call(
        pack_kernel,
        "pack_weights",
        [shape((shard_rows, 10 * HD), BF16), shape((shard_rows, 2 * units + 4 * HD), BF16)],
        *masters,
        in_spec=pl.BlockSpec(),
        limit=LIMIT_P,
    )
    members = chips // 2
    far_pairs = [(i, i ^ members) for i in range(chips)]
    teams = [list(range(members)), list(range(members, chips))]
    half = (lax.axis_index("batch") // members).astype(jnp.int32).reshape(1)
    lead_far = lax.ppermute(lead, "batch", far_pairs)
    rest_far = lax.ppermute(rest, "batch", far_pairs)
    team_of = lambda a: shape((members, 2) + a.shape, BF16)
    lead_pair = small_call(pair_kernel, "pair_lead", team_of(lead), half, lead, lead_far)
    lead_own = lax.all_to_all(lead_pair, "batch", 0, 0, axis_index_groups=teams)
    place = side.astype(jnp.int32).reshape(1)
    normal, masked, masked_t = prepare(place, lengths, tokens, cotangent)
    rest_pair = small_call(pair_kernel, "pair_rest", team_of(rest), half, rest, rest_far)
    lead_own, rest_pair, normal, masked, masked_t = lax.optimization_barrier(
        (lead_own, rest_pair, normal, masked, masked_t)
    )
    rest_own = lax.all_to_all(rest_pair, "batch", 0, 0, axis_index_groups=teams)
    lead_other = swap(lead_own)
    per_seq = lambda a: a.reshape(seqs, slot_rows, width)
    n1t, qkv, attended, linv, probs, wpairs, norms = forward(
        chips, norm_part, place, lengths, per_seq(normal), key_masks, lead_own, lead_other
    )
    rest_own, attended = lax.optimization_barrier((rest_own, attended))
    rest_other = swap(rest_own)
    mid, act, gmid, gatt, grest_own, grest_other, gnorm_two, weights = middle(
        tokens, masked, masked_t, attended, linv, rest_own, rest_other, norms
    )
    rest_sum = small_call(add_split_kernel, "add_rest", team_of(rest), grest_own, swap(grest_other))
    rest_sum, gatt = lax.optimization_barrier((rest_sum, gatt))
    rest_parts = lax.all_to_all(rest_sum, "batch", 0, 0, axis_index_groups=teams)
    gp, glead_own, glead_other = backward(place, lengths, n1t, qkv, probs, per_seq(gatt), attended)
    rest_mine, rest_theirs = small_call(
        sum_rest_kernel, "sum_rest", [shape(rest.shape, F32), shape(rest.shape, BF16)], half, rest_parts
    )
    rest_theirs, glead_own = lax.optimization_barrier((rest_theirs, glead_own))
    lead_sum = small_call(add_kernel, "add_lead", shape(glead_own.shape, BF16), glead_own, swap(glead_other))
    lead_sum, rest_parts = lax.optimization_barrier((lead_sum, rest_parts))
    lead_parts = lax.all_to_all(lead_sum.reshape(chips, shard_rows, 10 * HD), "batch", 0, 0)
    input_grad, terms, block_out = input_gradient(
        tokens, gp, per_seq(gmid), wpairs, norms, gnorm_two, per_seq(mid), act, weights
    )
    rest_far = lax.ppermute(rest_theirs, "batch", far_pairs)
    lead_shard, rest_shard, message = small_call(
        sum_lead_kernel,
        "sum_lead",
        [shape(lead.shape, F32), shape(rest.shape, F32), shape(terms.shape, F32)],
        lead_parts,
        rest_mine,
        rest_far,
        terms,
    )
    message = message + swap(message)
    stride = 1
    while stride < chips:
        across = [(2 * i + core, 2 * (i ^ stride) + 1 - core) for i in range(chips) for core in range(2)]
        message = message + lax.ppermute(message, ("batch", "head"), across)
        stride *= 2
    like = lambda a: shape(a.shape, F32)
    moments = (
        qkv_moments.transpose(0, 2, 1, 3),
        out_moments.transpose(0, 2, 1),
        up_moments,
        down_moments.transpose(0, 2, 1),
        norm_moments,
    )
    results = small_call(
        update_kernel,
        "update_weights",
        [shape((1, 1), F32)] + [like(a) for a in masters + moments] + [shape((1, norm_part), F32)],
        (lax.axis_index("batch") * 2 + side).astype(jnp.int32).reshape(1),
        message,
        lead_shard,
        rest_shard,
        *masters,
        *moments,
    )
    grad_norm, qkv_next, out_next, up_next, down_next, norm_next = results[:6]
    qkv_states, out_states, up_states, down_states, norm_states, norm_grads = results[6:]
    return (
        block_out,
        input_grad,
        grad_norm.reshape(()),
        qkv_next.transpose(1, 0, 2),
        out_next.T,
        up_next,
        down_next.T,
        norm_next[0],
        qkv_states.transpose(0, 2, 1, 3),
        out_states.transpose(0, 2, 1),
        up_states,
        down_states.transpose(0, 2, 1),
        norm_states,
        norm_grads[0],
    )


def solution(mesh):
    chips = mesh.shape["batch"]
    return jax.shard_map(
        functools.partial(per_device, chips),
        mesh=mesh,
        in_specs=(
            P(("batch", "head"), None, None),
            P(("batch", "head"), None, None),
            P("batch"),
            P("batch", None),
            P("batch", None, "head"),
            P("head", "batch"),
            P("batch", "head"),
            P("head", "batch"),
            P(("batch", "head")),
            P(None, "batch", None, "head"),
            P(None, "head", "batch"),
            P(None, "batch", "head"),
            P(None, "head", "batch"),
            P(None, ("batch", "head")),
        ),
        out_specs=(
            P(("batch", "head"), None, None),
            P(("batch", "head"), None, None),
            P(),
            P("batch", None, "head"),
            P("head", "batch"),
            P("batch", "head"),
            P("head", "batch"),
            P(("batch", "head")),
            P(None, "batch", None, "head"),
            P(None, "head", "batch"),
            P(None, "batch", "head"),
            P(None, "head", "batch"),
            P(None, ("batch", "head")),
            P(("batch", "head")),
        ),
        check_vma=False,
    )
```
